128 devices in a mesh: blk: 4 (over x_hi, core), batch: 32 (over x_lo, y, z).
Axes of the slice: x: 4 (x_hi: 2, x_lo: 2; x = x_hi * 2 + x_lo), y: 4, z: 4, core: 2. Of those that a mesh axis runs over, the one named last changes fastest.
Arguments:
- pixels: bfloat16 [32, 1024, 768], P('batch', 'blk'), may hold values from -6 to 6
- positions: bfloat16 [32, 1024, 1024], P('batch', 'blk'), may hold values from -4 to 4
- segments: int32 [32, 1024], P('batch'), may hold values from -1 to 2, as said below
- groups: int32 [32, 1024], P('batch', 'blk'), may hold values from 0 to 3, as said below
- cotangent: bfloat16 [32, 1024, 1024], P('batch', 'blk'), may hold values from -6 to 6
- emb_weight: bfloat16 [4, 768, 1024], replicated, may hold values from -0.21875 to 0.21875
- emb_bias: float32 [4, 1024], replicated, may hold values from -2 to 2
- norm1_gain: float32 [1024], replicated, may hold values from 0.5 to 1.5
- norm1_bias: float32 [1024], replicated, may hold values from -2 to 2
- qkv_weight: bfloat16 [1024, 3072], replicated, may hold values from -0.1875 to 0.1875
- query_bias: float32 [1024], replicated, may hold values from -3 to 3
- value_bias: float32 [1024], replicated, may hold values from -0.3 to 0.3
- out_weight: bfloat16 [1024, 1024], replicated, may hold values from -3.5 to 3.5
- out_bias: float32 [1024], replicated, may hold values from -2 to 2
- norm2_gain: float32 [1024], replicated, may hold values from 0.5 to 1.5
- norm2_bias: float32 [1024], replicated, may hold values from -2 to 2
- fc1_weight: bfloat16 [1024, 4096], replicated, may hold values from -0.1875 to 0.1875
- fc1_bias: float32 [4096], replicated, may hold values from -2 to 2
- fc2_weight: bfloat16 [4096, 1024], replicated, may hold values from -0.09375 to 0.09375
- fc2_bias: float32 [1024], replicated, may hold values from -2 to 2
Outputs:
- block_out: bfloat16 [32, 1024, 1024], P('batch', 'blk')
- pixel_grad: bfloat16 [32, 1024, 768], P('batch', 'blk')
- grad_emb_weight: float32 [4, 768, 1024], P(None, None, ('blk', 'batch'))
- grad_emb_bias: float32 [4, 1024], P(None, ('blk', 'batch'))
- grad_norm1_gain: float32 [1024], P(('blk', 'batch'))
- grad_norm1_bias: float32 [1024], P(('blk', 'batch'))
- grad_qkv_weight: float32 [1024, 3072], P(('blk', 'batch'))
- grad_query_bias: float32 [1024], P(('blk', 'batch'))
- grad_value_bias: float32 [1024], P(('blk', 'batch'))
- grad_out_weight: float32 [1024, 1024], P(('blk', 'batch'))
- grad_out_bias: float32 [1024], P(('blk', 'batch'))
- grad_norm2_gain: float32 [1024], P(('blk', 'batch'))
- grad_norm2_bias: float32 [1024], P(('blk', 'batch'))
- grad_fc1_weight: float32 [1024, 4096], P(('blk', 'batch'))
- grad_fc1_bias: float32 [4096], P(('blk', 'batch'))
- grad_fc2_weight: float32 [4096, 1024], P(('blk', 'batch'))
- grad_fc2_bias: float32 [1024], P(('blk', 'batch'))
The draws below stay inside these ranges and needn't reach their ends.
Inputs may be any that keep to these rules, and one draw needn't show every extreme that they name: `segments`: items are contiguous runs of slots numbered 0, 1, 2 in order along the row; a run of 196 slots is an RGB item, one of 588 slots a 13-band item; every other slot is padding (-1). `groups`: 3 on RGB items; the three runs of 196 slots of a 13-band item hold groups 0, 1 and 2 in some order; on padding any group.
All inputs are finite; a program needn't handle non-finite values.
Results may differ from the reference program's by a relative error of at most 0.015.
Values may be sent and summed in bfloat16 or wider, within the bound.
A program may use at most 256 MiB of HBM per device.

```python
import jax
import jax.numpy as jnp
import numpy as np
from jax import lax

D = 1024
FF = 4096
HD = 64
H = 16
PIX = 768
NG = 4
PATCHES = 196
SLOTS = 1024
ROWS = 32
N_BLK = 4


band_orders = np.array([[0, 1, 2], [0, 2, 1], [1, 0, 2], [1, 2, 0], [2, 0, 1], [2, 1, 0]], np.int32)


def slot_layout(key):
    span_low = max((N_BLK - 1) * SLOTS // N_BLK - 3 * PATCHES + 1, 0)
    span_high = min(SLOTS // N_BLK - 1, SLOTS - 3 * PATCHES)
    first_low = max(span_low, PATCHES)
    first_high = min(span_high, SLOTS - 4 * PATCHES)
    key_start, key_first, key_order, key_filler = jax.random.split(key, 4)
    begins = jax.random.randint(key_start, (ROWS,), span_low, span_high + 1)
    first_begin = jax.random.randint(key_first, (), first_low, first_high + 1)
    begins = begins.at[0].set(first_begin)
    slot_index = jnp.arange(SLOTS, dtype=jnp.int32)[None, :]
    begin_col = begins[:, None]
    finish_col = begin_col + 3 * PATCHES
    lead_item = (begin_col >= PATCHES).astype(jnp.int32)
    in_lead = (slot_index < PATCHES) & (lead_item > 0)
    in_main = (slot_index >= begin_col) & (slot_index < finish_col)
    trail_fits = SLOTS - finish_col >= PATCHES
    in_trail = trail_fits & (slot_index >= finish_col) & (slot_index < finish_col + PATCHES)
    segment_ids = jnp.where(in_lead, 0, jnp.where(in_main, lead_item, jnp.where(in_trail, lead_item + 1, -1)))
    order_pick = jax.random.randint(key_order, (ROWS,), 0, 6)
    part_index = jnp.clip((slot_index - begin_col) // PATCHES, 0, 2)
    order_rows = jnp.asarray(band_orders)[order_pick]
    band_main = jnp.take_along_axis(order_rows, part_index, axis=1)
    filler = jax.random.randint(key_filler, (ROWS, SLOTS), 0, NG)
    group_ids = jnp.where(in_main, band_main, jnp.where(in_lead | in_trail, NG - 1, filler))
    return (segment_ids.astype(jnp.int32), group_ids.astype(jnp.int32))


def draw_segments(key, part):
    shared = slot_layout(key)
    return shared[0]


def draw_groups(key, part):
    shared = slot_layout(key)
    return shared[1]


def block_scale(own_key, shape, shards, low, top_value):
    level = 1.0
    for dim, parts in shards:
        heights = jax.random.uniform(jax.random.fold_in(jax.random.fold_in(own_key, 6), dim), (parts,), jnp.float32, low / len(shards), top_value / len(shards))
        level = level * jnp.repeat(jnp.exp(heights), shape[dim] // parts).reshape((-1,) + (1,) * (len(shape) - 1 - dim))
    return level


def noise(rng, shape, deviation, bound, pieces=(), kind=jnp.bfloat16):
    factor_of = block_scale(rng, shape, pieces, -0.22, 0.18) if pieces else 1.0
    drawn = jax.random.normal(rng, shape, jnp.float32) * deviation * factor_of
    return jnp.minimum(jnp.maximum(drawn, -bound), bound).astype(kind)


def setup_inputs(seed: int = 0) -> dict:
    key_list = jax.random.split(jax.random.key(seed), 21)
    return {
        "pixels": noise(key_list[0], (ROWS, SLOTS, PIX), 1.0, 6.0, ((0, 32), (1, 4))),
        "positions": noise(key_list[1], (ROWS, SLOTS, D), 0.5, 4.0, ((0, 32), (1, 4))),
        "segments": draw_segments(jax.random.fold_in(key_list[20], 71), 0),
        "groups": draw_groups(jax.random.fold_in(key_list[20], 71), 0),
        "cotangent": noise(key_list[4], (ROWS, SLOTS, D), 1.0, 6.0, ((0, 32), (1, 4))),
        "emb_weight": noise(key_list[5], (NG, PIX, D), PIX ** -0.5, 0.21875),
        "emb_bias": noise(key_list[6], (NG, D), 0.3, 2.0, (), jnp.float32),
        "norm1_gain": jnp.clip(1.0 + 0.1 * jax.random.normal(key_list[7], (D,), jnp.float32), 0.5, 1.5),
        "norm1_bias": noise(key_list[8], (D,), 0.3, 2.0, (), jnp.float32),
        "qkv_weight": noise(key_list[9], (D, 3 * D), D ** -0.5, 0.1875),
        "query_bias": noise(key_list[10], (D,), 0.5, 3.0, (), jnp.float32),
        "value_bias": noise(key_list[11], (D,), 0.05, 0.3, (), jnp.float32),
        "out_weight": noise(key_list[12], (D, D), (max(1, D * 3 // SLOTS)) ** -0.5, 3.5),
        "out_bias": noise(key_list[13], (D,), 0.3, 2.0, (), jnp.float32),
        "norm2_gain": jnp.clip(1.0 + 0.1 * jax.random.normal(key_list[14], (D,), jnp.float32), 0.5, 1.5),
        "norm2_bias": noise(key_list[15], (D,), 0.3, 2.0, (), jnp.float32),
        "fc1_weight": noise(key_list[16], (D, FF), D ** -0.5, 0.1875),
        "fc1_bias": noise(key_list[17], (FF,), 0.3, 2.0, (), jnp.float32),
        "fc2_weight": noise(key_list[18], (FF, D), FF ** -0.5, 0.09375),
        "fc2_bias": noise(key_list[19], (D,), 0.3, 2.0, (), jnp.float32),
    }


@jax.custom_vjp
def low(v):
    return lax.optimization_barrier(v.astype(jnp.bfloat16)).astype(jnp.float32)

@jax.custom_vjp
def low_back(v):
    return v

def low_keep(v):
    return (low(v), None)

def low_pass(kept, grad):
    return (grad,)

def back_keep(v):
    return (v, None)

def back_low(kept, grad):
    return (low(grad),)
low.defvjp(low_keep, low_pass)
low_back.defvjp(back_keep, back_low)
NORM_EPS = 1e-06
MASKED = -1e+30

def matmul_high(left, right):
    return jnp.dot(left, right, precision=lax.Precision.HIGHEST, preferred_element_type=jnp.float32)

def normalize(values):
    center = values - lax.optimization_barrier(jnp.mean(values, axis=-1, keepdims=True))
    spread = lax.optimization_barrier(jnp.mean(center * center, axis=-1, keepdims=True))
    return center * lax.rsqrt(spread + NORM_EPS)

def row_forward(weights, row_pixels, row_positions, row_segments, row_groups):
    emb_w, emb_b, gain_one, bias_one, qkv_w, q_bias, v_bias, out_w, out_b, gain_two, bias_two, fc1_w, fc1_b, fc2_w, fc2_b = weights
    live_mask = (row_segments >= 0).astype(jnp.float32)[:, None]
    band_hot = (row_groups[:, None] == jnp.arange(emb_w.shape[0], dtype=jnp.int32)[None, :]).astype(jnp.float32)
    projected = jnp.einsum('sp,gpd->sgd', row_pixels, emb_w, precision=lax.Precision.HIGHEST)
    embedded = jnp.einsum('sg,sgd->sd', band_hot, projected, precision=lax.Precision.HIGHEST)
    embedded = embedded + matmul_high(band_hot, emb_b) + row_positions
    stream = low_back(embedded)
    normed_one = low(normalize(stream) * gain_one + bias_one)
    packed = matmul_high(normed_one, qkv_w)
    query = low_back(low(packed[:, :D] + q_bias)).reshape(SLOTS, H, HD)
    keys = low_back(low(packed[:, D:2 * D])).reshape(SLOTS, H, HD)
    values = low_back(low(packed[:, 2 * D:] + v_bias)).reshape(SLOTS, H, HD)
    scores = jnp.einsum('qhd,khd->hqk', query, keys, precision=lax.Precision.HIGHEST) * HD ** (-0.5)
    scores = low_back(scores)
    allowed = row_segments[:, None] == row_segments[None, :]
    scores = jnp.where(allowed[None], scores, MASKED)
    probs = low(jax.nn.softmax(scores, axis=-1))
    attended = jnp.einsum('hqk,khd->qhd', probs, values, precision=lax.Precision.HIGHEST).reshape(SLOTS, D)
    attended = low_back(low(attended))
    branch = low_back(matmul_high(attended, out_w) + out_b)
    middle = stream + branch
    normed_two = low(normalize(middle) * gain_two + bias_two)
    pre_act = low_back(matmul_high(normed_two, fc1_w) + fc1_b)
    hidden = low(jax.nn.gelu(pre_act, approximate=False))
    mlp_out = low_back(matmul_high(hidden, fc2_w) + fc2_b)
    return live_mask * (middle + mlp_out)

def reference(pixels, positions, segments, groups, cotangent, emb_weight, emb_bias, norm1_gain, norm1_bias, qkv_weight, query_bias, value_bias, out_weight, out_bias, norm2_gain, norm2_bias, fc1_weight, fc1_bias, fc2_weight, fc2_bias):
    weights = tuple((w.astype(jnp.float32) for w in (emb_weight, emb_bias, norm1_gain, norm1_bias, qkv_weight, query_bias, value_bias, out_weight, out_bias, norm2_gain, norm2_bias, fc1_weight, fc1_bias, fc2_weight, fc2_bias)))

    def step(totals, row_data):
        row_pixels, row_positions, row_segments, row_groups, row_cot = row_data
        position_f = row_positions.astype(jnp.float32)

        def forward(wts, pixel_f):
            return row_forward(wts, pixel_f, position_f, row_segments, row_groups)
        result, pullback = jax.vjp(forward, weights, row_pixels.astype(jnp.float32))
        weight_grads, pixel_grads = pullback(row_cot.astype(jnp.float32))
        totals = jax.tree.map(jnp.add, totals, weight_grads)
        return (totals, (result.astype(jnp.bfloat16), pixel_grads.astype(jnp.bfloat16)))
    zero_grads = jax.tree.map(jnp.zeros_like, weights)
    totals, (block_out, pixel_grad) = lax.scan(step, zero_grads, (pixels, positions, segments, groups, cotangent))
    return (block_out, pixel_grad, totals[0], totals[1], totals[2], totals[3], totals[4], totals[5], totals[6], totals[7], totals[8], totals[9], totals[10], totals[11], totals[12], totals[13], totals[14])
```

```python
from functools import partial

import jax
import jax.numpy as jnp
from jax import lax
from jax.experimental import pallas as pl
from jax.experimental.pallas import tpu as pltpu
from jax.sharding import PartitionSpec as P

HD = 64


NORM_EPS = 1e-06
MASKED = -1e30


MESH = pl.DeviceIdType.MESH
AXES = ("xb", "xa", "yb", "ya", "zb", "za")
ROTATION = ("xa", "ya", "za", "xb", "yb", "zb")
GRAY = (0, 1, 3, 2)
BLOCKS = tuple(16 * x + 4 * y + z for x in GRAY for y in GRAY for z in GRAY)
CHUNKS = 30


def place():
    blk = lax.axis_index("blk")
    batch = lax.axis_index("batch")
    return blk // 2, blk % 2, batch // 16, (batch // 4) % 4, batch % 4


def neighbours(where):
    x_hi, core, x_lo, y, z = where

    def device(x_hi, core, x_lo, y, z):
        return (x_hi * 2 + core, x_lo * 16 + y * 4 + z)

    return {
        "core": device(x_hi, 1 - core, x_lo, y, z),
        "xa": device(x_hi, core, 1 - x_lo, y, z),
        "xb": device(1 - x_hi, core, 1 - x_lo, y, z),
        "ya": device(x_hi, core, x_lo, y + 1 - 2 * (y % 2), z),
        "yb": device(x_hi, core, x_lo, 3 - y, z),
        "za": device(x_hi, core, x_lo, y, z + 1 - 2 * (z % 2)),
        "zb": device(x_hi, core, x_lo, y, 3 - z),
    }


def own_bits(where):
    x_hi, _, x_lo, y, z = where
    return {
        "xb": x_hi,
        "xa": (x_hi + x_lo) % 2,
        "yb": y // 2,
        "ya": (y // 2 + y) % 2,
        "zb": z // 2,
        "za": (z // 2 + z) % 2,
    }


def class_dims(kind):
    return tuple(ROTATION[(kind + step) % 6] for step in range(6))


def split_shape(kind, step):
    dims = class_dims(kind)
    left = [axis for axis in AXES if axis not in dims[:step]]
    at = left.index(dims[step])
    return 2**at, 2 ** (len(left) - 1 - at)


KEEP_AT = (0, 32, 0, 16, 24, 28)
SEND_AT = (32, 48, 8, 20, 26, 29)
ARRIVE_AT = (0, 32, 48, 56, 60, 62)


def weight_grads_kernel(
    gs_in, pix_in, hot_in, n1_in, gp_in, att_in, gb_in, n2_in, gpre_in, hid_in, gout_in, row_in,
    emb_out, qkv_out, out_out, fc1_out, fc2_out, bias_out,
    x_buf, xh_buf, pix_buf, hot_buf, gp_buf, gb_buf, gpre_buf, gout_buf, row_buf, lanes,
    xt_buf, xht_buf, work, arrive, work_f, arrive_f,
    ex_send, ex_recv, ex_local, send_sem, recv_sem,
):
    where = place()
    x_hi, core, x_lo, y, z = where
    near = neighbours(where)
    bits = own_bits(where)

    barrier = pltpu.get_barrier_semaphore()
    for target in near.values():
        pl.semaphore_signal(barrier, inc=1, device_id=target, device_id_type=MESH)
    pl.semaphore_wait(barrier, 7)

    count = 0

    def exchange(source, dest, width):
        nonlocal count
        index, count = count, count + 1

        def cut(owner):
            if width is None:
                return source
            return source.at[:, pl.ds(pl.multiple_of(width[0] + owner * width[1], 128), width[1])]

        local = pltpu.make_async_copy(cut(core), dest(0), ex_local.at[index])
        remote = pltpu.make_async_remote_copy(
            src_ref=cut(1 - core),
            dst_ref=dest(1),
            send_sem=ex_send.at[index],
            recv_sem=ex_recv.at[index],
            device_id=near["core"],
            device_id_type=MESH,
        )
        return local, remote

    def slots(buf, columns=None):
        def dest(half):
            if columns is None:
                return buf.at[pl.ds(256 * half, 256), :]
            return buf.at[pl.ds(256 * half, 256), pl.ds(*columns)]

        return dest

    def halves(source, buf, span):
        return [
            exchange(source, slots(buf, (high * span, span)), (high * 2 * span, span))
            for high in (0, 1)
        ]

    groups = {
        "rows": [exchange(row_in, lambda half: row_buf.at[half], None)],
        "out": halves(att_in, x_buf.at[0], 256) + [exchange(gb_in, slots(gb_buf), None)],
        "qkv": halves(n1_in, x_buf.at[1], 256) + [exchange(gp_in, slots(gp_buf), None)],
        "fc1": halves(n2_in, x_buf.at[2], 256) + [exchange(gpre_in, slots(gpre_buf), None)],
        "emb": halves(gs_in, x_buf.at[3], 256)
        + [exchange(pix_in, slots(pix_buf), None), exchange(hot_in, slots(hot_buf), None)],
        "fc2": halves(hid_in, xh_buf, 1024) + [exchange(gout_in, slots(gout_buf), None)],
    }

    def begin(name):
        for local, remote in groups[name]:
            remote.start()
            local.start()

    def arrived(name):
        for local, remote in groups[name]:
            local.wait()
            remote.wait_recv()

    def transposed(buf, dest):
        turned = buf[...].astype(jnp.float32).T
        dest[...] = jnp.concatenate(
            [turned[8 * block : 8 * block + 8] for block in BLOCKS], axis=0
        ).astype(jnp.bfloat16)

    def hop(chunk, kind, step, floats=False):
        held, come, index = (
            (work_f, arrive_f, CHUNKS) if floats else (work.at[chunk], arrive.at[chunk], chunk)
        )
        half = 32 >> step
        return pltpu.make_async_remote_copy(
            src_ref=held.at[pl.ds(SEND_AT[step], half)],
            dst_ref=come.at[pl.ds(ARRIVE_AT[step], half)],
            send_sem=send_sem.at[index, step],
            recv_sem=recv_sem.at[index, step],
            device_id=near[class_dims(kind)[step]],
            device_id_type=MESH,
        )

    def put(chunk, kind, result, floats=False):
        held = work_f if floats else work.at[chunk]
        before, after = split_shape(kind, 0)
        own = bits[class_dims(kind)[0]]
        for a in range(before):
            for bit in (0, 1):
                other = own if bit == 0 else 1 - own
                piece = result[(2 * a + bit) * after : (2 * a + bit + 1) * after]
                held[pl.ds(other * 32 + a * after, after)] = piece
        hop(chunk, kind, 0, floats).start()

    def advance(chunk, kind, step, finish, floats=False):
        held, come = (work_f, arrive_f) if floats else (work.at[chunk], arrive.at[chunk])
        hop(chunk, kind, step, floats).wait_recv()
        keep, come_at = KEEP_AT[step], ARRIVE_AT[step]
        if step == 5:
            finish(held[keep].astype(jnp.float32) + come[come_at].astype(jnp.float32))
            return
        if step == 0:
            hop(chunk, kind, 0, floats).wait_send()
        before, after = split_shape(kind, step + 1)
        own = bits[class_dims(kind)[step + 1]]
        for bit, base in ((1 - own, SEND_AT[step + 1]), (own, KEEP_AT[step + 1])):

            def merge(a, carry, bit=bit, base=base):
                at = (2 * a + bit) * after
                held[pl.ds(base + a * after, after)] = (
                    held[pl.ds(keep + at, after)] + come[pl.ds(come_at + at, after)]
                )
                return carry

            lax.fori_loop(0, before, merge, 0, unroll=min(before, 8))
            if base == SEND_AT[step + 1]:
                hop(chunk, kind, step + 1, floats).start()

    def pair(left, right, tile):
        a = jnp.dot(left, right(2 * tile), preferred_element_type=jnp.float32)
        b = jnp.dot(left, right(2 * tile + 1), preferred_element_type=jnp.float32)
        return jnp.concatenate(
            (a.reshape(64, 8, 256), b.reshape(64, 8, 256)), axis=1
        ).astype(jnp.bfloat16)

    def columns_of(buf):
        return lambda tile: buf[:, 256 * tile : 256 * tile + 256]

    def band_pixels(tile):
        band, at = tile // 3, tile % 3
        picked = pix_buf[:, 256 * at : 256 * at + 256].astype(jnp.float32)
        chosen = hot_buf[:, band : band + 1].astype(jnp.float32)
        return (picked * chosen).astype(jnp.bfloat16)

    plan = []
    for name, x_at, right, tiles, dest in (
        ("out", 0, columns_of(gb_buf), 2, out_out),
        ("qkv", 1, columns_of(gp_buf), 6, qkv_out),
        ("fc1", 2, columns_of(gpre_buf), 8, fc1_out),
        ("emb", 3, band_pixels, 6, emb_out),
    ):
        for tile in range(tiles):
            plan.append((name, x_at, right, tile, dest))
    for tile in range(8):
        plan.append(("fc2", None, columns_of(gout_buf), tile, fc2_out))

    def finisher(chunk):
        name, _, _, tile, dest = plan[chunk]

        def finish(total):
            if name == "fc2":
                dest[
                    16 * (tile % 2) : 16 * (tile % 2) + 16, 256 * (tile // 2) : 256 * (tile // 2) + 256
                ] = total
            else:
                dest[:, 512 * tile : 512 * tile + 256] = total[:8]
                dest[:, 512 * tile + 256 : 512 * tile + 512] = total[8:]

        return finish

    def finish_bias(total):
        bias_out[...] = total

    ready = set()

    def compute(chunk):
        name, x_at, right, tile, _ = plan[chunk]
        if name not in ready:
            ready.add(name)
            arrived(name)
            if name == "fc2":
                turned = xh_buf[...].astype(jnp.float32).T.astype(jnp.bfloat16)
                xht_buf[...] = jnp.concatenate(
                    [turned[32 * block : 32 * block + 32] for block in BLOCKS], axis=0
                )
            else:
                transposed(x_buf.at[x_at], xt_buf.at[x_at])
        if name != "fc2":
            put(chunk, chunk % 6, pair(xt_buf[x_at], right, tile))
        elif tile % 2 == 0:
            both = jnp.dot(
                xht_buf[...], right(tile // 2), preferred_element_type=jnp.float32
            ).reshape(64, 32, 256)
            put(chunk, chunk % 6, both[:, :16].astype(jnp.bfloat16))
            put(chunk + 1, (chunk + 1) % 6, both[:, 16:].astype(jnp.bfloat16))

    begin("rows")
    begin("out")
    begin("qkv")
    waves = CHUNKS // 6
    for turn in range(waves + 6):
        if turn < waves:
            for chunk in range(6 * turn, 6 * turn + 6):
                compute(chunk)
            if turn == 0:
                begin("fc1")
                begin("emb")
                arrived("rows")
                lanes[...] = jnp.zeros_like(lanes)
                for high in (0, 1):
                    span = pl.ds(pl.multiple_of(high * 512 + core * 256, 128), 256)
                    lanes[0:16, 256 * high : 256 * high + 256] = (
                        row_buf[0, :, span] + row_buf[1, :, span]
                    )
                turned = lanes[...].T.reshape(64, 8, 128)
                put(None, 0, jnp.concatenate([turned[b : b + 1] for b in BLOCKS], axis=0), True)
            if turn == 1:
                begin("fc2")
        for step in range(6):
            wave = turn - 1 - step
            if 0 <= wave < waves:
                for chunk in range(6 * wave, 6 * wave + 6):
                    advance(chunk, chunk % 6, step, finisher(chunk))
                if wave == 0:
                    advance(None, 0, step, finish_bias, True)
    for name in groups:
        for _, remote in groups[name]:
            remote.wait_send()
    for step in range(1, 6):
        for chunk in range(CHUNKS):
            hop(chunk, chunk % 6, step).wait_send()
        hop(None, 0, step, True).wait_send()


def weight_grads(*operands):
    any_space = pl.BlockSpec(memory_space=pl.ANY)
    in_vmem = pl.BlockSpec(memory_space=pltpu.VMEM)
    half, full = jnp.bfloat16, jnp.float32
    return pl.pallas_call(
        weight_grads_kernel,
        out_shape=(
            jax.ShapeDtypeStruct((8, 3072), full),
            jax.ShapeDtypeStruct((8, 3072), full),
            jax.ShapeDtypeStruct((8, 1024), full),
            jax.ShapeDtypeStruct((8, 4096), full),
            jax.ShapeDtypeStruct((32, 1024), full),
            jax.ShapeDtypeStruct((8, 128), full),
        ),
        in_specs=[any_space] * 12,
        out_specs=(in_vmem,) * 6,
        scratch_shapes=[
            pltpu.VMEM((4, 512, 512), half),
            pltpu.VMEM((512, 2048), half),
            pltpu.VMEM((512, 768), half),
            pltpu.VMEM((512, 128), half),
            pltpu.VMEM((512, 3072), half),
            pltpu.VMEM((512, 1024), half),
            pltpu.VMEM((512, 4096), half),
            pltpu.VMEM((512, 1024), half),
            pltpu.VMEM((2, 16, 1024), full),
            pltpu.VMEM((128, 512), full),
            pltpu.VMEM((4, 512, 512), half),
            pltpu.VMEM((2048, 512), half),
            pltpu.VMEM((CHUNKS, 64, 16, 256), half),
            pltpu.VMEM((CHUNKS, 63, 16, 256), half),
            pltpu.VMEM((64, 8, 128), full),
            pltpu.VMEM((63, 8, 128), full),
            pltpu.SemaphoreType.DMA((20,)),
            pltpu.SemaphoreType.DMA((20,)),
            pltpu.SemaphoreType.DMA((20,)),
            pltpu.SemaphoreType.DMA((CHUNKS + 1, 6)),
            pltpu.SemaphoreType.DMA((CHUNKS + 1, 6)),
        ],
        compiler_params=pltpu.CompilerParams(
            collective_id=0, has_side_effects=True, vmem_limit_bytes=60 << 20
        ),
        name="weight_grads",
    )(*operands)


def normalize(values):
    center = values - jnp.mean(values, axis=-1, keepdims=True)
    spread = jnp.mean(center * center, axis=-1, keepdims=True)
    return center * lax.rsqrt(spread + NORM_EPS)


def norm_apply(values, gain, shift):
    return normalize(values) * gain + shift


def on_device(
    pixels,
    positions,
    segments,
    groups,
    cotangent,
    emb_weight,
    emb_bias,
    norm1_gain,
    norm1_bias,
    qkv_weight,
    query_bias,
    value_bias,
    out_weight,
    out_bias,
    norm2_gain,
    norm2_bias,
    fc1_weight,
    fc1_bias,
    fc2_weight,
    fc2_bias,
):
    rows_dev, slice_len, pix_len = pixels.shape
    model_width = qkv_weight.shape[0]
    head_count = model_width // HD
    band_count = emb_weight.shape[0]
    tok_count = rows_dev * slice_len
    score_scale = HD ** (-0.5)
    offset = lax.axis_index("blk") * slice_len
    query_seg = lax.dynamic_slice_in_dim(segments, offset, slice_len, 1)
    live_mask = (query_seg >= 0).astype(jnp.float32).reshape(tok_count, 1)
    allowed = query_seg[:, None, :, None] == segments[:, None, None, :]
    flat_pixels = pixels.reshape(tok_count, pix_len)
    band_hot = (
        groups.reshape(tok_count, 1) == jnp.arange(band_count, dtype=jnp.int32)[None, :]
    ).astype(jnp.float32)
    embedded = positions.reshape(tok_count, model_width).astype(jnp.float32)
    embedded = embedded + jnp.dot(band_hot, emb_bias, precision=lax.Precision.HIGHEST)
    for band_index in range(band_count):
        embedded = embedded + band_hot[:, band_index : band_index + 1] * jnp.dot(
            flat_pixels, emb_weight[band_index], preferred_element_type=jnp.float32
        )
    normed_one = norm_apply(embedded, norm1_gain, norm1_bias).astype(jnp.bfloat16)
    packed = jnp.dot(normed_one, qkv_weight, preferred_element_type=jnp.float32)
    query = (
        (packed[:, :model_width] + query_bias)
        .astype(jnp.bfloat16)
        .reshape(rows_dev, slice_len, head_count, HD)
    )
    keys = (
        packed[:, model_width : 2 * model_width]
        .astype(jnp.bfloat16)
        .reshape(rows_dev, slice_len, model_width)
    )
    values = (
        (packed[:, 2 * model_width :] + value_bias)
        .astype(jnp.bfloat16)
        .reshape(rows_dev, slice_len, model_width)
    )

    def score_block(key_piece):
        key_heads = key_piece.reshape(rows_dev, key_piece.shape[1], head_count, HD)
        raw = (
            jnp.einsum("rqhd,rkhd->rhqk", query, key_heads, preferred_element_type=jnp.float32)
            * score_scale
        )
        return jnp.where(allowed, raw, MASKED)

    key_all, value_all = (
        lax.all_gather(keys, "blk", axis=1, tiled=True),
        lax.all_gather(values, "blk", axis=1, tiled=True),
    )
    scores = score_block(key_all)
    row_peak = jnp.max(scores, axis=-1, keepdims=True)
    expo = jnp.exp(scores - row_peak)
    row_total = jnp.sum(expo, axis=-1, keepdims=True)
    probs_b = (expo / row_total).astype(jnp.bfloat16)
    log_total = row_peak + jnp.log(row_total)
    attended = jnp.einsum(
        "rhqk,rkhd->rqhd",
        probs_b,
        value_all.reshape(rows_dev, -1, head_count, HD),
        preferred_element_type=jnp.float32,
    )
    attended_b = attended.reshape(tok_count, model_width).astype(jnp.bfloat16)
    middle = (
        embedded + jnp.dot(attended_b, out_weight, preferred_element_type=jnp.float32) + out_bias
    )
    normed_two = norm_apply(middle, norm2_gain, norm2_bias).astype(jnp.bfloat16)
    pre_act = jnp.dot(normed_two, fc1_weight, preferred_element_type=jnp.float32) + fc1_bias
    hidden_b = jax.nn.gelu(pre_act, approximate=False).astype(jnp.bfloat16)
    mlp_out = jnp.dot(hidden_b, fc2_weight, preferred_element_type=jnp.float32) + fc2_bias
    block_out = (
        (live_mask * (middle + mlp_out))
        .astype(jnp.bfloat16)
        .reshape(rows_dev, slice_len, model_width)
    )
    upstream = cotangent.reshape(tok_count, model_width).astype(jnp.float32) * live_mask
    upstream_b = upstream.astype(jnp.bfloat16)
    grad_fc2_bias = jnp.sum(upstream_b.astype(jnp.float32), axis=0)
    hidden_grad = jnp.einsum(
        "td,fd->tf", upstream_b, fc2_weight, preferred_element_type=jnp.float32
    )
    gelu_out, gelu_pull = jax.vjp(partial(jax.nn.gelu, approximate=False), pre_act)
    pre_grad_b = gelu_pull(hidden_grad)[0].astype(jnp.bfloat16)
    grad_fc1_bias = jnp.sum(pre_grad_b.astype(jnp.float32), axis=0)
    normed_two_grad = jnp.einsum(
        "tf,df->td", pre_grad_b, fc1_weight, preferred_element_type=jnp.float32
    )
    norm_out, norm_two_pull = jax.vjp(norm_apply, middle, norm2_gain, norm2_bias)
    middle_grad_norm, grad_gain_two, grad_bias_two = norm_two_pull(normed_two_grad)
    middle_grad = upstream + middle_grad_norm
    branch_grad_b = middle_grad.astype(jnp.bfloat16)
    grad_out_bias = jnp.sum(branch_grad_b.astype(jnp.float32), axis=0)
    attended_grad = jnp.einsum(
        "te,de->td", branch_grad_b, out_weight, preferred_element_type=jnp.float32
    )
    attended_grad = attended_grad.astype(jnp.bfloat16).reshape(rows_dev, slice_len, head_count, HD)
    key_heads_all = key_all.reshape(rows_dev, -1, head_count, HD)
    value_heads_all = value_all.reshape(rows_dev, -1, head_count, HD)
    probs = jnp.exp(score_block(key_all) - log_total)
    probs_back = probs.astype(jnp.bfloat16)
    prob_grad = jnp.einsum(
        "rqhd,rkhd->rhqk", attended_grad, value_heads_all, preferred_element_type=jnp.float32
    )
    score_grad_b = (
        probs * (prob_grad - jnp.sum(probs * prob_grad, axis=-1, keepdims=True))
    ).astype(jnp.bfloat16)
    query_grad = (
        jnp.einsum(
            "rhqk,rkhd->rqhd", score_grad_b, key_heads_all, preferred_element_type=jnp.float32
        )
        * score_scale
    )
    key_term = (
        jnp.einsum("rhqk,rqhd->krhd", score_grad_b, query, preferred_element_type=jnp.float32)
        * score_scale
    )
    value_term = jnp.einsum(
        "rhqk,rqhd->krhd", probs_back, attended_grad, preferred_element_type=jnp.float32
    )
    kv_grad = lax.psum_scatter(
        jnp.concatenate((key_term, value_term), axis=2)
        .reshape(lax.axis_size("blk") * slice_len, rows_dev, 2 * model_width)
        .astype(jnp.bfloat16),
        "blk",
        scatter_dimension=0,
        tiled=True,
    ).astype(jnp.float32)
    kv_grad = jnp.swapaxes(kv_grad, 0, 1).reshape(tok_count, 2 * model_width)
    packed_grad_b = jnp.concatenate(
        (query_grad.reshape(tok_count, model_width), kv_grad), axis=1
    ).astype(jnp.bfloat16)
    grad_query_bias = jnp.sum(packed_grad_b[:, :model_width].astype(jnp.float32), axis=0)
    grad_value_bias = jnp.sum(packed_grad_b[:, 2 * model_width :].astype(jnp.float32), axis=0)
    normed_one_grad = jnp.einsum(
        "te,de->td", packed_grad_b, qkv_weight, preferred_element_type=jnp.float32
    )
    norm_first, norm_one_pull = jax.vjp(norm_apply, embedded, norm1_gain, norm1_bias)
    stream_grad_norm, grad_gain_one, grad_bias_one = norm_one_pull(normed_one_grad)
    stream_grad_b = (middle_grad + stream_grad_norm).astype(jnp.bfloat16)
    pixel_grad = jnp.zeros((tok_count, pix_len), jnp.float32)
    for band_index in range(band_count):
        band_col = band_hot[:, band_index : band_index + 1]
        pixel_grad = pixel_grad + band_col * jnp.einsum(
            "td,pd->tp", stream_grad_b, emb_weight[band_index], preferred_element_type=jnp.float32
        )
    grad_emb_bias = jnp.einsum(
        "tg,td->gd", band_hot, stream_grad_b.astype(jnp.float32), precision=lax.Precision.HIGHEST
    )
    pixel_out = pixel_grad.astype(jnp.bfloat16).reshape(rows_dev, slice_len, pix_len)
    bias_rows = jnp.concatenate(
        (
            grad_emb_bias,
            jnp.stack(
                (
                    grad_gain_one,
                    grad_bias_one,
                    grad_query_bias,
                    grad_value_bias,
                    grad_out_bias,
                    grad_gain_two,
                    grad_bias_two,
                    grad_fc2_bias,
                )
            ),
            jnp.swapaxes(grad_fc1_bias.reshape(128, 4, 8), 0, 1).reshape(4, 1024),
        )
    )
    hot_lanes = jnp.pad(band_hot, ((0, 0), (0, 128 - band_count))).astype(jnp.bfloat16)
    emb_sum, qkv_sum, out_sum, fc1_sum, fc2_sum, bias_sum = weight_grads(
        stream_grad_b,
        flat_pixels,
        hot_lanes,
        normed_one,
        packed_grad_b,
        attended_b,
        branch_grad_b,
        normed_two,
        pre_grad_b,
        hidden_b,
        upstream_b,
        bias_rows,
    )
    bias_cols = bias_sum[:, :16].T
    summed = (
        emb_sum.T.reshape(band_count, pix_len, 8),
        bias_cols[0:4],
        bias_cols[4],
        bias_cols[5],
        qkv_sum,
        bias_cols[6],
        bias_cols[7],
        out_sum,
        bias_cols[8],
        bias_cols[9],
        bias_cols[10],
        fc1_sum,
        bias_cols[12:16].reshape(32),
        fc2_sum,
        bias_cols[11],
    )
    return (
        block_out,
        pixel_out,
        summed[0],
        summed[1],
        summed[2],
        summed[3],
        summed[4],
        summed[5],
        summed[6],
        summed[7],
        summed[8],
        summed[9],
        summed[10],
        summed[11],
        summed[12],
        summed[13],
        summed[14],
    )


def solution(mesh):
    return jax.shard_map(
        on_device,
        mesh=mesh,
        in_specs=(
            P("batch", "blk", None),
            P("batch", "blk", None),
            P("batch", None),
            P("batch", "blk"),
            P("batch", "blk", None),
            P(),
            P(),
            P(),
            P(),
            P(),
            P(),
            P(),
            P(),
            P(),
            P(),
            P(),
            P(),
            P(),
            P(),
            P(),
        ),
        out_specs=(
            P("batch", "blk", None),
            P("batch", "blk", None),
            P(None, None, ("blk", "batch")),
            P(None, ("blk", "batch")),
            P(("blk", "batch")),
            P(("blk", "batch")),
            P(("blk", "batch"), None),
            P(("blk", "batch")),
            P(("blk", "batch")),
            P(("blk", "batch"), None),
            P(("blk", "batch")),
            P(("blk", "batch")),
            P(("blk", "batch")),
            P(("blk", "batch"), None),
            P(("blk", "batch")),
            P(("blk", "batch"), None),
            P(("blk", "batch")),
        ),
        check_vma=False,
    )
```

```python
import jax
import jax.numpy as jnp
from jax import lax
from jax.experimental import pallas as pl
from jax.experimental.pallas import tpu as pltpu
from jax.sharding import PartitionSpec as P

HD = 64
NORM_EPS = 1e-06
MASKED = -1e30

MESH = pl.DeviceIdType.MESH
AXES = ("xb", "xa", "yb", "ya", "zb", "za")
ROTATION = ("xa", "ya", "za", "xb", "yb", "zb")
GRAY = (0, 1, 3, 2)
BLOCKS = tuple(16 * x + 4 * y + z for x in GRAY for y in GRAY for z in GRAY)


def place():
    blk = lax.axis_index("blk")
    batch = lax.axis_index("batch")
    return blk // 2, blk % 2, batch // 16, (batch // 4) % 4, batch % 4


def neighbours(where):
    x_hi, core, x_lo, y, z = where

    def device(x_hi, core, x_lo, y, z):
        return (x_hi * 2 + core, x_lo * 16 + y * 4 + z)

    return {
        "core": device(x_hi, 1 - core, x_lo, y, z),
        "xa": device(x_hi, core, 1 - x_lo, y, z),
        "xb": device(1 - x_hi, core, 1 - x_lo, y, z),
        "ya": device(x_hi, core, x_lo, y + 1 - 2 * (y % 2), z),
        "yb": device(x_hi, core, x_lo, 3 - y, z),
        "za": device(x_hi, core, x_lo, y, z + 1 - 2 * (z % 2)),
        "zb": device(x_hi, core, x_lo, y, 3 - z),
    }


def own_bits(where):
    x_hi, _, x_lo, y, z = where
    return {
        "xb": x_hi,
        "xa": (x_hi + x_lo) % 2,
        "yb": y // 2,
        "ya": (y // 2 + y) % 2,
        "zb": z // 2,
        "za": (z // 2 + z) % 2,
    }


def class_dims(kind):
    return tuple(ROTATION[(kind + step) % 6] for step in range(6))


def split_shape(kind, step):
    dims = class_dims(kind)
    left = [axis for axis in AXES if axis not in dims[:step]]
    at = left.index(dims[step])
    return 2**at, 2 ** (len(left) - 1 - at)


KEEP_AT = (0, 32, 0, 16, 24, 28)
SEND_AT = (32, 48, 8, 20, 26, 29)
ARRIVE_AT = (0, 32, 48, 56, 60, 62)


def nt_dot(left, right):
    return lax.dot_general(left, right, (((1,), (1,)), ((), ())), preferred_element_type=jnp.float32)


def tn_dot(left, right):
    return lax.dot_general(left, right, (((0,), (0,)), ((), ())), preferred_element_type=jnp.float32)


def norm_parts(values):
    center = values - jnp.mean(values, axis=-1, keepdims=True)
    spread = jnp.mean(center * center, axis=-1, keepdims=True)
    scale = lax.rsqrt(spread + NORM_EPS)
    return center * scale, scale


ROW_EMB, ROW_GAIN1, ROW_BIAS1, ROW_QUERY, ROW_VALUE, ROW_OUT, ROW_GAIN2, ROW_BIAS2, ROW_FC2, ROW_FC1 = (
    0, 4, 5, 6, 7, 8, 9, 10, 11, 12,
)
TILE = 512


def forward_kernel(
    pix_in, pos_in, cot_in, hot_in, mask_in, rows, emb_in, qkv_in, ow_in, fc1_in, fc2_in,
    block_out, stream_out, n1_out, q_out, kv_out, lse_out, att_out, n2_out, hid_out, gpre_out,
    gout_out, gbr_out, gatt_out, gmid_out, sums,
    pix, pos, cot, hot, mask, emb_w, qkv_w, out_w, fc1_w, fc2_w,
    stream, n1, q_pairs, kv, att, middle, xhat, n2, gout, hid, gpre, acc, acc_back, gbr, gatt, blk_buf,
    load_sem, save_sem, send_sem, recv_sem,
):
    where = place()
    x_hi, core, x_lo, y, z = where
    partner = (x_hi * 2 + 1 - core, x_lo * 16 + y * 4 + z)
    across = ((1 - x_hi) * 2 + core, x_lo * 16 + y * 4 + z)
    barrier = pltpu.get_barrier_semaphore()
    for target in (partner, across):
        pl.semaphore_signal(barrier, inc=1, device_id=target, device_id_type=MESH)

    loads = {}

    def load(name, source, dest):
        copy = pltpu.make_async_copy(source, dest, load_sem.at[len(loads)])
        copy.start()
        loads[name] = copy

    saves = []

    def save(source, dest):
        copy = pltpu.make_async_copy(source, dest, save_sem.at[len(saves)])
        copy.start()
        saves.append(copy)

    load("hot", hot_in, hot)
    load("pix", pix_in, pix)
    for band in range(4):
        span = pl.ds(768 * band, 768)
        load("emb%d" % band, emb_in.at[span, :], emb_w.at[span, :])
    load("pos", pos_in, pos)
    for part in (1, 2, 0):
        span = pl.ds(1024 * part, 1024)
        load("qkv%d" % part, qkv_in.at[:, span], qkv_w.at[:, span])
    load("mask", mask_in, mask)

    loads["hot"].wait()
    loads["pix"].wait()
    total = None
    for band in range(4):
        chosen = hot[:, band : band + 1]
        picked = (pix[...].astype(jnp.float32) * chosen).astype(jnp.bfloat16)
        loads["emb%d" % band].wait()
        term = jnp.dot(
            picked, emb_w[768 * band : 768 * band + 768, :], preferred_element_type=jnp.float32
        ) + chosen * rows[ROW_EMB + band : ROW_EMB + band + 1, :]
        total = term if total is None else total + term
    loads["pos"].wait()
    stream[...] = total + pos[...].astype(jnp.float32)
    load("cot", cot_in, cot)
    load("out", ow_in, out_w)
    load("fc2", fc2_in, fc2_w)
    load("fc1", fc1_in, fc1_w)
    save(stream, stream_out)
    hat, _ = norm_parts(stream[...])
    n1[...] = (
        hat * rows[ROW_GAIN1 : ROW_GAIN1 + 1, :] + rows[ROW_BIAS1 : ROW_BIAS1 + 1, :]
    ).astype(jnp.bfloat16)
    save(n1, n1_out)

    own_rows = pl.ds(pl.multiple_of((x_hi * 2 + core) * 256, 256), 256)
    far_rows = pl.ds(pl.multiple_of(((1 - x_hi) * 2 + core) * 256, 256), 256)

    def push(pair, which, rows_at, target):
        piece = kv.at[pair, :, rows_at, :]
        return pltpu.make_async_remote_copy(
            src_ref=piece,
            dst_ref=piece,
            send_sem=send_sem.at[which, pair],
            recv_sem=recv_sem.at[which, pair],
            device_id=target,
            device_id_type=MESH,
        )

    def to_across(pair):
        return push(pair, 0, own_rows, across)

    def to_partner(pair):
        return push(pair, 1, own_rows, partner)

    def forward_far(pair):
        return push(pair, 2, far_rows, partner)

    loads["qkv1"].wait()
    loads["qkv2"].wait()
    pl.semaphore_wait(barrier, 2)

    def project(tile, carry):
        span = pl.ds(pl.multiple_of(1024 + 256 * tile, 256), 256)
        keys = jnp.dot(n1[...], qkv_w[:, span], preferred_element_type=jnp.float32).astype(
            jnp.bfloat16
        )
        span = pl.ds(pl.multiple_of(2048 + 256 * tile, 256), 256)
        shift = rows[ROW_VALUE : ROW_VALUE + 1, pl.ds(pl.multiple_of(256 * tile, 256), 256)]
        values = (
            jnp.dot(n1[...], qkv_w[:, span], preferred_element_type=jnp.float32) + shift
        ).astype(jnp.bfloat16)
        for side in (0, 1):
            kv[2 * tile + side, 0, own_rows, :] = keys[:, 128 * side : 128 * side + 128]
            kv[2 * tile + side, 1, own_rows, :] = values[:, 128 * side : 128 * side + 128]
            to_across(2 * tile + side).start()
            to_partner(2 * tile + side).start()
        return carry

    lax.fori_loop(0, 4, project, 0)
    loads["qkv0"].wait()

    def project_query(tile, carry):
        span = pl.ds(pl.multiple_of(256 * tile, 256), 256)
        query = (
            jnp.dot(n1[...], qkv_w[:, span], preferred_element_type=jnp.float32)
            + rows[ROW_QUERY : ROW_QUERY + 1, span]
        ).astype(jnp.bfloat16)
        query = (query.astype(jnp.float32) * HD ** (-0.5)).astype(jnp.bfloat16)
        for side in (0, 1):
            q_pairs[2 * tile + side] = query[:, 128 * side : 128 * side + 128]
        return carry

    lax.fori_loop(0, 4, project_query, 0)
    save(q_pairs, q_out)
    loads["cot"].wait()
    gout[...] = (cot[...].astype(jnp.float32) * hot[:, 4:5]).astype(jnp.bfloat16)
    save(gout, gout_out)
    loads["mask"].wait()

    def pass_on(pair):
        to_across(pair).wait_recv()
        forward_far(pair).start()

    pass_on(0)

    def attend(pair, carry):
        @pl.when(pair < 7)
        def _():
            pass_on(pair + 1)

        to_partner(pair).wait_recv()
        forward_far(pair).wait_recv()
        turned = q_pairs[pair].astype(jnp.float32).T
        at = lax.broadcasted_iota(jnp.int32, (128, 256), 0)
        value_rows = kv[pair, 1].T
        heads = []
        for head in (0, 1):
            own = (at < 64) if head == 0 else (at >= 64)
            mine = jnp.where(own, turned, 0.0).astype(jnp.bfloat16)
            scores = jnp.dot(kv[pair, 0], mine, preferred_element_type=jnp.float32) + mask[...]
            peak = jnp.max(scores, axis=0, keepdims=True)
            expo = jnp.exp(scores - peak)
            norm = jnp.sum(expo, axis=0, keepdims=True)
            heads.append(
                jnp.dot(
                    value_rows[64 * head : 64 * head + 64],
                    expo.astype(jnp.bfloat16),
                    preferred_element_type=jnp.float32,
                )
                / norm
            )
            lse_out[pair, head : head + 1, :] = peak + jnp.log(norm)
        att[:, pl.ds(pl.multiple_of(pair * 128, 128), 128)] = jnp.concatenate(
            heads, axis=0
        ).T.astype(jnp.bfloat16)
        return carry

    lax.fori_loop(0, 8, attend, 0)
    save(kv, kv_out)
    save(att, att_out)

    loads["out"].wait()
    middle[...] = (
        stream[...]
        + jnp.dot(att[...], out_w[...], preferred_element_type=jnp.float32)
        + rows[ROW_OUT : ROW_OUT + 1, :]
    )
    hat, scale = norm_parts(middle[...])
    xhat[...] = hat
    n2[...] = (
        hat * rows[ROW_GAIN2 : ROW_GAIN2 + 1, :] + rows[ROW_BIAS2 : ROW_BIAS2 + 1, :]
    ).astype(jnp.bfloat16)
    save(n2, n2_out)
    loads["fc1"].wait()
    loads["fc2"].wait()
    acc[...] = jnp.zeros_like(acc)
    acc_back[...] = jnp.zeros_like(acc_back)
    for tile in range(4096 // TILE):
        span = slice(TILE * tile, TILE * tile + TILE)
        row, at = ROW_FC1 + TILE * tile // 1024, TILE * tile % 1024
        pre = (
            jnp.dot(n2[...], fc1_w[:, span], preferred_element_type=jnp.float32)
            + rows[row : row + 1, at : at + TILE]
        )
        cdf = 0.5 * (1.0 + lax.erf(pre * (0.5**0.5)))
        hidden = (pre * cdf).astype(jnp.bfloat16)
        hid[:, span] = hidden
        slope = cdf + pre * (jnp.exp(-0.5 * pre * pre) * 0.3989422804014327)
        back = (nt_dot(gout[...], fc2_w[span, :]) * slope).astype(jnp.bfloat16)
        gpre[:, span] = back
        acc[...] += jnp.dot(hidden, fc2_w[span, :], preferred_element_type=jnp.float32)
        acc_back[...] += nt_dot(back, fc1_w[:, span])
        sums[4 + TILE * tile // 1024 : 5 + TILE * tile // 1024, at : at + TILE] = jnp.sum(
            back.astype(jnp.float32), axis=0, keepdims=True
        )
    save(hid, hid_out)
    save(gpre, gpre_out)
    blk_buf[...] = (
        hot[:, 4:5] * (middle[...] + (acc[...] + rows[ROW_FC2 : ROW_FC2 + 1, :]))
    ).astype(jnp.bfloat16)
    save(blk_buf, block_out)
    upstream = gout[...].astype(jnp.float32)
    sums[3:4, :] = jnp.sum(upstream, axis=0, keepdims=True)
    grown = acc_back[...]
    sums[1:2, :] = jnp.sum(grown * xhat[...], axis=0, keepdims=True)
    sums[2:3, :] = jnp.sum(grown, axis=0, keepdims=True)
    grown = grown * rows[ROW_GAIN2 : ROW_GAIN2 + 1, :]
    middle[...] = upstream + scale * (
        grown
        - jnp.mean(grown, axis=-1, keepdims=True)
        - xhat[...] * jnp.mean(grown * xhat[...], axis=-1, keepdims=True)
    )
    save(middle, gmid_out)
    gbr[...] = middle[...].astype(jnp.bfloat16)
    save(gbr, gbr_out)
    sums[0:1, :] = jnp.sum(gbr[...].astype(jnp.float32), axis=0, keepdims=True)
    back = nt_dot(gbr[...], out_w[...]).astype(jnp.bfloat16)
    for pair in range(8):
        gatt[pair] = back[:, 128 * pair : 128 * pair + 128]
    save(gatt, gatt_out)
    for copy in saves:
        copy.wait()

    def drain(pair, carry):
        to_across(pair).wait_send()
        to_partner(pair).wait_send()
        forward_far(pair).wait_send()
        return carry

    lax.fori_loop(0, 8, drain, 0)


def forward(*operands):
    any_space = pl.BlockSpec(memory_space=pl.ANY)
    in_vmem = pl.BlockSpec(memory_space=pltpu.VMEM)
    half, full = jnp.bfloat16, jnp.float32
    shape = jax.ShapeDtypeStruct
    return pl.pallas_call(
        forward_kernel,
        out_shape=(
            shape((256, 1024), half),
            shape((256, 1024), full),
            shape((256, 1024), half),
            shape((8, 256, 128), half),
            shape((8, 2, 1024, 128), half),
            shape((8, 2, 256), full),
            shape((256, 1024), half),
            shape((256, 1024), half),
            shape((256, 4096), half),
            shape((256, 4096), half),
            shape((256, 1024), half),
            shape((256, 1024), half),
            shape((8, 256, 128), half),
            shape((256, 1024), full),
            shape((8, 1024), full),
        ),
        in_specs=[any_space] * 5 + [in_vmem] + [any_space] * 5,
        out_specs=(any_space,) * 5 + (in_vmem,) + (any_space,) * 8 + (in_vmem,),
        scratch_shapes=[
            pltpu.VMEM((256, 768), half),
            pltpu.VMEM((256, 1024), half),
            pltpu.VMEM((256, 1024), half),
            pltpu.VMEM((256, 128), full),
            pltpu.VMEM((1024, 256), full),
            pltpu.VMEM((3072, 1024), half),
            pltpu.VMEM((1024, 3072), half),
            pltpu.VMEM((1024, 1024), half),
            pltpu.VMEM((1024, 4096), half),
            pltpu.VMEM((4096, 1024), half),
            pltpu.VMEM((256, 1024), full),
            pltpu.VMEM((256, 1024), half),
            pltpu.VMEM((8, 256, 128), half),
            pltpu.VMEM((8, 2, 1024, 128), half),
            pltpu.VMEM((256, 1024), half),
            pltpu.VMEM((256, 1024), full),
            pltpu.VMEM((256, 1024), full),
            pltpu.VMEM((256, 1024), half),
            pltpu.VMEM((256, 1024), half),
            pltpu.VMEM((256, 4096), half),
            pltpu.VMEM((256, 4096), half),
            pltpu.VMEM((256, 1024), full),
            pltpu.VMEM((256, 1024), full),
            pltpu.VMEM((256, 1024), half),
            pltpu.VMEM((8, 256, 128), half),
            pltpu.VMEM((256, 1024), half),
            pltpu.SemaphoreType.DMA((20,)),
            pltpu.SemaphoreType.DMA((20,)),
            pltpu.SemaphoreType.DMA((3, 8)),
            pltpu.SemaphoreType.DMA((3, 8)),
        ],
        compiler_params=pltpu.CompilerParams(
            collective_id=1, has_side_effects=True, vmem_limit_bytes=60 << 20
        ),
        name="forward",
    )(*operands)


def reducer(near, bits, work, arrive, send_sem, recv_sem):
    def hop(chunk, kind, step):
        half = 32 >> step
        return pltpu.make_async_remote_copy(
            src_ref=work.at[chunk, pl.ds(SEND_AT[step], half)],
            dst_ref=arrive.at[chunk, pl.ds(ARRIVE_AT[step], half)],
            send_sem=send_sem.at[chunk, step],
            recv_sem=recv_sem.at[chunk, step],
            device_id=near[class_dims(kind)[step]],
            device_id_type=MESH,
        )

    def put(chunk, kind, result):
        before, after = split_shape(kind, 0)
        own = bits[class_dims(kind)[0]]
        for a in range(before):
            for bit in (0, 1):
                other = own if bit == 0 else 1 - own
                piece = result[(2 * a + bit) * after : (2 * a + bit + 1) * after]
                work[chunk, pl.ds(other * 32 + a * after, after)] = piece
        hop(chunk, kind, 0).start()

    def advance(chunk, kind, step, finish):
        hop(chunk, kind, step).wait_recv()
        keep, come_at = KEEP_AT[step], ARRIVE_AT[step]
        if step == 5:
            finish(
                work[chunk, keep].astype(jnp.float32) + arrive[chunk, come_at].astype(jnp.float32)
            )
            return
        if step == 0:
            hop(chunk, kind, 0).wait_send()
        before, after = split_shape(kind, step + 1)
        own = bits[class_dims(kind)[step + 1]]
        for bit, base in ((1 - own, SEND_AT[step + 1]), (own, KEEP_AT[step + 1])):

            def merge(a, carry, bit=bit, base=base):
                at = (2 * a + bit) * after
                work[chunk, pl.ds(base + a * after, after)] = (
                    work[chunk, pl.ds(keep + at, after)] + arrive[chunk, pl.ds(come_at + at, after)]
                )
                return carry

            lax.fori_loop(0, before, merge, 0, unroll=min(before, 8))
            if base == SEND_AT[step + 1]:
                hop(chunk, kind, step + 1).start()

    def drain(chunk, kind):
        for step in range(1, 6):
            hop(chunk, kind, step).wait_send()

    return put, advance, drain


def exchanger(core, partner, ex_send, ex_recv, ex_local):
    made = []

    def exchange(source, dest, cut=None):
        index = len(made)

        def part(owner):
            if cut is None:
                return source
            at, span = cut
            return source.at[:, pl.ds(pl.multiple_of(at + owner * span, 128), span)]

        made.append(
            (
                pltpu.make_async_copy(part(core), dest(0), ex_local.at[index]),
                pltpu.make_async_remote_copy(
                    src_ref=part(1 - core),
                    dst_ref=dest(1),
                    send_sem=ex_send.at[index],
                    recv_sem=ex_recv.at[index],
                    device_id=partner,
                    device_id_type=MESH,
                ),
            )
        )
        return made[-1]

    def whole(source, buf):
        return [exchange(source, lambda half: buf.at[pl.ds(256 * half, 256), :])]

    def halves(source, buf, span):
        return [
            exchange(
                source,
                lambda half, high=high: buf.at[pl.ds(256 * half, 256), pl.ds(high * span, span)],
                (high * 2 * span, span),
            )
            for high in (0, 1)
        ]

    return exchange, whole, halves, made


def begin(copies):
    for local, remote in copies:
        remote.start()
        local.start()


def arrived(copies):
    for local, remote in copies:
        local.wait()
        remote.wait_recv()


def greet(targets):
    barrier = pltpu.get_barrier_semaphore()
    for target in targets:
        pl.semaphore_signal(barrier, inc=1, device_id=target, device_id_type=MESH)
    pl.semaphore_wait(barrier, len(targets))


def turn_rows(buf, dest):
    turned = buf[...].astype(jnp.float32).T
    dest[...] = jnp.concatenate(
        [turned[8 * block : 8 * block + 8] for block in BLOCKS], axis=0
    ).astype(jnp.bfloat16)


def chunk_product(left, right_a, right_b):
    a = jnp.dot(left, right_a, preferred_element_type=jnp.float32)
    b = jnp.dot(left, right_b, preferred_element_type=jnp.float32)
    return jnp.concatenate((a.reshape(64, 8, 256), b.reshape(64, 8, 256)), axis=1).astype(
        jnp.bfloat16
    )


def wide_finish(dest, tile):
    def finish(total):
        dest[:, 512 * tile : 512 * tile + 256] = total[:8]
        dest[:, 512 * tile + 256 : 512 * tile + 512] = total[8:]

    return finish


def attention_back_kernel(
    att_in, gbr_in, n2_in, gpre_in, hid_in, gout_in, q_in, kv_in, lse, gatt_in, mask_in,
    gp_out, out_out, fc1_out, fc2_out,
    x_buf, xh_buf, gbr_buf, gpre_buf, gout_buf, xt_buf, xht_buf, work, arrive,
    q_pairs, kv, gatt, mask, near_send, near_come, far_send, far_come, held, far_held, whole_grad, packed,
    ex_send, ex_recv, ex_local, send_sem, recv_sem, load_sem, kv_send_sem, kv_recv_sem,
):
    where = place()
    x_hi, core, x_lo, y, z = where
    near = neighbours(where)
    bits = own_bits(where)
    partner = near["core"]
    across = ((1 - x_hi) * 2 + core, x_lo * 16 + y * 4 + z)

    loads = []
    for source, dest in ((q_in, q_pairs), (kv_in, kv), (gatt_in, gatt), (mask_in, mask)):
        loads.append(pltpu.make_async_copy(source, dest, load_sem.at[len(loads)]))
        loads[-1].start()
    greet(tuple(near.values()) + (across,))

    put, advance, drain = reducer(near, bits, work, arrive, send_sem, recv_sem)
    _, whole, halves, made = exchanger(core, partner, ex_send, ex_recv, ex_local)
    groups = {
        "fc2": halves(hid_in, xh_buf, 1024) + whole(gout_in, gout_buf),
        "fc1": halves(n2_in, x_buf.at[0], 256) + whole(gpre_in, gpre_buf),
        "out": halves(att_in, x_buf.at[1], 256) + whole(gbr_in, gbr_buf),
    }
    for name in groups:
        begin(groups[name])

    plan = [("fc2", tile) for tile in range(8)] + [("fc1", tile) for tile in range(8)]
    plan += [("out", tile) for tile in range(2)]
    ready = set()

    def compute(chunk):
        name, tile = plan[chunk]
        if name not in ready:
            ready.add(name)
            arrived(groups[name])
            if name == "fc2":
                turned = xh_buf[...].astype(jnp.float32).T.astype(jnp.bfloat16)
                xht_buf[...] = jnp.concatenate(
                    [turned[32 * block : 32 * block + 32] for block in BLOCKS], axis=0
                )
            else:
                index = 0 if name == "fc1" else 1
                turn_rows(x_buf.at[index], xt_buf.at[index])
        if name != "fc2":
            right = gpre_buf if name == "fc1" else gbr_buf
            put(
                chunk,
                chunk % 6,
                chunk_product(
                    xt_buf[0 if name == "fc1" else 1],
                    right[:, 512 * tile : 512 * tile + 256],
                    right[:, 512 * tile + 256 : 512 * tile + 512],
                ),
            )
        elif tile % 2 == 0:
            both = jnp.dot(
                xht_buf[...],
                gout_buf[:, 128 * tile : 128 * tile + 256],
                preferred_element_type=jnp.float32,
            ).reshape(64, 32, 256)
            put(chunk, chunk % 6, both[:, :16].astype(jnp.bfloat16))
            put(chunk + 1, (chunk + 1) % 6, both[:, 16:].astype(jnp.bfloat16))

    def finisher(chunk):
        name, tile = plan[chunk]
        if name == "fc2":

            def finish(total):
                at = 16 * (tile % 2)
                fc2_out[at : at + 16, 128 * (tile - tile % 2) : 128 * (tile - tile % 2) + 256] = total

            return finish
        return wide_finish(fc1_out if name == "fc1" else out_out, tile)

    def wave(index):
        for chunk in range(6 * index, 6 * index + 6):
            compute(chunk)

    def step_wave(index, step):
        for chunk in range(6 * index, 6 * index + 6):
            advance(chunk, chunk % 6, step, finisher(chunk))

    def block_at(high, low):
        return pl.ds(pl.multiple_of((high * 2 + low) * 256, 256), 256)

    def near_copy(pair):
        return pltpu.make_async_remote_copy(
            src_ref=near_send.at[pair],
            dst_ref=near_come.at[pair],
            send_sem=kv_send_sem.at[0, pair],
            recv_sem=kv_recv_sem.at[0, pair],
            device_id=partner,
            device_id_type=MESH,
        )

    def far_copy(pair):
        return pltpu.make_async_remote_copy(
            src_ref=far_send.at[pair],
            dst_ref=far_come.at[pair],
            send_sem=kv_send_sem.at[1, pair],
            recv_sem=kv_recv_sem.at[1, pair],
            device_id=across,
            device_id_type=MESH,
        )

    def heads_back(pair):
        at = lax.broadcasted_iota(jnp.int32, (128, 256), 0)
        lane = lax.broadcasted_iota(jnp.int32, (256, 128), 1)
        query = q_pairs[pair].astype(jnp.float32)
        grad = gatt[pair].astype(jnp.float32)
        query_t, grad_t = query.T, grad.T
        key_rows = kv[pair, 0].T
        key_grad = value_grad = None
        query_grads = []
        for head in (0, 1):
            own = (at < 64) if head == 0 else (at >= 64)
            mine = (lane < 64) if head == 0 else (lane >= 64)
            scores = (
                jnp.dot(
                    kv[pair, 0],
                    jnp.where(own, query_t, 0.0).astype(jnp.bfloat16),
                    preferred_element_type=jnp.float32,
                )
                + mask[...]
            )
            probs = jnp.exp(scores - lse[pair, head : head + 1, :])
            prob_grad = jnp.dot(
                kv[pair, 1],
                jnp.where(own, grad_t, 0.0).astype(jnp.bfloat16),
                preferred_element_type=jnp.float32,
            )
            mean = jnp.sum(probs * prob_grad, axis=0, keepdims=True)
            score_grad = (probs * (prob_grad - mean)).astype(jnp.bfloat16)
            query_grads.append(
                jnp.dot(
                    key_rows[64 * head : 64 * head + 64],
                    score_grad,
                    preferred_element_type=jnp.float32,
                )
            )
            key_part = jnp.dot(
                score_grad,
                jnp.where(mine, query, 0.0).astype(jnp.bfloat16),
                preferred_element_type=jnp.float32,
            )
            value_part = jnp.dot(
                probs.astype(jnp.bfloat16),
                jnp.where(mine, grad, 0.0).astype(jnp.bfloat16),
                preferred_element_type=jnp.float32,
            )
            key_grad = key_part if head == 0 else key_grad + key_part
            value_grad = value_part if head == 0 else value_grad + value_part
        packed[:, 128 * pair : 128 * pair + 128] = (
            jnp.concatenate(query_grads, axis=0).T * HD ** (-0.5)
        ).astype(jnp.bfloat16)
        whole_grad[0] = key_grad
        whole_grad[1] = value_grad
        for kind in (0, 1):
            near_send[pair, 0, kind] = whole_grad[kind, block_at(x_hi, 1 - core), :].astype(
                jnp.bfloat16
            )
            near_send[pair, 1, kind] = whole_grad[kind, block_at(1 - x_hi, 1 - core), :].astype(
                jnp.bfloat16
            )
        near_copy(pair).start()
        for kind in (0, 1):
            held[pair, kind] = whole_grad[kind, block_at(x_hi, core), :]
            far_held[pair % 2, kind] = whole_grad[kind, block_at(1 - x_hi, core), :]

    def pass_far(pair):
        near_copy(pair).wait_recv()
        for kind in (0, 1):
            far_send[pair, kind] = (
                far_held[pair % 2, kind] + near_come[pair, 1, kind].astype(jnp.float32)
            ).astype(jnp.bfloat16)
        far_copy(pair).start()

    def close(pair):
        far_copy(pair).wait_recv()
        for kind in (0, 1):
            at = 1024 * (kind + 1) + 128 * pair
            packed[:, at : at + 128] = (
                held[pair, kind]
                + near_come[pair, 0, kind].astype(jnp.float32)
                + far_come[pair, kind].astype(jnp.float32)
            ).astype(jnp.bfloat16)

    for copy in loads:
        copy.wait()
    heads_back(0)
    wave(0)
    heads_back(1)
    pass_far(0)
    wave(1)
    heads_back(2)
    pass_far(1)
    step_wave(0, 0)
    heads_back(3)
    pass_far(2)
    close(0)
    wave(2)
    later = (
        ((1, 0), (0, 1)),
        ((2, 0), (1, 1), (0, 2)),
        ((2, 1), (1, 2), (0, 3)),
        ((2, 2), (1, 3), (0, 4)),
    )
    for pair in range(4, 8):
        heads_back(pair)
        pass_far(pair - 1)
        close(pair - 3)
        for index, step in later[pair - 4]:
            step_wave(index, step)
    pass_far(7)
    close(5)
    for index, step in ((2, 3), (1, 4), (0, 5)):
        step_wave(index, step)
    close(6)
    close(7)
    out = pltpu.make_async_copy(packed, gp_out, load_sem.at[4])
    out.start()
    for index, step in ((2, 4), (1, 5), (2, 5)):
        step_wave(index, step)
    out.wait()
    for _, remote in made:
        remote.wait_send()
    for pair in range(8):
        near_copy(pair).wait_send()
        far_copy(pair).wait_send()
    for chunk in range(18):
        drain(chunk, chunk % 6)


def attention_back(*operands):
    any_space = pl.BlockSpec(memory_space=pl.ANY)
    in_vmem = pl.BlockSpec(memory_space=pltpu.VMEM)
    half, full = jnp.bfloat16, jnp.float32
    shape = jax.ShapeDtypeStruct
    return pl.pallas_call(
        attention_back_kernel,
        out_shape=(
            shape((256, 3072), half),
            shape((8, 1024), full),
            shape((8, 4096), full),
            shape((32, 1024), full),
        ),
        in_specs=[any_space] * 8 + [in_vmem] + [any_space] * 2,
        out_specs=(any_space,) + (in_vmem,) * 3,
        scratch_shapes=[
            pltpu.VMEM((2, 512, 512), half),
            pltpu.VMEM((512, 2048), half),
            pltpu.VMEM((512, 1024), half),
            pltpu.VMEM((512, 4096), half),
            pltpu.VMEM((512, 1024), half),
            pltpu.VMEM((2, 512, 512), half),
            pltpu.VMEM((2048, 512), half),
            pltpu.VMEM((18, 64, 16, 256), half),
            pltpu.VMEM((18, 63, 16, 256), half),
            pltpu.VMEM((8, 256, 128), half),
            pltpu.VMEM((8, 2, 1024, 128), half),
            pltpu.VMEM((8, 256, 128), half),
            pltpu.VMEM((1024, 256), full),
            pltpu.VMEM((8, 2, 2, 256, 128), half),
            pltpu.VMEM((8, 2, 2, 256, 128), half),
            pltpu.VMEM((8, 2, 256, 128), half),
            pltpu.VMEM((8, 2, 256, 128), half),
            pltpu.VMEM((8, 2, 256, 128), full),
            pltpu.VMEM((2, 2, 256, 128), full),
            pltpu.VMEM((2, 1024, 128), full),
            pltpu.VMEM((256, 3072), half),
            pltpu.SemaphoreType.DMA((9,)),
            pltpu.SemaphoreType.DMA((9,)),
            pltpu.SemaphoreType.DMA((9,)),
            pltpu.SemaphoreType.DMA((18, 6)),
            pltpu.SemaphoreType.DMA((18, 6)),
            pltpu.SemaphoreType.DMA((5,)),
            pltpu.SemaphoreType.DMA((2, 8)),
            pltpu.SemaphoreType.DMA((2, 8)),
        ],
        compiler_params=pltpu.CompilerParams(
            collective_id=2, has_side_effects=True, vmem_limit_bytes=60 << 20
        ),
        name="attention_back",
    )(*operands)


def input_back_kernel(
    gp_in, n1_in, stream_in, gmid_in, pix_in, hot_in, sums, vectors, emb_in, qkv_in,
    pix_out, emb_out, qkv_out, bias_out,
    gp_buf, x_buf, pix_buf, hot_buf, row_buf, lanes, xt_buf, work, arrive, work_f, arrive_f,
    stream, gmid, emb_w, qkv_w, gs, pix_grad,
    ex_send, ex_recv, ex_local, send_sem, recv_sem, send_f, recv_f, load_sem,
):
    where = place()
    x_hi, core, x_lo, y, z = where
    near = neighbours(where)
    bits = own_bits(where)
    partner = near["core"]

    loads = []
    for source, dest in ((qkv_in, qkv_w), (stream_in, stream), (gmid_in, gmid), (emb_in, emb_w)):
        loads.append(pltpu.make_async_copy(source, dest, load_sem.at[len(loads)]))
        loads[-1].start()
    greet(tuple(near.values()))
    put, advance, drain = reducer(near, bits, work, arrive, send_sem, recv_sem)
    put_f, advance_f, drain_f = reducer(near, bits, work_f, arrive_f, send_f, recv_f)
    exchange, whole, halves, made = exchanger(core, partner, ex_send, ex_recv, ex_local)
    gp_copies = whole(gp_in, gp_buf)
    n1_copies = halves(n1_in, x_buf.at[0], 256)
    side_copies = whole(pix_in, pix_buf) + whole(hot_in, hot_buf)
    gs_copies = halves(gs, x_buf.at[1], 256)
    row_copies = [exchange(lanes.at[pl.ds(0, 16), :], lambda half: row_buf.at[half])]
    begin(gp_copies)
    begin(n1_copies)
    begin(side_copies)

    for copy in loads[:3]:
        copy.wait()
    gp_copies[0][0].wait()
    grown = nt_dot(gp_buf[0:256, :], qkv_w[...])
    hat, scale = norm_parts(stream[...])
    lanes[...] = jnp.zeros_like(lanes)
    lanes[4:5, :] = jnp.sum(grown * hat, axis=0, keepdims=True)
    lanes[5:6, :] = jnp.sum(grown, axis=0, keepdims=True)
    grown = grown * vectors[ROW_GAIN1 : ROW_GAIN1 + 1, :]
    gs[...] = (
        gmid[...]
        + scale
        * (
            grown
            - jnp.mean(grown, axis=-1, keepdims=True)
            - hat * jnp.mean(grown * hat, axis=-1, keepdims=True)
        )
    ).astype(jnp.bfloat16)
    begin(gs_copies)

    gp_copies[0][1].wait_recv()
    arrived(n1_copies)
    turn_rows(x_buf.at[0], xt_buf.at[0])
    for tile in range(6):
        put(
            tile,
            tile,
            chunk_product(
                xt_buf[0],
                gp_buf[:, 512 * tile : 512 * tile + 256],
                gp_buf[:, 512 * tile + 256 : 512 * tile + 512],
            ),
        )

    arrived(side_copies)
    lanes[6:7, :] = jnp.sum(gp_buf[0:256, 0:1024].astype(jnp.float32), axis=0, keepdims=True)
    lanes[7:8, :] = jnp.sum(gp_buf[0:256, 2048:3072].astype(jnp.float32), axis=0, keepdims=True)
    lanes[0:4, :] = tn_dot(hot_buf[0:256, :].astype(jnp.bfloat16), gs[...])[0:4]
    lanes[8:16, :] = sums[...]
    begin(row_copies)

    arrived(gs_copies)
    turn_rows(x_buf.at[1], xt_buf.at[1])

    def band_pixels(tile):
        band, at = tile // 3, tile % 3
        picked = pix_buf[:, 256 * at : 256 * at + 256].astype(jnp.float32)
        return (picked * hot_buf[:, band : band + 1]).astype(jnp.bfloat16)

    for tile in range(6):
        put(
            6 + tile,
            tile,
            chunk_product(xt_buf[1], band_pixels(2 * tile), band_pixels(2 * tile + 1)),
        )

    def step_wave(index, step):
        for tile in range(6):
            dest = qkv_out if index == 0 else emb_out
            advance(6 * index + tile, tile, step, wide_finish(dest, tile))

    def finish_bias(total):
        bias_out[...] = total

    arrived(row_copies)
    row_copies[0][1].wait_send()
    lanes[0:16, :] = row_buf[0] + row_buf[1]
    turned = jnp.concatenate(
        [lanes[:, pl.ds(pl.multiple_of(high * 512 + core * 256, 128), 256)].T for high in (0, 1)],
        axis=0,
    ).reshape(64, 8, 128)
    put_f(0, 0, jnp.concatenate([turned[b : b + 1] for b in BLOCKS], axis=0))
    step_wave(0, 0)

    loads[3].wait()
    total = None
    for band in range(4):
        term = hot_buf[0:256, band : band + 1] * nt_dot(
            gs[...], emb_w[768 * band : 768 * band + 768, :]
        )
        total = term if total is None else total + term
    pix_grad[...] = total.astype(jnp.bfloat16)
    out = pltpu.make_async_copy(pix_grad, pix_out, load_sem.at[4])
    out.start()

    for step in range(6):
        step_wave(1, step)
        advance_f(0, 0, step, finish_bias)
        if step < 5:
            step_wave(0, step + 1)
    out.wait()
    for _, remote in made[:-1]:
        remote.wait_send()
    for chunk in range(12):
        drain(chunk, chunk % 6)
    drain_f(0, 0)


def input_back(*operands):
    any_space = pl.BlockSpec(memory_space=pl.ANY)
    in_vmem = pl.BlockSpec(memory_space=pltpu.VMEM)
    half, full = jnp.bfloat16, jnp.float32
    shape = jax.ShapeDtypeStruct
    return pl.pallas_call(
        input_back_kernel,
        out_shape=(
            shape((256, 768), half),
            shape((8, 3072), full),
            shape((8, 3072), full),
            shape((8, 128), full),
        ),
        in_specs=[any_space] * 6 + [in_vmem] * 2 + [any_space] * 2,
        out_specs=(any_space,) + (in_vmem,) * 3,
        scratch_shapes=[
            pltpu.VMEM((512, 3072), half),
            pltpu.VMEM((2, 512, 512), half),
            pltpu.VMEM((512, 768), half),
            pltpu.VMEM((512, 128), full),
            pltpu.VMEM((2, 16, 1024), full),
            pltpu.VMEM((128, 1024), full),
            pltpu.VMEM((2, 512, 512), half),
            pltpu.VMEM((12, 64, 16, 256), half),
            pltpu.VMEM((12, 63, 16, 256), half),
            pltpu.VMEM((1, 64, 8, 128), full),
            pltpu.VMEM((1, 63, 8, 128), full),
            pltpu.VMEM((256, 1024), full),
            pltpu.VMEM((256, 1024), full),
            pltpu.VMEM((3072, 1024), half),
            pltpu.VMEM((1024, 3072), half),
            pltpu.VMEM((256, 1024), half),
            pltpu.VMEM((256, 768), half),
            pltpu.SemaphoreType.DMA((8,)),
            pltpu.SemaphoreType.DMA((8,)),
            pltpu.SemaphoreType.DMA((8,)),
            pltpu.SemaphoreType.DMA((12, 6)),
            pltpu.SemaphoreType.DMA((12, 6)),
            pltpu.SemaphoreType.DMA((1, 6)),
            pltpu.SemaphoreType.DMA((1, 6)),
            pltpu.SemaphoreType.DMA((5,)),
        ],
        compiler_params=pltpu.CompilerParams(
            collective_id=3, has_side_effects=True, vmem_limit_bytes=60 << 20
        ),
        name="input_back",
    )(*operands)


def on_device(
    pixels,
    positions,
    segments,
    groups,
    cotangent,
    emb_weight,
    emb_bias,
    norm1_gain,
    norm1_bias,
    qkv_weight,
    query_bias,
    value_bias,
    out_weight,
    out_bias,
    norm2_gain,
    norm2_bias,
    fc1_weight,
    fc1_bias,
    fc2_weight,
    fc2_bias,
):
    rows_dev, slice_len, pix_len = pixels.shape
    model_width = qkv_weight.shape[0]
    band_count = emb_weight.shape[0]
    tok_count = rows_dev * slice_len
    query_seg = lax.dynamic_slice_in_dim(
        segments, lax.axis_index("blk") * slice_len, slice_len, 1
    )
    band = groups.reshape(tok_count, 1)
    lane = jnp.arange(128, dtype=jnp.int32)[None, :]
    hot_live = jnp.where(
        lane == band_count,
        (query_seg >= 0).reshape(tok_count, 1),
        (lane == band) & (lane < band_count),
    ).astype(jnp.float32)
    mask = jnp.where(segments[0][:, None] == query_seg[0][None, :], 0.0, MASKED)
    vectors = jnp.concatenate(
        (
            emb_bias,
            jnp.stack(
                (
                    norm1_gain,
                    norm1_bias,
                    query_bias,
                    value_bias,
                    out_bias,
                    norm2_gain,
                    norm2_bias,
                    fc2_bias,
                )
            ),
            fc1_bias.reshape(4, 1024),
        )
    )
    flat_pixels = pixels.reshape(tok_count, pix_len)
    flat_emb = emb_weight.reshape(band_count * pix_len, model_width)
    (
        block_out,
        stream,
        normed_one,
        query_pairs,
        key_value,
        log_sums,
        attended,
        normed_two,
        hidden,
        pre_grad,
        upstream,
        branch_grad,
        attended_grad,
        middle_grad,
        row_sums,
    ) = forward(
        flat_pixels,
        positions.reshape(tok_count, model_width),
        cotangent.reshape(tok_count, model_width),
        hot_live,
        mask,
        vectors,
        flat_emb,
        qkv_weight,
        out_weight,
        fc1_weight,
        fc2_weight,
    )
    packed_grad, out_sum, fc1_sum, fc2_sum = attention_back(
        attended,
        branch_grad,
        normed_two,
        pre_grad,
        hidden,
        upstream,
        query_pairs,
        key_value,
        log_sums,
        attended_grad,
        mask,
    )
    row_sums = jnp.concatenate(
        (
            row_sums[:4],
            jnp.swapaxes(row_sums[4:].reshape(128, 4, 8), 0, 1).reshape(4, 1024),
        )
    )
    pixel_grad, emb_sum, qkv_sum, bias_sum = input_back(
        packed_grad,
        normed_one,
        stream,
        middle_grad,
        flat_pixels,
        hot_live,
        row_sums,
        vectors,
        flat_emb,
        qkv_weight,
    )
    bias_cols = bias_sum[:, :16].T
    return (
        block_out.reshape(rows_dev, slice_len, model_width),
        pixel_grad.reshape(rows_dev, slice_len, pix_len),
        emb_sum.T.reshape(band_count, pix_len, 8),
        bias_cols[0:4],
        bias_cols[4],
        bias_cols[5],
        qkv_sum,
        bias_cols[6],
        bias_cols[7],
        out_sum,
        bias_cols[8],
        bias_cols[9],
        bias_cols[10],
        fc1_sum,
        bias_cols[12:16].reshape(32),
        fc2_sum,
        bias_cols[11],
    )


def solution(mesh):
    return jax.shard_map(
        on_device,
        mesh=mesh,
        in_specs=(
            P("batch", "blk", None),
            P("batch", "blk", None),
            P("batch", None),
            P("batch", "blk"),
            P("batch", "blk", None),
            P(),
            P(),
            P(),
            P(),
            P(),
            P(),
            P(),
            P(),
            P(),
            P(),
            P(),
            P(),
            P(),
            P(),
            P(),
        ),
        out_specs=(
            P("batch", "blk", None),
            P("batch", "blk", None),
            P(None, None, ("blk", "batch")),
            P(None, ("blk", "batch")),
            P(("blk", "batch")),
            P(("blk", "batch")),
            P(("blk", "batch"), None),
            P(("blk", "batch")),
            P(("blk", "batch")),
            P(("blk", "batch"), None),
            P(("blk", "batch")),
            P(("blk", "batch")),
            P(("blk", "batch")),
            P(("blk", "batch"), None),
            P(("blk", "batch")),
            P(("blk", "batch"), None),
            P(("blk", "batch")),
        ),
        check_vma=False,
    )
```

```python
import jax
import jax.numpy as jnp
from jax import lax
from jax.experimental import pallas as pl
from jax.experimental.pallas import tpu as pltpu
from jax.sharding import PartitionSpec as P

HD = 64
NORM_EPS = 1e-06
MASKED = -1e30
VMEM_BYTES = 64 << 20

MESH = pl.DeviceIdType.MESH
AXES = ("xb", "xa", "yb", "ya", "zb", "za")
ROTATION = ("xa", "ya", "za", "xb", "yb", "zb")
GRAY = (0, 1, 3, 2)
BLOCKS = tuple(16 * x + 4 * y + z for x in GRAY for y in GRAY for z in GRAY)


def place():
    blk = lax.axis_index("blk")
    batch = lax.axis_index("batch")
    return blk // 2, blk % 2, batch // 16, (batch // 4) % 4, batch % 4


def neighbours(where):
    x_hi, core, x_lo, y, z = where

    def device(x_hi, core, x_lo, y, z):
        return (x_hi * 2 + core, x_lo * 16 + y * 4 + z)

    return {
        "core": device(x_hi, 1 - core, x_lo, y, z),
        "xa": device(x_hi, core, 1 - x_lo, y, z),
        "xb": device(1 - x_hi, core, 1 - x_lo, y, z),
        "ya": device(x_hi, core, x_lo, y + 1 - 2 * (y % 2), z),
        "yb": device(x_hi, core, x_lo, 3 - y, z),
        "za": device(x_hi, core, x_lo, y, z + 1 - 2 * (z % 2)),
        "zb": device(x_hi, core, x_lo, y, 3 - z),
    }


def own_bits(where):
    x_hi, _, x_lo, y, z = where
    return {
        "xb": x_hi,
        "xa": (x_hi + x_lo) % 2,
        "yb": y // 2,
        "ya": (y // 2 + y) % 2,
        "zb": z // 2,
        "za": (z // 2 + z) % 2,
    }


DIMS = (
    (2, 0, 4, 5, 1, 3),
    (1, 2, 4, 5, 0, 3),
    (0, 1, 2, 3, 4, 5),
    (1, 2, 3, 4, 5, 0),
    (0, 4, 5, 3, 1, 2),
    (2, 4, 5, 1, 0, 3),
    (2, 4, 5, 1, 0, 3),
    (3, 5, 1, 0, 2, 4),
    (4, 5, 1, 2, 3, 0),
    (4, 5, 0, 1, 2, 3),
    (1, 2, 4, 5, 3, 0),
    (5, 1, 2, 4, 0, 3),
    (3, 4, 5, 0, 1, 2),
    (4, 5, 1, 2, 3, 0),
    (5, 1, 2, 4, 3, 0),
    (1, 2, 3, 4, 5, 0),
    (2, 4, 5, 1, 0, 3),
    (5, 1, 2, 4, 0, 3),
    (2, 4, 5, 1, 3, 0),
    (0, 2, 4, 3, 5, 1),
    (1, 0, 2, 4, 5, 3),
    (4, 3, 5, 1, 2, 0),
    (5, 1, 2, 4, 0, 3),
    (3, 4, 5, 0, 1, 2),
    (0, 4, 5, 3, 1, 2),
    (1, 2, 4, 5, 3, 0),
    (1, 2, 3, 4, 5, 0),
    (4, 3, 5, 1, 2, 0),
    (2, 3, 4, 5, 0, 1),
    (5, 0, 1, 2, 3, 4),
)


def chunk_dims(chunk):
    return tuple(ROTATION[axis] for axis in DIMS[chunk])


def split_shape(dims, step):
    left = [axis for axis in AXES if axis not in dims[:step]]
    at = left.index(dims[step])
    return 2**at, 2 ** (len(left) - 1 - at)


KEEP_AT = (0, 32, 0, 0, 8, 12)
SEND_AT = (32, 48, 8, 4, 10, 13)
ARRIVE_AT = (0, 32, 48, 0, 4, 6)
SLOTS = 18


def reducer(near, bits, dims_of, buffers, send_sem, recv_sem, credit, chunks):
    work, arrive, work_end, arrive_end = buffers

    def held(chunk, step):
        return work.at[chunk % SLOTS] if step < 3 else work_end.at[chunk]

    def come(chunk, step):
        return arrive.at[chunk % SLOTS] if step < 3 else arrive_end.at[chunk]

    def hop(chunk, step):
        half = 32 >> step
        return pltpu.make_async_remote_copy(
            src_ref=held(chunk, step).at[pl.ds(SEND_AT[step], half)],
            dst_ref=come(chunk, step).at[pl.ds(ARRIVE_AT[step], half)],
            send_sem=send_sem.at[chunk, step],
            recv_sem=recv_sem.at[chunk, step],
            device_id=near[dims_of(chunk)[step]],
            device_id_type=MESH,
        )

    def send(chunk, step):
        if step < 3 and chunk >= SLOTS:
            pl.semaphore_wait(credit.at[chunk - SLOTS, step], 1)
        hop(chunk, step).start()

    def put(chunk, result):
        if chunk >= SLOTS:
            for step in (1, 2):
                hop(chunk - SLOTS, step).wait_send()
        dims = dims_of(chunk)
        before, after = split_shape(dims, 0)
        own = bits[dims[0]]
        for a in range(before):
            for bit in (0, 1):
                other = own if bit == 0 else 1 - own
                piece = result[(2 * a + bit) * after : (2 * a + bit + 1) * after]
                held(chunk, 0)[pl.ds(other * 32 + a * after, after)] = piece
        send(chunk, 0)

    def advance(chunk, step, finish):
        hop(chunk, step).wait_recv()
        keep, come_at = KEEP_AT[step], ARRIVE_AT[step]
        here, there = held(chunk, step), come(chunk, step)
        if step == 5:
            finish(here[keep].astype(jnp.float32) + there[come_at].astype(jnp.float32))
            return
        if step == 0:
            hop(chunk, 0).wait_send()
        dims = dims_of(chunk)
        before, after = split_shape(dims, step + 1)
        own = bits[dims[step + 1]]
        target = held(chunk, step + 1)
        for bit, base in ((1 - own, SEND_AT[step + 1]), (own, KEEP_AT[step + 1])):

            def merge(a, carry, bit=bit, base=base):
                at = (2 * a + bit) * after
                target[pl.ds(base + a * after, after)] = (
                    here[pl.ds(keep + at, after)] + there[pl.ds(come_at + at, after)]
                )
                return carry

            lax.fori_loop(0, before, merge, 0, unroll=min(before, 8))
            if base == SEND_AT[step + 1]:
                send(chunk, step + 1)
        if step < 3 and chunk + SLOTS < chunks:
            pl.semaphore_signal(
                credit.at[chunk, step],
                inc=1,
                device_id=near[dims_of(chunk + SLOTS)[step]],
                device_id_type=MESH,
            )

    def drain(chunk):
        for step in range(1 if chunk + SLOTS >= chunks else 3, 6):
            hop(chunk, step).wait_send()

    return put, advance, drain


def nt_dot(left, right):
    return lax.dot_general(left, right, (((1,), (1,)), ((), ())), preferred_element_type=jnp.float32)


def tn_dot(left, right):
    return lax.dot_general(left, right, (((0,), (0,)), ((), ())), preferred_element_type=jnp.float32)


def norm_parts(values):
    center = values - jnp.mean(values, axis=-1, keepdims=True)
    spread = jnp.mean(center * center, axis=-1, keepdims=True)
    scale = lax.rsqrt(spread + NORM_EPS)
    return center * scale, scale


def row(vector):
    return vector[...].reshape(1, 1024)


def forward_kernel(
    pix_in, pos_in, seg_in, band_in, emb_bias_in, gain1_in, bias1_in, query_bias_in, value_bias_in, emb_in, qkv_in,
    hot_out, mask_out, stream_out, n1_out, q_out, kv_out, lse_out, att_out,
    pix, pos, hot, mask, emb_w, qkv_w, stream, flat, n1, q_pairs, kv, att, *small,
):
    (
        seg, band_of, emb_bias, gain1, bias1, query_bias, value_bias,
        load_sem, save_sem, pair_sem, send_sem, recv_sem,
    ) = small
    where = place()
    x_hi, core, x_lo, y, z = where
    partner = (x_hi * 2 + 1 - core, x_lo * 16 + y * 4 + z)
    across = ((1 - x_hi) * 2 + core, x_lo * 16 + y * 4 + z)
    barrier = pltpu.get_barrier_semaphore()
    for target in (partner, across):
        pl.semaphore_signal(barrier, inc=1, device_id=target, device_id_type=MESH)

    loads = {}

    def load(name, source, dest):
        copy = pltpu.make_async_copy(source, dest, load_sem.at[len(loads)])
        copy.start()
        loads[name] = copy

    saves = []

    def save(source, dest):
        copy = pltpu.make_async_copy(source, dest, save_sem.at[len(saves)])
        copy.start()
        saves.append(copy)

    load("seg", seg_in, seg)
    load("band", band_in, band_of)
    load("pix", pix_in, pix)
    load("eb", emb_bias_in, emb_bias)
    load("g1", gain1_in, gain1)
    load("b1", bias1_in, bias1)
    load("qb", query_bias_in, query_bias)
    load("vb", value_bias_in, value_bias)
    for band in range(4):
        span = pl.ds(768 * band, 768)
        load("emb%d" % band, emb_in.at[span, :], emb_w.at[span, :])
    load("pos", pos_in, pos)
    for part in (1, 2, 0):
        span = pl.ds(1024 * part, 1024)
        load("qkv%d" % part, qkv_in.at[:, span], qkv_w.at[:, span])
    loads["seg"].wait()
    loads["band"].wait()
    own_seg = seg[:, pl.ds(pl.multiple_of((x_hi * 2 + core) * 256, 256), 256)]
    at = lax.broadcasted_iota(jnp.int32, (128, 256), 0)
    hot[...] = (
        jnp.where(at == band_of[...], 1.0, 0.0)
        + jnp.where(at == 4, 1.0, 0.0) * jnp.where(own_seg >= 0, 1.0, 0.0)
    ).T
    save(hot, hot_out)

    for name in ("eb", "g1", "b1", "qb", "vb"):
        loads[name].wait()
    flat[0:1, :] = row(query_bias)
    flat[1:2, :] = row(value_bias)

    loads["pix"].wait()
    total = None
    for band in range(4):
        chosen = hot[:, band : band + 1]
        picked = (pix[...].astype(jnp.float32) * chosen).astype(jnp.bfloat16)
        loads["emb%d" % band].wait()
        term = jnp.dot(
            picked, emb_w[768 * band : 768 * band + 768, :], preferred_element_type=jnp.float32
        ) + chosen * emb_bias[band : band + 1, :]
        total = term if total is None else total + term
    loads["pos"].wait()
    stream[...] = total + pos[...].astype(jnp.float32)
    save(stream, stream_out)
    hat, _ = norm_parts(stream[...])
    n1[...] = (
        hat * row(gain1) + row(bias1)
    ).astype(jnp.bfloat16)
    save(n1, n1_out)

    own_rows = pl.ds(pl.multiple_of((x_hi * 2 + core) * 256, 256), 256)
    far_rows = pl.ds(pl.multiple_of(((1 - x_hi) * 2 + core) * 256, 256), 256)

    def push(pair, which, rows_at, target):
        piece = kv.at[pair, :, rows_at, :]
        return pltpu.make_async_remote_copy(
            src_ref=piece,
            dst_ref=piece,
            send_sem=send_sem.at[which, pair],
            recv_sem=recv_sem.at[which, pair],
            device_id=target,
            device_id_type=MESH,
        )

    def to_across(pair):
        return push(pair, 0, own_rows, across)

    def to_partner(pair):
        return push(pair, 1, own_rows, partner)

    def forward_far(pair):
        return push(pair, 2, far_rows, partner)

    loads["qkv1"].wait()
    loads["qkv2"].wait()
    pl.semaphore_wait(barrier, 2)

    def project(tile, carry):
        span = pl.ds(pl.multiple_of(1024 + 256 * tile, 256), 256)
        keys = jnp.dot(n1[...], qkv_w[:, span], preferred_element_type=jnp.float32).astype(
            jnp.bfloat16
        )
        span = pl.ds(pl.multiple_of(2048 + 256 * tile, 256), 256)
        shift = flat[1:2, pl.ds(pl.multiple_of(256 * tile, 256), 256)]
        values = (
            jnp.dot(n1[...], qkv_w[:, span], preferred_element_type=jnp.float32) + shift
        ).astype(jnp.bfloat16)
        for side in (0, 1):
            kv[2 * tile + side, 0, own_rows, :] = keys[:, 128 * side : 128 * side + 128]
            kv[2 * tile + side, 1, own_rows, :] = values[:, 128 * side : 128 * side + 128]
            to_across(2 * tile + side).start()
            to_partner(2 * tile + side).start()
        return carry

    lax.fori_loop(0, 4, project, 0)
    loads["qkv0"].wait()

    def project_query(tile, carry):
        span = pl.ds(pl.multiple_of(256 * tile, 256), 256)
        query = (
            jnp.dot(n1[...], qkv_w[:, span], preferred_element_type=jnp.float32)
            + flat[0:1, span]
        ).astype(jnp.bfloat16)
        query = (query.astype(jnp.float32) * HD ** (-0.5)).astype(jnp.bfloat16)
        for side in (0, 1):
            q_pairs[2 * tile + side] = query[:, 128 * side : 128 * side + 128]
        return carry

    lax.fori_loop(0, 4, project_query, 0)
    save(q_pairs, q_out)
    key_seg = jnp.broadcast_to(seg[...].astype(jnp.float32), (128, 1024)).T[:, 0:1]
    mask[...] = jnp.where(key_seg == own_seg.astype(jnp.float32), 0.0, MASKED)
    save(mask, mask_out)

    def pass_on(pair):
        to_across(pair).wait_recv()
        forward_far(pair).start()

    pass_on(0)

    def attend(pair, carry):
        @pl.when(pair < 7)
        def _():
            pass_on(pair + 1)

        to_partner(pair).wait_recv()
        forward_far(pair).wait_recv()
        pltpu.make_async_copy(kv.at[pair], kv_out.at[pair], pair_sem.at[pair]).start()
        turned = q_pairs[pair].astype(jnp.float32).T
        at = lax.broadcasted_iota(jnp.int32, (128, 256), 0)
        value_rows = kv[pair, 1].T
        heads = []
        for head in (0, 1):
            own = (at < 64) if head == 0 else (at >= 64)
            mine = jnp.where(own, turned, 0.0).astype(jnp.bfloat16)
            scores = jnp.dot(kv[pair, 0], mine, preferred_element_type=jnp.float32) + mask[...]
            peak = jnp.max(scores, axis=0, keepdims=True)
            expo = jnp.exp(scores - peak)
            norm = jnp.sum(expo, axis=0, keepdims=True)
            heads.append(
                jnp.dot(
                    value_rows[64 * head : 64 * head + 64],
                    expo.astype(jnp.bfloat16),
                    preferred_element_type=jnp.float32,
                )
                / norm
            )
            lse_out[pair, head : head + 1, :] = peak + jnp.log(norm)
        att[:, pl.ds(pl.multiple_of(pair * 128, 128), 128)] = jnp.concatenate(
            heads, axis=0
        ).T.astype(jnp.bfloat16)
        return carry

    lax.fori_loop(0, 8, attend, 0)
    save(att, att_out)
    for copy in saves:
        copy.wait()

    def drain(pair, carry):
        to_across(pair).wait_send()
        to_partner(pair).wait_send()
        forward_far(pair).wait_send()
        pltpu.make_async_copy(kv.at[pair], kv_out.at[pair], pair_sem.at[pair]).wait()
        return carry

    lax.fori_loop(0, 8, drain, 0)


def forward(*operands):
    any_space = pl.BlockSpec(memory_space=pl.ANY)
    in_vmem = pl.BlockSpec(memory_space=pltpu.VMEM)
    half, full = jnp.bfloat16, jnp.float32
    shape = jax.ShapeDtypeStruct
    return pl.pallas_call(
        forward_kernel,
        out_shape=(
            shape((256, 128), full),
            shape((1024, 256), full),
            shape((256, 1024), full),
            shape((256, 1024), half),
            shape((8, 256, 128), half),
            shape((8, 2, 1024, 128), half),
            shape((8, 2, 256), full),
            shape((256, 1024), half),
        ),
        in_specs=[any_space] * 11,
        out_specs=(any_space,) * 6 + (in_vmem, any_space),
        scratch_shapes=[
            pltpu.VMEM((256, 768), half),
            pltpu.VMEM((256, 1024), half),
            pltpu.VMEM((256, 128), full),
            pltpu.VMEM((1024, 256), full),
            pltpu.VMEM((3072, 1024), half),
            pltpu.VMEM((1024, 3072), half),
            pltpu.VMEM((256, 1024), full),
            pltpu.VMEM((8, 1024), full),
            pltpu.VMEM((256, 1024), half),
            pltpu.VMEM((8, 256, 128), half),
            pltpu.VMEM((8, 2, 1024, 128), half),
            pltpu.VMEM((256, 1024), half),
            pltpu.VMEM((1, 1024), jnp.int32),
            pltpu.VMEM((1, 256), jnp.int32),
            pltpu.VMEM((4, 1024), full),
            pltpu.VMEM((1024,), full),
            pltpu.VMEM((1024,), full),
            pltpu.VMEM((1024,), full),
            pltpu.VMEM((1024,), full),
            pltpu.SemaphoreType.DMA((20,)),
            pltpu.SemaphoreType.DMA((8,)),
            pltpu.SemaphoreType.DMA((8,)),
            pltpu.SemaphoreType.DMA((3, 8)),
            pltpu.SemaphoreType.DMA((3, 8)),
        ],
        compiler_params=pltpu.CompilerParams(
            collective_id=1, has_side_effects=True, vmem_limit_bytes=VMEM_BYTES
        ),
        name="forward",
    )(*operands)


def exchanger(core, partner, ex_send, ex_recv, ex_local):
    made = []

    def exchange(source, dest, cut=None):
        index = len(made)

        def part(owner):
            if cut is None:
                return source
            at, span = cut
            return source.at[:, pl.ds(pl.multiple_of(at + owner * span, 128), span)]

        made.append(
            (
                pltpu.make_async_copy(part(core), dest(0), ex_local.at[index]),
                pltpu.make_async_remote_copy(
                    src_ref=part(1 - core),
                    dst_ref=dest(1),
                    send_sem=ex_send.at[index],
                    recv_sem=ex_recv.at[index],
                    device_id=partner,
                    device_id_type=MESH,
                ),
            )
        )
        return made[-1]

    def whole(source, buf):
        return [exchange(source, lambda half: buf.at[pl.ds(256 * half, 256), :])]

    def halves(source, buf, span):
        return [
            exchange(
                source,
                lambda half, high=high: buf.at[pl.ds(256 * half, 256), pl.ds(high * span, span)],
                (high * 2 * span, span),
            )
            for high in (0, 1)
        ]

    return exchange, whole, halves, made


def begin(copies):
    for local, remote in copies:
        remote.start()
        local.start()


def arrived(copies):
    for local, remote in copies:
        local.wait()
        remote.wait_recv()


def greet(targets):
    barrier = pltpu.get_barrier_semaphore()
    for target in targets:
        pl.semaphore_signal(barrier, inc=1, device_id=target, device_id_type=MESH)
    pl.semaphore_wait(barrier, len(targets))


def turn_rows(buf, dest):
    turned = buf[...].astype(jnp.float32).T
    dest[...] = jnp.concatenate(
        [turned[8 * block : 8 * block + 8] for block in BLOCKS], axis=0
    ).astype(jnp.bfloat16)


def chunk_product(left, right_a, right_b):
    a = jnp.dot(left, right_a, preferred_element_type=jnp.float32)
    b = jnp.dot(left, right_b, preferred_element_type=jnp.float32)
    return jnp.concatenate((a.reshape(64, 8, 256), b.reshape(64, 8, 256)), axis=1).astype(
        jnp.bfloat16
    )


def wide_finish(dest, tile):
    def finish(total):
        dest[:, 512 * tile : 512 * tile + 256] = total[:8]
        dest[:, 512 * tile + 256 : 512 * tile + 512] = total[8:]

    return finish


HEADS, FAR, CLOSE, GP, PUT, ADV, THROUGH, NORM, ROWS, BIAS, ADVB, PIX, POST, GATT = range(14)
SCHEDULE = (
    (POST,), (PUT, 0), (PUT, 2), (PUT, 8), (PUT, 11), (PUT, 12), (PUT, 6), (PUT, 4), (PUT, 9), (PUT, 14),
    (GATT,), (PUT, 10), (HEADS, 0), (ADV, 0, 0), (ADV, 8, 0), (ADV, 1, 0), (ADV, 2, 0), (ADV, 11, 0),
    (PUT, 13), (ADV, 12, 0), (HEADS, 1), (FAR, 0), (ADV, 6, 0), (HEADS, 2), (FAR, 1), (ADV, 7, 0),
    (ADV, 9, 0), (ADV, 3, 0), (ADV, 14, 0), (ADV, 4, 0), (HEADS, 3), (FAR, 2), (GP, 0), (ADV, 10, 0),
    (ADV, 8, 1), (ADV, 5, 0), (CLOSE, 0), (ADV, 0, 1), (HEADS, 4), (FAR, 3), (CLOSE, 1), (ADV, 13, 0),
    (ADV, 2, 1), (ADV, 7, 1), (ADV, 1, 1), (PUT, 15), (ADV, 12, 1), (PUT, 16), (FAR, 4), (ADV, 3, 1),
    (ADV, 9, 1), (ADV, 11, 1), (PUT, 17), (CLOSE, 2), (HEADS, 5), (CLOSE, 3), (GP, 2), (GP, 3),
    (ADV, 10, 1), (ADV, 2, 2), (ADV, 6, 1), (ADV, 14, 1), (ADV, 13, 1), (HEADS, 6), (FAR, 5), (CLOSE, 4),
    (ADV, 3, 2), (ADV, 4, 1), (ADV, 7, 2), (ADV, 8, 2), (ADV, 12, 2), (ADV, 5, 1), (PUT, 20), (ADV, 2, 3),
    (ADV, 9, 2), (FAR, 6), (HEADS, 7), (GP, 1), (ADV, 16, 0), (ADV, 0, 2), (ADV, 1, 2), (ADV, 15, 0),
    (ADV, 11, 2), (ADV, 17, 0), (CLOSE, 5), (ADV, 10, 2), (ADV, 6, 2), (PUT, 21), (ADV, 7, 3), (ADV, 3, 3),
    (ADV, 2, 4), (ADV, 14, 2), (THROUGH, 0), (FAR, 7), (ADV, 13, 2), (ADV, 4, 2), (ADV, 8, 3), (ADV, 12, 3),
    (PUT, 18), (PUT, 19), (ADV, 5, 2), (THROUGH, 1), (ADV, 0, 3), (THROUGH, 2), (CLOSE, 6), (ADV, 16, 1),
    (ADV, 15, 1), (ADV, 1, 3), (ADV, 10, 3), (THROUGH, 3), (ADV, 7, 4), (ADV, 11, 3), (ADV, 3, 4),
    (ADV, 13, 3), (ADV, 2, 5), (ADV, 20, 0), (CLOSE, 7), (GP, 4), (GP, 5), (THROUGH, 4), (ADV, 9, 3),
    (ADV, 4, 3), (ADV, 8, 4), (ADV, 16, 2), (THROUGH, 5), (NORM,), (ADV, 15, 2), (ADV, 10, 4), (ADV, 13, 4),
    (PUT, 22), (ADV, 17, 1), (PUT, 23), (ADV, 21, 0), (ADV, 6, 3), (ROWS,), (ADV, 18, 0), (ADV, 12, 4),
    (ADV, 14, 3), (ADV, 9, 4), (PUT, 25), (ADV, 5, 3), (ADV, 15, 3), (ADV, 19, 0), (ADV, 4, 4), (ADV, 0, 4),
    (PUT, 27), (ADV, 1, 4), (ADV, 11, 4), (ADV, 16, 3), (PUT, 28), (ADV, 17, 2), (PUT, 24), (PUT, 29),
    (PUT, 26), (ADV, 7, 5), (ADV, 3, 5), (ADV, 12, 5), (BIAS,), (PIX,), (ADV, 6, 4), (ADV, 5, 4),
    (ADV, 19, 1), (ADV, 20, 1), (ADV, 18, 1), (ADV, 8, 5), (ADV, 16, 4), (ADV, 22, 0), (ADV, 10, 5),
    (ADV, 13, 5), (ADV, 4, 5), (ADV, 15, 4), (ADV, 23, 0), (ADV, 25, 0), (ADV, 21, 1), (ADV, 14, 4),
    (ADV, 9, 5), (ADV, 0, 5), (ADV, 27, 0), (ADV, 1, 5), (ADV, 11, 5), (ADV, 6, 5), (ADV, 5, 5),
    (ADV, 17, 3), (ADV, 16, 5), (ADV, 28, 0), (ADV, 24, 0), (ADV, 29, 0), (ADV, 19, 2), (ADV, 20, 2),
    (ADV, 18, 2), (ADV, 26, 0), (ADVB, 0), (ADV, 15, 5), (ADV, 14, 5), (ADV, 21, 2), (ADV, 23, 1),
    (ADV, 27, 1), (ADV, 17, 4), (ADV, 25, 1), (ADV, 22, 1), (ADV, 18, 3), (ADV, 24, 1), (ADV, 28, 1),
    (ADV, 29, 1), (ADV, 23, 2), (ADV, 20, 3), (ADV, 19, 3), (ADV, 26, 1), (ADV, 17, 5), (ADVB, 1),
    (ADV, 21, 3), (ADV, 18, 4), (ADV, 27, 2), (ADV, 25, 2), (ADV, 22, 2), (ADV, 23, 3), (ADV, 24, 2),
    (ADV, 28, 2), (ADV, 29, 2), (ADV, 20, 4), (ADVB, 2), (ADV, 18, 5), (ADV, 19, 4), (ADV, 21, 4),
    (ADV, 26, 2), (ADV, 27, 3), (ADV, 25, 3), (ADV, 22, 3), (ADV, 23, 4), (ADV, 24, 3), (ADV, 28, 3),
    (ADV, 19, 5), (ADV, 29, 3), (ADV, 20, 5), (ADV, 21, 5), (ADVB, 3), (ADV, 26, 3), (ADV, 27, 4),
    (ADV, 25, 4), (ADV, 22, 4), (ADV, 23, 5), (ADV, 24, 4), (ADV, 28, 4), (ADV, 29, 4), (ADVB, 4),
    (ADV, 27, 5), (ADV, 26, 4), (ADV, 25, 5), (ADV, 22, 5), (ADV, 24, 5), (ADV, 28, 5), (ADV, 29, 5),
    (ADVB, 5), (ADV, 26, 5),
)


CHUNKS = 30


def backward_kernel(
    att_in, stream_in, cot_in, hot_in, mask_in, q_in, kv_in, lse_in, n1_in, pix_in,
    gain1_in, gain2_in, bias2_in, out_bias_in, fc1_bias_in, fc2_bias_in, emb_in, qkv_in, ow_in, fc1_in, fc2_in,
    block_out, pix_out, emb_out, qkv_out, out_out, fc1_out, fc2_out, bias_out,
    x_buf, hid, hid_come, gbr_buf, gpre_buf, gout_buf, gp_buf, pix_buf, hot_buf, row_buf, lanes, sums,
    xt_buf, xht_buf, work, arrive, work_end, arrive_end, work_f, arrive_f, work_end_f, arrive_end_f,
    q_pairs, kv, gatt, mask, near_send, near_come, far_send, far_come, held, far_held, whole_grad,
    n2, stream, middle, acc, grown_buf, gs, pix_grad, tall, wide,
    lse, gain1, gain2, bias2, out_bias, fc1_bias, fc2_bias,
    ex_send, ex_recv, ex_local, send_sem, recv_sem, credit, send_f, recv_f, load_sem, kv_sem, tall_sem, wide_sem,
    kv_send_sem, kv_recv_sem, kv_credit, gp_send, gp_recv, pre_send, pre_recv, tok_send, tok_recv,
):
    where = place()
    x_hi, core, x_lo, y, z = where
    near = neighbours(where)
    bits = own_bits(where)
    partner = near["core"]
    across = ((1 - x_hi) * 2 + core, x_lo * 16 + y * 4 + z)

    def kv_load(pair):
        return pltpu.make_async_copy(kv_in.at[pair], kv.at[pair % 2], kv_sem.at[pair % 2])

    order = (0, 1, 2, 4, 3, 5)

    def tall_load(index):
        if index < 8:
            source = fc1_in.at[:, pl.ds(512 * index, 512)]
        else:
            source = qkv_in.at[:, pl.ds(512 * order[index - 8], 512)]
        return pltpu.make_async_copy(source, tall.at[index % 3], tall_sem.at[index % 3])

    def wide_load(index):
        if index < 2 or index in (10, 11):
            source = ow_in.at[pl.ds(512 * (index % 2), 512), :]
        elif index < 10:
            source = fc2_in.at[pl.ds(512 * (index - 2), 512), :]
        else:
            source = emb_in.at[pl.ds(512 * (index - 12), 512), :]
        return pltpu.make_async_copy(source, wide.at[index % 3], wide_sem.at[index % 3])

    def used(load, index, last):
        if index + 3 < last:
            load(index + 3).start()

    loads = []
    for source, dest in (
        (att_in, n2), (stream_in, stream), (hot_in, hot_buf.at[pl.ds(0, 256), :]), (cot_in, gs),
        (gain1_in, gain1), (gain2_in, gain2), (bias2_in, bias2), (out_bias_in, out_bias),
        (fc1_bias_in, fc1_bias), (fc2_bias_in, fc2_bias), (lse_in, lse), (q_in, q_pairs), (mask_in, mask),
    ):
        loads.append(pltpu.make_async_copy(source, dest, load_sem.at[len(loads)]))
    loads[0].start()
    for index in range(2):
        wide_load(index).start()
    for copy in loads[1:10]:
        copy.start()
    wide_load(2).start()
    for index in range(3):
        tall_load(index).start()
    for copy in loads[10:]:
        copy.start()
    for pair in range(2):
        kv_load(pair).start()
    greet(tuple(near.values()) + (across,))

    put, advance, drain = reducer(
        near, bits, chunk_dims, (work, arrive, work_end, arrive_end), send_sem, recv_sem, credit, CHUNKS
    )
    put_f, advance_f, drain_f = reducer(
        near, bits, lambda chunk: ROTATION, (work_f, arrive_f, work_end_f, arrive_end_f),
        send_f, recv_f, None, 1,
    )
    exchange, whole, halves, made = exchanger(core, partner, ex_send, ex_recv, ex_local)
    groups = {
        "fc1": halves(n2, x_buf.at[0], 256),
        "out": halves(att_in, x_buf.at[1], 256),
        "qkv": halves(n1_in, x_buf.at[2], 256),
        "side": whole(pix_in, pix_buf),
        "emb": halves(gs, x_buf.at[0], 256),
        "rows": [exchange(lanes.at[pl.ds(0, 16), :], lambda half: row_buf.at[half])],
    }
    begin(groups["out"])
    begin(groups["qkv"])
    begin(groups["side"])

    def mirror(buf, index, span=slice(None)):
        return pltpu.make_async_remote_copy(
            src_ref=buf.at[pl.ds(0, 256), span],
            dst_ref=buf.at[pl.ds(256, 256), span],
            send_sem=tok_send.at[index],
            recv_sem=tok_recv.at[index],
            device_id=partner,
            device_id_type=MESH,
        )

    def gout_copy():
        return mirror(gout_buf, 0)

    def gbr_copy():
        return mirror(gbr_buf, 1)

    def hot_copy():
        return mirror(hot_buf, 2)

    def hid_copy(high):
        return pltpu.make_async_remote_copy(
            src_ref=hid.at[1 - core, :, pl.ds(1024 * high, 1024)],
            dst_ref=hid_come.at[:, pl.ds(1024 * high, 1024)],
            send_sem=tok_send.at[3 + high],
            recv_sem=tok_recv.at[3 + high],
            device_id=partner,
            device_id_type=MESH,
        )

    def gpre_copy(tile):
        span = pl.ds(512 * tile, 512)
        return pltpu.make_async_remote_copy(
            src_ref=gpre_buf.at[pl.ds(0, 256), span],
            dst_ref=gpre_buf.at[pl.ds(256, 256), span],
            send_sem=pre_send.at[tile],
            recv_sem=pre_recv.at[tile],
            device_id=partner,
            device_id_type=MESH,
        )

    def gp_copy(index):
        span = pl.ds(512 * order[index], 512)
        return pltpu.make_async_remote_copy(
            src_ref=gp_buf.at[pl.ds(0, 256), span],
            dst_ref=gp_buf.at[pl.ds(256, 256), span],
            send_sem=gp_send.at[index],
            recv_sem=gp_recv.at[index],
            device_id=partner,
            device_id_type=MESH,
        )

    plan = [("fc2", tile) for tile in range(8)] + [("fc1", tile) for tile in range(8)]
    plan += [("out", tile) for tile in range(2)] + [("qkv", index) for index in range(6)]
    plan += [("emb", tile) for tile in range(6)]
    turned_from = {"fc1": 0, "out": 1, "qkv": 2, "emb": 0}
    ready = set()

    def band_pixels(tile):
        band, at = tile // 3, tile % 3
        picked = pix_buf[:, 256 * at : 256 * at + 256].astype(jnp.float32)
        return (picked * hot_buf[:, band : band + 1]).astype(jnp.bfloat16)

    def turn_wide(buf, at):
        turned = buf[...].astype(jnp.float32).T.astype(jnp.bfloat16)
        xht_buf[:, at : at + 256] = jnp.concatenate(
            [turned[32 * block : 32 * block + 32] for block in BLOCKS], axis=0
        )

    def compute(chunk):
        name, tile = plan[chunk]
        if name not in ready:
            ready.add(name)
            if name == "fc2":
                turn_wide(hid.at[core], 0)
                for high in (0, 1):
                    hid_copy(high).wait_recv()
                turn_wide(hid_come, 256)
                gout_copy().wait_recv()
            else:
                arrived(groups[name])
                if name == "out":
                    gbr_copy().wait_recv()
                turn_rows(x_buf.at[turned_from[name]], xt_buf)
        if name == "fc2":
            if tile % 2 == 0:
                both = jnp.dot(
                    xht_buf[...],
                    gout_buf[:, 128 * tile : 128 * tile + 256],
                    preferred_element_type=jnp.float32,
                ).reshape(64, 32, 256)
                put(chunk, both[:, :16].astype(jnp.bfloat16))
                put(chunk + 1, both[:, 16:].astype(jnp.bfloat16))
            return
        if name == "emb":
            right = (band_pixels(2 * tile), band_pixels(2 * tile + 1))
        else:
            if name == "qkv":
                gp_copy(tile).wait_recv()
                tile = order[tile]
            if name == "fc1":
                gpre_copy(tile).wait_recv()
            buf = {"fc1": gpre_buf, "out": gbr_buf, "qkv": gp_buf}[name]
            right = (
                buf[:, 512 * tile : 512 * tile + 256],
                buf[:, 512 * tile + 256 : 512 * tile + 512],
            )
        put(chunk, chunk_product(xt_buf[...], *right))

    def finisher(chunk):
        name, tile = plan[chunk]
        if name == "fc2":

            def finish(total):
                at = 16 * (tile % 2)
                fc2_out[at : at + 16, 128 * (tile - tile % 2) : 128 * (tile - tile % 2) + 256] = total

            return finish
        if name == "qkv":
            tile = order[tile]
        return wide_finish({"fc1": fc1_out, "out": out_out, "qkv": qkv_out, "emb": emb_out}[name], tile)

    def wave(index):
        for chunk in range(6 * index, 6 * index + 6):
            compute(chunk)

    def step_wave(*pairs):
        for index, step in pairs:
            for chunk in range(6 * index, 6 * index + 6):
                advance(chunk, step, finisher(chunk))

    def block_at(high, low):
        return pl.ds(pl.multiple_of((high * 2 + low) * 256, 256), 256)

    def near_copy(pair):
        return pltpu.make_async_remote_copy(
            src_ref=near_send.at[pair % 2],
            dst_ref=near_come.at[pair % 4],
            send_sem=kv_send_sem.at[0, pair],
            recv_sem=kv_recv_sem.at[0, pair],
            device_id=partner,
            device_id_type=MESH,
        )

    def far_copy(pair):
        return pltpu.make_async_remote_copy(
            src_ref=far_send.at[pair % 2],
            dst_ref=far_come.at[pair],
            send_sem=kv_send_sem.at[1, pair],
            recv_sem=kv_recv_sem.at[1, pair],
            device_id=across,
            device_id_type=MESH,
        )

    def heads_back(pair):
        slot = pair % 2
        kv_load(pair).wait()
        at = lax.broadcasted_iota(jnp.int32, (128, 256), 0)
        lane = lax.broadcasted_iota(jnp.int32, (256, 128), 1)
        query = q_pairs[pair].astype(jnp.float32)
        grad = gatt[pair].astype(jnp.float32)
        query_t, grad_t = query.T, grad.T
        key_rows = kv[slot, 0].T
        key_grad = value_grad = None
        query_grads = []
        for head in (0, 1):
            own = (at < 64) if head == 0 else (at >= 64)
            mine = (lane < 64) if head == 0 else (lane >= 64)
            scores = (
                jnp.dot(
                    kv[slot, 0],
                    jnp.where(own, query_t, 0.0).astype(jnp.bfloat16),
                    preferred_element_type=jnp.float32,
                )
                + mask[...]
            )
            probs = jnp.exp(scores - lse[pair, head : head + 1, :])
            prob_grad = jnp.dot(
                kv[slot, 1],
                jnp.where(own, grad_t, 0.0).astype(jnp.bfloat16),
                preferred_element_type=jnp.float32,
            )
            mean = jnp.sum(probs * prob_grad, axis=0, keepdims=True)
            score_grad = (probs * (prob_grad - mean)).astype(jnp.bfloat16)
            query_grads.append(
                jnp.dot(
                    key_rows[64 * head : 64 * head + 64],
                    score_grad,
                    preferred_element_type=jnp.float32,
                )
            )
            key_part = jnp.dot(
                score_grad,
                jnp.where(mine, query, 0.0).astype(jnp.bfloat16),
                preferred_element_type=jnp.float32,
            )
            value_part = jnp.dot(
                probs.astype(jnp.bfloat16),
                jnp.where(mine, grad, 0.0).astype(jnp.bfloat16),
                preferred_element_type=jnp.float32,
            )
            key_grad = key_part if head == 0 else key_grad + key_part
            value_grad = value_part if head == 0 else value_grad + value_part
        if pair + 2 < 8:
            kv_load(pair + 2).start()
        if pair >= 2:
            near_copy(pair - 2).wait_send()
        gp_buf[0:256, 128 * pair : 128 * pair + 128] = (
            jnp.concatenate(query_grads, axis=0).T * HD ** (-0.5)
        ).astype(jnp.bfloat16)
        whole_grad[0] = key_grad
        whole_grad[1] = value_grad
        for kind in (0, 1):
            near_send[pair % 2, 0, kind] = whole_grad[kind, block_at(x_hi, 1 - core), :].astype(
                jnp.bfloat16
            )
            near_send[pair % 2, 1, kind] = whole_grad[kind, block_at(1 - x_hi, 1 - core), :].astype(
                jnp.bfloat16
            )
        if pair >= 4:
            pl.semaphore_wait(kv_credit.at[pair - 4], 1)
        near_copy(pair).start()
        for kind in (0, 1):
            held[pair % 2, kind] = whole_grad[kind, block_at(x_hi, core), :]
            far_held[pair % 2, kind] = whole_grad[kind, block_at(1 - x_hi, core), :]

    def pass_far(pair):
        near_copy(pair).wait_recv()
        if pair >= 2:
            far_copy(pair - 2).wait_send()
        for kind in (0, 1):
            far_send[pair % 2, kind] = (
                far_held[pair % 2, kind] + near_come[pair % 4, 1, kind].astype(jnp.float32)
            ).astype(jnp.bfloat16)
        far_copy(pair).start()
        for kind in (0, 1):
            at = 1024 * (kind + 1) + 128 * pair
            gp_buf[0:256, at : at + 128] = (
                held[pair % 2, kind] + near_come[pair % 4, 0, kind].astype(jnp.float32)
            ).astype(jnp.bfloat16)
        if pair < 4:
            pl.semaphore_signal(
                kv_credit.at[pair], inc=1, device_id=partner, device_id_type=MESH
            )

    def close(pair):
        far_copy(pair).wait_recv()
        for kind in (0, 1):
            at = 1024 * (kind + 1) + 128 * pair
            gp_buf[0:256, at : at + 128] = (
                gp_buf[0:256, at : at + 128].astype(jnp.float32)
                + far_come[pair, kind].astype(jnp.float32)
            ).astype(jnp.bfloat16)

    def through_qkv(index):
        tall_load(8 + index).wait()
        tile = order[index]
        part = nt_dot(gp_buf[0:256, 512 * tile : 512 * tile + 512], tall[(8 + index) % 3])
        grown_buf[...] = part if index == 0 else grown_buf[...] + part
        used(tall_load, 8 + index, 14)

    for copy in loads[:3] + loads[4:10]:
        copy.wait()
    hot_copy().start()
    total = stream[...] + row(out_bias)
    for index in (0, 1):
        wide_load(index).wait()
        total = total + jnp.dot(
            n2[:, 512 * index : 512 * index + 512], wide[index], preferred_element_type=jnp.float32
        )
        used(wide_load, index, 18)
    middle[...] = total
    hat, _ = norm_parts(total)
    n2[...] = (hat * row(gain2) + row(bias2)).astype(jnp.bfloat16)
    begin(groups["fc1"])
    loads[3].wait()
    gout_buf[0:256, :] = (gs[...].astype(jnp.float32) * hot_buf[0:256, 4:5]).astype(jnp.bfloat16)
    gout_copy().start()
    for tile in range(8):
        span = slice(512 * tile, 512 * tile + 512)
        tall_load(tile).wait()
        wide_load(2 + tile).wait()
        pre = jnp.dot(n2[...], tall[tile % 3], preferred_element_type=jnp.float32) + fc1_bias[
            span
        ].reshape(1, 512)
        cdf = 0.5 * (1.0 + lax.erf(pre * (0.5**0.5)))
        hidden = (pre * cdf).astype(jnp.bfloat16)
        at = 1024 * (tile // 4) + 512 * (tile % 2)
        hid[(tile // 2) % 2, :, at : at + 512] = hidden
        slope = cdf + pre * (jnp.exp(-0.5 * pre * pre) * 0.3989422804014327)
        back = (nt_dot(gout_buf[0:256, :], wide[(2 + tile) % 3]) * slope).astype(jnp.bfloat16)
        gpre_buf[0:256, span] = back
        gpre_copy(tile).start()
        ahead = jnp.dot(hidden, wide[(2 + tile) % 3], preferred_element_type=jnp.float32)
        used(wide_load, 2 + tile, 18)
        behind = nt_dot(back, tall[tile % 3])
        used(tall_load, tile, 14)
        acc[...] = ahead if tile == 0 else acc[...] + ahead
        grown_buf[...] = behind if tile == 0 else grown_buf[...] + behind
        quarter, at = tile // 2, 512 * (tile % 2)
        sums[4 + quarter : 5 + quarter, at : at + 512] = jnp.sum(
            back.astype(jnp.float32), axis=0, keepdims=True
        )
        if tile % 4 == 3:
            hid_copy(tile // 4).start()

    block_copy = pltpu.make_async_copy(gs, block_out, load_sem.at[13])

    def mlp_back():
        gs[...] = (
            hot_buf[0:256, 4:5] * (middle[...] + (acc[...] + row(fc2_bias)))
        ).astype(jnp.bfloat16)
        block_copy.start()
        upstream = gout_buf[0:256, :].astype(jnp.float32)
        sums[3:4, :] = jnp.sum(upstream, axis=0, keepdims=True)
        grown = grown_buf[...]
        hat, scale = norm_parts(middle[...])
        sums[1:2, :] = jnp.sum(grown * hat, axis=0, keepdims=True)
        sums[2:3, :] = jnp.sum(grown, axis=0, keepdims=True)
        grown = grown * row(gain2)
        middle[...] = upstream + scale * (
            grown
            - jnp.mean(grown, axis=-1, keepdims=True)
            - hat * jnp.mean(grown * hat, axis=-1, keepdims=True)
        )
        gbr_buf[0:256, :] = middle[...].astype(jnp.bfloat16)
        gbr_copy().start()
        sums[0:1, :] = jnp.sum(gbr_buf[0:256, :].astype(jnp.float32), axis=0, keepdims=True)

    def attention_grad():
        for index in (0, 1):
            wide_load(10 + index).wait()
            back = nt_dot(gbr_buf[0:256, :], wide[(10 + index) % 3]).astype(jnp.bfloat16)
            used(wide_load, 10 + index, 18)
            for pair in range(4):
                gatt[4 * index + pair] = back[:, 128 * pair : 128 * pair + 128]

    def norm_back():
        block_copy.wait()
        grown = grown_buf[...]
        hat, scale = norm_parts(stream[...])
        lanes[...] = jnp.zeros_like(lanes)
        lanes[4:5, :] = jnp.sum(grown * hat, axis=0, keepdims=True)
        lanes[5:6, :] = jnp.sum(grown, axis=0, keepdims=True)
        grown = grown * row(gain1)
        gs[...] = (
            middle[...]
            + scale
            * (
                grown
                - jnp.mean(grown, axis=-1, keepdims=True)
                - hat * jnp.mean(grown * hat, axis=-1, keepdims=True)
            )
        ).astype(jnp.bfloat16)
        begin(groups["emb"])
        arrived(groups["side"])
        hot_copy().wait_recv()

    def side_rows():
        lanes[6:7, :] = jnp.sum(gp_buf[0:256, 0:1024].astype(jnp.float32), axis=0, keepdims=True)
        lanes[7:8, :] = jnp.sum(gp_buf[0:256, 2048:3072].astype(jnp.float32), axis=0, keepdims=True)
        lanes[0:4, :] = tn_dot(hot_buf[0:256, :].astype(jnp.bfloat16), gs[...])[0:4]
        lanes[8:16, :] = sums[...]
        begin(groups["rows"])

    def bias_chunk():
        arrived(groups["rows"])
        groups["rows"][0][1].wait_send()
        lanes[0:16, :] = row_buf[0] + row_buf[1]
        halves_t = [
            lanes[:, pl.ds(pl.multiple_of(high * 512 + core * 256, 128), 256)].T.reshape(32, 8, 128)
            for high in (0, 1)
        ]
        lane = lax.broadcasted_iota(jnp.int32, (32, 8, 128), 2)
        quarters = lanes[...].T.reshape(32, 4, 8, 128)
        for high in (0, 1):
            wide = jnp.where(lane < 12, halves_t[high], 0.0)
            for part in range(4):
                here = jnp.where(
                    core == 0,
                    quarters[:, part, :, 12 + 2 * high : 13 + 2 * high],
                    quarters[:, part, :, 13 + 2 * high : 14 + 2 * high],
                )
                wide = wide + jnp.where(lane == 12 + part, here, 0.0)
            halves_t[high] = wide
        turned = jnp.concatenate(halves_t, axis=0)
        put_f(0, jnp.concatenate([turned[b : b + 1] for b in BLOCKS], axis=0))

    out = pltpu.make_async_copy(pix_grad, pix_out, load_sem.at[14])

    def pixels_back():
        parts = [None] * 3
        for index in range(6):
            wide_load(12 + index).wait()
            for side in (0, 1):
                band, third = divmod(2 * index + side, 3)
                term = hot_buf[0:256, band : band + 1] * nt_dot(
                    gs[...], wide[(12 + index) % 3, 256 * side : 256 * side + 256, :]
                )
                parts[third] = term if parts[third] is None else parts[third] + term
            used(wide_load, 12 + index, 18)
        for third in range(3):
            pix_grad[:, 256 * third : 256 * third + 256] = parts[third].astype(jnp.bfloat16)
        out.start()

    def finish_bias(total):
        bias_out[...] = total

    actions = {
        HEADS: heads_back,
        FAR: pass_far,
        CLOSE: close,
        GP: lambda index: gp_copy(index).start(),
        PUT: compute,
        ADV: lambda chunk, step: advance(chunk, step, finisher(chunk)),
        THROUGH: through_qkv,
        NORM: norm_back,
        ROWS: side_rows,
        BIAS: bias_chunk,
        ADVB: lambda step: advance_f(0, step, finish_bias),
        PIX: pixels_back,
        POST: mlp_back,
        GATT: attention_grad,
    }
    for copy in loads[10:]:
        copy.wait()
    for name, *where_at in SCHEDULE:
        actions[name](*where_at)
    out.wait()
    for _, remote in made[:-1]:
        remote.wait_send()
    for pair in range(8):
        if pair >= 6:
            near_copy(pair).wait_send()
            far_copy(pair).wait_send()
    for index in range(6):
        gp_copy(index).wait_send()
    for tile in range(8):
        gpre_copy(tile).wait_send()
    for copy in (gout_copy(), gbr_copy(), hot_copy(), hid_copy(0), hid_copy(1)):
        copy.wait_send()
    for chunk in range(CHUNKS):
        drain(chunk)
    drain_f(0)


def backward(*operands):
    any_space = pl.BlockSpec(memory_space=pl.ANY)
    in_vmem = pl.BlockSpec(memory_space=pltpu.VMEM)
    half, full = jnp.bfloat16, jnp.float32
    shape = jax.ShapeDtypeStruct
    dma = pltpu.SemaphoreType.DMA
    return pl.pallas_call(
        backward_kernel,
        out_shape=(
            shape((256, 1024), half),
            shape((256, 768), half),
            shape((8, 3072), full),
            shape((8, 3072), full),
            shape((8, 1024), full),
            shape((8, 4096), full),
            shape((32, 1024), full),
            shape((8, 128), full),
        ),
        in_specs=[any_space] * 21,
        out_specs=(any_space,) * 2 + (in_vmem,) * 6,
        scratch_shapes=[
            pltpu.VMEM((3, 512, 512), half),
            pltpu.VMEM((2, 256, 2048), half),
            pltpu.VMEM((256, 2048), half),
            pltpu.VMEM((512, 1024), half),
            pltpu.VMEM((512, 4096), half),
            pltpu.VMEM((512, 1024), half),
            pltpu.VMEM((512, 3072), half),
            pltpu.VMEM((512, 768), half),
            pltpu.VMEM((512, 128), full),
            pltpu.VMEM((2, 16, 1024), full),
            pltpu.VMEM((128, 1024), full),
            pltpu.VMEM((8, 1024), full),
            pltpu.VMEM((512, 512), half),
            pltpu.VMEM((2048, 512), half),
            pltpu.VMEM((SLOTS, 64, 16, 256), half),
            pltpu.VMEM((SLOTS, 56, 16, 256), half),
            pltpu.VMEM((CHUNKS, 14, 16, 256), half),
            pltpu.VMEM((CHUNKS, 7, 16, 256), half),
            pltpu.VMEM((1, 64, 8, 128), full),
            pltpu.VMEM((1, 56, 8, 128), full),
            pltpu.VMEM((1, 14, 8, 128), full),
            pltpu.VMEM((1, 7, 8, 128), full),
            pltpu.VMEM((8, 256, 128), half),
            pltpu.VMEM((2, 2, 1024, 128), half),
            pltpu.VMEM((8, 256, 128), half),
            pltpu.VMEM((1024, 256), full),
            pltpu.VMEM((2, 2, 2, 256, 128), half),
            pltpu.VMEM((4, 2, 2, 256, 128), half),
            pltpu.VMEM((2, 2, 256, 128), half),
            pltpu.VMEM((8, 2, 256, 128), half),
            pltpu.VMEM((2, 2, 256, 128), full),
            pltpu.VMEM((2, 2, 256, 128), full),
            pltpu.VMEM((2, 1024, 128), full),
            pltpu.VMEM((256, 1024), half),
            pltpu.VMEM((256, 1024), full),
            pltpu.VMEM((256, 1024), full),
            pltpu.VMEM((256, 1024), full),
            pltpu.VMEM((256, 1024), full),
            pltpu.VMEM((256, 1024), half),
            pltpu.VMEM((256, 768), half),
            pltpu.VMEM((3, 1024, 512), half),
            pltpu.VMEM((3, 512, 1024), half),
            pltpu.VMEM((8, 2, 256), full),
            pltpu.VMEM((1024,), full),
            pltpu.VMEM((1024,), full),
            pltpu.VMEM((1024,), full),
            pltpu.VMEM((1024,), full),
            pltpu.VMEM((4096,), full),
            pltpu.VMEM((1024,), full),
            dma((10,)),
            dma((10,)),
            dma((10,)),
            dma((CHUNKS, 6)),
            dma((CHUNKS, 6)),
            pltpu.SemaphoreType.REGULAR((CHUNKS - SLOTS, 3)),
            dma((1, 6)),
            dma((1, 6)),
            dma((15,)),
            dma((2,)),
            dma((3,)),
            dma((3,)),
            dma((2, 8)),
            dma((2, 8)),
            pltpu.SemaphoreType.REGULAR((4,)),
            dma((6,)),
            dma((6,)),
            dma((8,)),
            dma((8,)),
            dma((5,)),
            dma((5,)),
        ],
        compiler_params=pltpu.CompilerParams(
            collective_id=2, has_side_effects=True, vmem_limit_bytes=VMEM_BYTES
        ),
        name="backward",
    )(*operands)


def finish_kernel(*refs):
    sources, dests, bufs = refs[:8], refs[8:25], refs[25:33]
    cols, bands, flat, in_sem, out_sem = refs[33:]
    loads = []
    for source, buf in zip(sources, bufs):
        loads.append(pltpu.make_async_copy(source, buf, in_sem.at[len(loads)]))
    for copy in reversed(loads):
        copy.start()
    stores = []

    def store(source, dest):
        stores.append(pltpu.make_async_copy(source, dest, out_sem.at[len(stores)]))
        stores[-1].start()

    loads[7].wait()
    sums = bufs[7][...]
    cols[...] = sums.T[0:16, :]
    for index in range(8):
        store(cols.at[pl.ds(4 + index, 1), :], dests[8 + index])
    bands[...] = cols[0:4, :]
    store(bands, dests[7])
    lane = lax.broadcasted_iota(jnp.int32, (8, 128), 1)
    wide = jnp.zeros((8, 128), jnp.float32)
    for part in range(4):
        wide = wide + jnp.where(lane // 8 == part, sums[:, 12 + part : 13 + part], 0.0)
    wide = jnp.where(lane % 8 == lax.broadcasted_iota(jnp.int32, (8, 128), 0), wide, 0.0)
    flat[...] = jnp.sum(wide, axis=0, keepdims=True)[:, 0:32]
    store(flat, dests[16])
    for index in range(7):
        loads[index].wait()
        if index < 6:
            store(bufs[index], dests[index])
    for band in range(4):
        store(bufs[6].at[:, pl.ds(768 * band, 768)], dests[6].at[band])
    for copy in stores:
        copy.wait()


def finish(*operands):
    any_space = pl.BlockSpec(memory_space=pl.ANY)
    full = jnp.float32
    shape = jax.ShapeDtypeStruct
    return pl.pallas_call(
        finish_kernel,
        out_shape=tuple(shape(array.shape, array.dtype) for array in operands[:6])
        + (shape((4, 8, 768), full), shape((4, 8), full))
        + (shape((1, 8), full),) * 8
        + (shape((1, 32), full),),
        in_specs=[any_space] * 8,
        out_specs=(any_space,) * 17,
        scratch_shapes=[pltpu.VMEM(array.shape, array.dtype) for array in operands]
        + [
            pltpu.VMEM((16, 8), full),
            pltpu.VMEM((4, 8), full),
            pltpu.VMEM((1, 32), full),
            pltpu.SemaphoreType.DMA((8,)),
            pltpu.SemaphoreType.DMA((20,)),
        ],
        compiler_params=pltpu.CompilerParams(vmem_limit_bytes=VMEM_BYTES),
        name="finish",
    )(*operands)


def on_device(
    pixels,
    positions,
    segments,
    groups,
    cotangent,
    emb_weight,
    emb_bias,
    norm1_gain,
    norm1_bias,
    qkv_weight,
    query_bias,
    value_bias,
    out_weight,
    out_bias,
    norm2_gain,
    norm2_bias,
    fc1_weight,
    fc1_bias,
    fc2_weight,
    fc2_bias,
):
    rows_dev, slice_len, pix_len = pixels.shape
    model_width = qkv_weight.shape[0]
    band_count = emb_weight.shape[0]
    tok_count = rows_dev * slice_len
    flat_pixels = pixels.reshape(tok_count, pix_len)
    flat_emb = emb_weight.reshape(band_count * pix_len, model_width)
    hot_live, mask, stream, normed_one, query_pairs, key_value, log_sums, attended = forward(
        flat_pixels,
        positions.reshape(tok_count, model_width),
        segments,
        groups,
        emb_bias,
        norm1_gain,
        norm1_bias,
        query_bias,
        value_bias,
        flat_emb,
        qkv_weight,
    )
    block_out, pixel_grad, emb_sum, qkv_sum, out_sum, fc1_sum, fc2_sum, bias_sum = backward(
        attended,
        stream,
        cotangent.reshape(tok_count, model_width),
        hot_live,
        mask,
        query_pairs,
        key_value,
        log_sums,
        normed_one,
        flat_pixels,
        norm1_gain,
        norm2_gain,
        norm2_bias,
        out_bias,
        fc1_bias,
        fc2_bias,
        flat_emb,
        qkv_weight,
        out_weight,
        fc1_weight,
        fc2_weight,
    )
    block_out, pixel_grad, qkv_sum, out_sum, fc1_sum, fc2_sum, emb_sum, *rest = finish(
        block_out, pixel_grad, qkv_sum, out_sum, fc1_sum, fc2_sum, emb_sum, bias_sum
    )
    emb_bias_sum, gain1, bias1, query, value, out, gain2, bias2, last, wide = (
        part if index == 0 else part.reshape(-1) for index, part in enumerate(rest)
    )
    return (
        block_out.reshape(rows_dev, slice_len, model_width),
        pixel_grad.reshape(rows_dev, slice_len, pix_len),
        jnp.swapaxes(emb_sum, 1, 2),
        emb_bias_sum,
        gain1,
        bias1,
        qkv_sum,
        query,
        value,
        out_sum,
        out,
        gain2,
        bias2,
        fc1_sum,
        wide,
        fc2_sum,
        last,
    )


def solution(mesh):
    return jax.shard_map(
        on_device,
        mesh=mesh,
        in_specs=(
            P("batch", "blk", None),
            P("batch", "blk", None),
            P("batch", None),
            P("batch", "blk"),
            P("batch", "blk", None),
            P(),
            P(),
            P(),
            P(),
            P(),
            P(),
            P(),
            P(),
            P(),
            P(),
            P(),
            P(),
            P(),
            P(),
            P(),
        ),
        out_specs=(
            P("batch", "blk", None),
            P("batch", "blk", None),
            P(None, None, ("blk", "batch")),
            P(None, ("blk", "batch")),
            P(("blk", "batch")),
            P(("blk", "batch")),
            P(("blk", "batch"), None),
            P(("blk", "batch")),
            P(("blk", "batch")),
            P(("blk", "batch"), None),
            P(("blk", "batch")),
            P(("blk", "batch")),
            P(("blk", "batch")),
            P(("blk", "batch"), None),
            P(("blk", "batch")),
            P(("blk", "batch"), None),
            P(("blk", "batch")),
        ),
        check_vma=False,
    )
```

```python
import jax
import jax.numpy as jnp
from jax import lax
from jax.experimental import pallas as pl
from jax.experimental.pallas import tpu as pltpu
from jax.sharding import PartitionSpec as P

HD = 64
NORM_EPS = 1e-06
MASKED = -1e30
VMEM_BYTES = 64 << 20

MESH = pl.DeviceIdType.MESH
AXES = ("xb", "xa", "yb", "ya", "zb", "za")
ROTATION = ("xa", "ya", "za", "xb", "yb", "zb")
GRAY = (0, 1, 3, 2)
BLOCKS = tuple(16 * x + 4 * y + z for x in GRAY for y in GRAY for z in GRAY)


def place():
    blk = lax.axis_index("blk")
    batch = lax.axis_index("batch")
    return blk // 2, blk % 2, batch // 16, (batch // 4) % 4, batch % 4


def neighbours(where):
    x_hi, core, x_lo, y, z = where

    def device(x_hi, core, x_lo, y, z):
        return (x_hi * 2 + core, x_lo * 16 + y * 4 + z)

    return {
        "core": device(x_hi, 1 - core, x_lo, y, z),
        "xa": device(x_hi, core, 1 - x_lo, y, z),
        "xb": device(1 - x_hi, core, 1 - x_lo, y, z),
        "ya": device(x_hi, core, x_lo, y + 1 - 2 * (y % 2), z),
        "yb": device(x_hi, core, x_lo, 3 - y, z),
        "za": device(x_hi, core, x_lo, y, z + 1 - 2 * (z % 2)),
        "zb": device(x_hi, core, x_lo, y, 3 - z),
    }


def own_bits(where):
    x_hi, _, x_lo, y, z = where
    return {
        "xb": x_hi,
        "xa": (x_hi + x_lo) % 2,
        "yb": y // 2,
        "ya": (y // 2 + y) % 2,
        "zb": z // 2,
        "za": (z // 2 + z) % 2,
    }


DIMS = (
    (1, 2, 4, 5, 0, 3),
    (2, 4, 5, 1, 3, 0),
    (4, 5, 1, 2, 3, 0),
    (5, 1, 2, 4, 0, 3),
    (0, 5, 1, 3, 2, 4),
    (2, 4, 5, 1, 0, 3),
    (4, 5, 1, 2, 0, 3),
    (1, 2, 3, 4, 5, 0),
    (2, 4, 5, 1, 0, 3),
    (1, 2, 4, 5, 3, 0),
    (3, 4, 5, 0, 1, 2),
    (1, 2, 4, 5, 0, 3),
    (5, 1, 2, 4, 0, 3),
    (3, 2, 4, 0, 5, 1),
    (5, 1, 2, 4, 0, 3),
    (2, 0, 4, 5, 1, 3),
    (3, 1, 2, 0, 4, 5),
    (4, 0, 5, 1, 2, 3),
    (1, 2, 3, 4, 5, 0),
    (4, 5, 0, 1, 2, 3),
    (5, 3, 1, 2, 4, 0),
    (4, 3, 5, 1, 2, 0),
    (5, 0, 1, 2, 3, 4),
    (2, 3, 4, 5, 0, 1),
    (2, 4, 5, 1, 3, 0),
    (0, 1, 2, 3, 4, 5),
    (5, 0, 1, 2, 4, 3),
    (4, 5, 0, 1, 2, 3),
    (1, 2, 3, 4, 5, 0),
    (3, 1, 2, 0, 4, 5),
)


def chunk_dims(chunk):
    return tuple(ROTATION[axis] for axis in DIMS[chunk])


def split_shape(dims, step):
    left = [axis for axis in AXES if axis not in dims[:step]]
    at = left.index(dims[step])
    return 2**at, 2 ** (len(left) - 1 - at)


KEEP_AT = (0, 32, 0, 0, 8, 12)
SEND_AT = (32, 48, 8, 4, 10, 13)
ARRIVE_AT = (0, 32, 48, 0, 4, 6)
SLOTS = 18


def reducer(near, bits, dims_of, buffers, send_sem, recv_sem, credit, chunks):
    work, arrive, work_end, arrive_end = buffers

    def held(chunk, step):
        return work.at[chunk % SLOTS] if step < 3 else work_end.at[chunk]

    def come(chunk, step):
        return arrive.at[chunk % SLOTS] if step < 3 else arrive_end.at[chunk]

    def hop(chunk, step):
        half = 32 >> step
        return pltpu.make_async_remote_copy(
            src_ref=held(chunk, step).at[pl.ds(SEND_AT[step], half)],
            dst_ref=come(chunk, step).at[pl.ds(ARRIVE_AT[step], half)],
            send_sem=send_sem.at[chunk, step],
            recv_sem=recv_sem.at[chunk, step],
            device_id=near[dims_of(chunk)[step]],
            device_id_type=MESH,
        )

    def send(chunk, step):
        if step < 3 and chunk >= SLOTS:
            pl.semaphore_wait(credit.at[chunk - SLOTS, step], 1)
        hop(chunk, step).start()

    def put(chunk, result):
        if chunk >= SLOTS:
            for step in (1, 2):
                hop(chunk - SLOTS, step).wait_send()
        dims = dims_of(chunk)
        before, after = split_shape(dims, 0)
        own = bits[dims[0]]
        for a in range(before):
            for bit in (0, 1):
                other = own if bit == 0 else 1 - own
                piece = result[(2 * a + bit) * after : (2 * a + bit + 1) * after]
                held(chunk, 0)[pl.ds(other * 32 + a * after, after)] = piece
        send(chunk, 0)

    def advance(chunk, step, finish):
        hop(chunk, step).wait_recv()
        keep, come_at = KEEP_AT[step], ARRIVE_AT[step]
        here, there = held(chunk, step), come(chunk, step)
        if step == 5:
            finish(here[keep].astype(jnp.float32) + there[come_at].astype(jnp.float32))
            return
        if step == 0:
            hop(chunk, 0).wait_send()
        dims = dims_of(chunk)
        before, after = split_shape(dims, step + 1)
        own = bits[dims[step + 1]]
        target = held(chunk, step + 1)
        for bit, base in ((1 - own, SEND_AT[step + 1]), (own, KEEP_AT[step + 1])):

            def merge(a, carry, bit=bit, base=base):
                at = (2 * a + bit) * after
                target[pl.ds(base + a * after, after)] = (
                    here[pl.ds(keep + at, after)] + there[pl.ds(come_at + at, after)]
                )
                return carry

            lax.fori_loop(0, before, merge, 0, unroll=min(before, 8))
            if base == SEND_AT[step + 1]:
                send(chunk, step + 1)
        if step < 3 and chunk + SLOTS < chunks:
            pl.semaphore_signal(
                credit.at[chunk, step],
                inc=1,
                device_id=near[dims_of(chunk + SLOTS)[step]],
                device_id_type=MESH,
            )

    def drain(chunk):
        for step in range(1 if chunk + SLOTS >= chunks else 3, 6):
            hop(chunk, step).wait_send()

    return put, advance, drain


def nt_dot(left, right):
    return lax.dot_general(left, right, (((1,), (1,)), ((), ())), preferred_element_type=jnp.float32)


def tn_dot(left, right):
    return lax.dot_general(left, right, (((0,), (0,)), ((), ())), preferred_element_type=jnp.float32)


def norm_parts(values):
    center = values - jnp.mean(values, axis=-1, keepdims=True)
    spread = jnp.mean(center * center, axis=-1, keepdims=True)
    scale = lax.rsqrt(spread + NORM_EPS)
    return center * scale, scale


def row(vector):
    return vector[...].reshape(1, 1024)


def forward_kernel(
    pix_in, pos_in, seg_in, band_in, emb_bias_in, gain1_in, bias1_in, query_bias_in, value_bias_in, emb_in, qkv_in,
    hot_out, mask_out, stream_out, n1_out, q_out, kv_out, lse_out, att_out,
    pix, pos, hot, mask, emb_w, qkv_w, stream, flat, n1, q_pairs, kv, att,
    far_n1, run_max, run_sum, run_out, *small,
):
    (
        seg, band_of, emb_bias, gain1, bias1, query_bias, value_bias,
        load_sem, save_sem, pair_sem, send_sem, recv_sem,
    ) = small
    where = place()
    x_hi, core, x_lo, y, z = where
    partner = (x_hi * 2 + 1 - core, x_lo * 16 + y * 4 + z)
    across = ((1 - x_hi) * 2 + core, x_lo * 16 + y * 4 + z)
    barrier = pltpu.get_barrier_semaphore()
    for target in (partner, across):
        pl.semaphore_signal(barrier, inc=1, device_id=target, device_id_type=MESH)

    loads = {}

    def load(name, source, dest):
        copy = pltpu.make_async_copy(source, dest, load_sem.at[len(loads)])
        copy.start()
        loads[name] = copy

    saves = []

    def save(source, dest):
        copy = pltpu.make_async_copy(source, dest, save_sem.at[len(saves)])
        copy.start()
        saves.append(copy)

    load("seg", seg_in, seg)
    load("band", band_in, band_of)
    load("pix", pix_in, pix)
    load("eb", emb_bias_in, emb_bias)
    load("g1", gain1_in, gain1)
    load("b1", bias1_in, bias1)
    load("qb", query_bias_in, query_bias)
    load("vb", value_bias_in, value_bias)
    for band in range(4):
        span = pl.ds(768 * band, 768)
        load("emb%d" % band, emb_in.at[span, :], emb_w.at[span, :])
    load("pos", pos_in, pos)
    for part in (1, 2, 0):
        span = pl.ds(1024 * part, 1024)
        load("qkv%d" % part, qkv_in.at[:, span], qkv_w.at[:, span])
    loads["seg"].wait()
    loads["band"].wait()
    own_seg = seg[:, pl.ds(pl.multiple_of((x_hi * 2 + core) * 256, 256), 256)]
    at = lax.broadcasted_iota(jnp.int32, (128, 256), 0)
    hot[...] = (
        jnp.where(at == band_of[...], 1.0, 0.0)
        + jnp.where(at == 4, 1.0, 0.0) * jnp.where(own_seg >= 0, 1.0, 0.0)
    ).T
    save(hot, hot_out)

    for name in ("eb", "g1", "b1", "qb", "vb"):
        loads[name].wait()
    flat[0:1, :] = row(query_bias)
    flat[1:2, :] = row(value_bias)

    loads["pix"].wait()
    total = None
    for band in range(4):
        chosen = hot[:, band : band + 1]
        picked = (pix[...].astype(jnp.float32) * chosen).astype(jnp.bfloat16)
        loads["emb%d" % band].wait()
        term = jnp.dot(
            picked, emb_w[768 * band : 768 * band + 768, :], preferred_element_type=jnp.float32
        ) + chosen * emb_bias[band : band + 1, :]
        total = term if total is None else total + term
    loads["pos"].wait()
    stream[...] = total + pos[...].astype(jnp.float32)
    save(stream, stream_out)
    hat, _ = norm_parts(stream[...])
    n1[...] = (hat * row(gain1) + row(bias1)).astype(jnp.bfloat16)

    own_rows = pl.ds(pl.multiple_of((x_hi * 2 + core) * 256, 256), 256)

    def far_rows(low, piece):
        return pl.ds(pl.multiple_of(((1 - x_hi) * 2 + low) * 256 + 128 * piece, 128), 128)

    def push(source, dest, which, index, target):
        return pltpu.make_async_remote_copy(
            src_ref=source,
            dst_ref=dest,
            send_sem=send_sem.at[which, index],
            recv_sem=recv_sem.at[which, index],
            device_id=target,
            device_id_type=MESH,
        )

    def norm_copy(piece):
        span = pl.ds(128 * piece, 128)
        return push(n1.at[span, :], far_n1.at[span, :], 0, piece, across)

    def to_partner(pair):
        piece = kv.at[pair, :, own_rows, :]
        return push(piece, piece, 1, pair, partner)

    def far_copy(piece):
        part = kv.at[:, :, far_rows(core, piece), :]
        return push(part, part, 2, piece, partner)

    pl.semaphore_wait(barrier, 2)
    for piece in (0, 1):
        norm_copy(piece).start()
    save(n1, n1_out)
    loads["qkv1"].wait()
    loads["qkv2"].wait()

    def keys_values(source, tile, target):
        span = pl.ds(pl.multiple_of(1024 + 256 * tile, 256), 256)
        keys = jnp.dot(source, qkv_w[:, span], preferred_element_type=jnp.float32).astype(
            jnp.bfloat16
        )
        span = pl.ds(pl.multiple_of(2048 + 256 * tile, 256), 256)
        shift = flat[1:2, pl.ds(pl.multiple_of(256 * tile, 256), 256)]
        values = (
            jnp.dot(source, qkv_w[:, span], preferred_element_type=jnp.float32) + shift
        ).astype(jnp.bfloat16)
        for side in (0, 1):
            kv[2 * tile + side, 0, target, :] = keys[:, 128 * side : 128 * side + 128]
            kv[2 * tile + side, 1, target, :] = values[:, 128 * side : 128 * side + 128]

    def project(tile, carry):
        keys_values(n1[...], tile, own_rows)
        for side in (0, 1):
            to_partner(2 * tile + side).start()
        return carry

    lax.fori_loop(0, 4, project, 0)
    loads["qkv0"].wait()

    def project_query(tile, carry):
        span = pl.ds(pl.multiple_of(256 * tile, 256), 256)
        query = (
            jnp.dot(n1[...], qkv_w[:, span], preferred_element_type=jnp.float32)
            + flat[0:1, span]
        ).astype(jnp.bfloat16)
        query = (query.astype(jnp.float32) * HD ** (-0.5)).astype(jnp.bfloat16)
        for side in (0, 1):
            q_pairs[2 * tile + side] = query[:, 128 * side : 128 * side + 128]
        return carry

    lax.fori_loop(0, 4, project_query, 0)
    save(q_pairs, q_out)
    key_seg = jnp.broadcast_to(seg[...].astype(jnp.float32), (128, 1024)).T[:, 0:1]
    mask[...] = jnp.where(key_seg == own_seg.astype(jnp.float32), 0.0, MASKED)
    save(mask, mask_out)

    def project_far(piece):
        norm_copy(piece).wait_recv()

        def step(tile, carry):
            keys_values(far_n1[128 * piece : 128 * piece + 128, :], tile, far_rows(core, piece))
            return carry

        lax.fori_loop(0, 4, step, 0)
        far_copy(piece).start()

    def attend(span, first=False, last=False):
        def body(pair, carry):
            if first:
                to_partner(pair).wait_recv()
            if last:
                pltpu.make_async_copy(kv.at[pair], kv_out.at[pair], pair_sem.at[pair]).start()
            keys = kv[pair, 0, span, :]
            value_rows = kv[pair, 1, span, :].T
            bias = mask[span, :]
            turned = q_pairs[pair].astype(jnp.float32).T
            at = lax.broadcasted_iota(jnp.int32, (128, 256), 0)
            heads = []
            for head in (0, 1):
                own = (at < 64) if head == 0 else (at >= 64)
                mine = jnp.where(own, turned, 0.0).astype(jnp.bfloat16)
                scores = jnp.dot(keys, mine, preferred_element_type=jnp.float32) + bias
                peak = jnp.max(scores, axis=0, keepdims=True)
                if not first:
                    before = run_max[pair, head : head + 1, :]
                    peak = jnp.maximum(peak, before)
                    fade = jnp.exp(before - peak)
                expo = jnp.exp(scores - peak)
                norm = jnp.sum(expo, axis=0, keepdims=True)
                out = jnp.dot(
                    value_rows[64 * head : 64 * head + 64],
                    expo.astype(jnp.bfloat16),
                    preferred_element_type=jnp.float32,
                )
                if not first:
                    norm = norm + fade * run_sum[pair, head : head + 1, :]
                    out = out + fade * run_out[pair, 64 * head : 64 * head + 64, :]
                if last:
                    heads.append(out / norm)
                    lse_out[pair, head : head + 1, :] = peak + jnp.log(norm)
                else:
                    run_max[pair, head : head + 1, :] = peak
                    run_sum[pair, head : head + 1, :] = norm
                    run_out[pair, 64 * head : 64 * head + 64, :] = out
            if last:
                att[:, pl.ds(pl.multiple_of(pair * 128, 128), 128)] = jnp.concatenate(
                    heads, axis=0
                ).T.astype(jnp.bfloat16)
            return carry

        lax.fori_loop(0, 8, body, 0, unroll=2)

    attend(pl.ds(pl.multiple_of(x_hi * 512, 512), 512), first=True)
    for piece in (0, 1):
        project_far(piece)
    for piece in (0, 1):
        far_copy(piece).wait_recv()
    attend(pl.ds(pl.multiple_of((1 - x_hi) * 512, 512), 512), last=True)
    save(att, att_out)
    for copy in saves:
        copy.wait()

    def drain(pair, carry):
        to_partner(pair).wait_send()
        pltpu.make_async_copy(kv.at[pair], kv_out.at[pair], pair_sem.at[pair]).wait()
        return carry

    lax.fori_loop(0, 8, drain, 0)
    for piece in (0, 1):
        norm_copy(piece).wait_send()
        far_copy(piece).wait_send()


def forward(*operands):
    any_space = pl.BlockSpec(memory_space=pl.ANY)
    in_vmem = pl.BlockSpec(memory_space=pltpu.VMEM)
    half, full = jnp.bfloat16, jnp.float32
    shape = jax.ShapeDtypeStruct
    return pl.pallas_call(
        forward_kernel,
        out_shape=(
            shape((256, 128), full),
            shape((1024, 256), full),
            shape((256, 1024), full),
            shape((256, 1024), half),
            shape((8, 256, 128), half),
            shape((8, 2, 1024, 128), half),
            shape((8, 2, 256), full),
            shape((256, 1024), half),
        ),
        in_specs=[any_space] * 11,
        out_specs=(any_space,) * 6 + (in_vmem, any_space),
        scratch_shapes=[
            pltpu.VMEM((256, 768), half),
            pltpu.VMEM((256, 1024), half),
            pltpu.VMEM((256, 128), full),
            pltpu.VMEM((1024, 256), full),
            pltpu.VMEM((3072, 1024), half),
            pltpu.VMEM((1024, 3072), half),
            pltpu.VMEM((256, 1024), full),
            pltpu.VMEM((8, 1024), full),
            pltpu.VMEM((256, 1024), half),
            pltpu.VMEM((8, 256, 128), half),
            pltpu.VMEM((8, 2, 1024, 128), half),
            pltpu.VMEM((256, 1024), half),
            pltpu.VMEM((256, 1024), half),
            pltpu.VMEM((8, 2, 256), full),
            pltpu.VMEM((8, 2, 256), full),
            pltpu.VMEM((8, 128, 256), full),
            pltpu.VMEM((1, 1024), jnp.int32),
            pltpu.VMEM((1, 256), jnp.int32),
            pltpu.VMEM((4, 1024), full),
            pltpu.VMEM((1024,), full),
            pltpu.VMEM((1024,), full),
            pltpu.VMEM((1024,), full),
            pltpu.VMEM((1024,), full),
            pltpu.SemaphoreType.DMA((20,)),
            pltpu.SemaphoreType.DMA((8,)),
            pltpu.SemaphoreType.DMA((8,)),
            pltpu.SemaphoreType.DMA((3, 8)),
            pltpu.SemaphoreType.DMA((3, 8)),
        ],
        compiler_params=pltpu.CompilerParams(
            collective_id=1, has_side_effects=True, vmem_limit_bytes=VMEM_BYTES
        ),
        name="forward",
    )(*operands)


def exchanger(core, partner, ex_send, ex_recv, ex_local):
    made = []

    def exchange(source, dest, cut=None):
        index = len(made)

        def part(owner):
            if cut is None:
                return source
            at, span = cut
            return source.at[:, pl.ds(pl.multiple_of(at + owner * span, 128), span)]

        made.append(
            (
                pltpu.make_async_copy(part(core), dest(0), ex_local.at[index]),
                pltpu.make_async_remote_copy(
                    src_ref=part(1 - core),
                    dst_ref=dest(1),
                    send_sem=ex_send.at[index],
                    recv_sem=ex_recv.at[index],
                    device_id=partner,
                    device_id_type=MESH,
                ),
            )
        )
        return made[-1]

    def whole(source, buf):
        return [exchange(source, lambda half: buf.at[pl.ds(256 * half, 256), :])]

    def halves(source, buf, span):
        return [
            exchange(
                source,
                lambda half, high=high: buf.at[pl.ds(256 * half, 256), pl.ds(high * span, span)],
                (high * 2 * span, span),
            )
            for high in (0, 1)
        ]

    return exchange, whole, halves, made


def begin(copies):
    for local, remote in copies:
        remote.start()
        local.start()


def arrived(copies):
    for local, remote in copies:
        local.wait()
        remote.wait_recv()


def greet(targets):
    barrier = pltpu.get_barrier_semaphore()
    for target in targets:
        pl.semaphore_signal(barrier, inc=1, device_id=target, device_id_type=MESH)
    pl.semaphore_wait(barrier, len(targets))


def turn_rows(buf, dest):
    turned = buf[...].astype(jnp.float32).T
    dest[...] = jnp.concatenate(
        [turned[8 * block : 8 * block + 8] for block in BLOCKS], axis=0
    ).astype(jnp.bfloat16)


def chunk_product(left, right_a, right_b):
    a = jnp.dot(left, right_a, preferred_element_type=jnp.float32)
    b = jnp.dot(left, right_b, preferred_element_type=jnp.float32)
    return jnp.concatenate((a.reshape(64, 8, 256), b.reshape(64, 8, 256)), axis=1).astype(
        jnp.bfloat16
    )


def wide_finish(dest, tile):
    def finish(total):
        dest[:, 512 * tile : 512 * tile + 256] = total[:8]
        dest[:, 512 * tile + 256 : 512 * tile + 512] = total[8:]

    return finish


HEADS, FAR, CLOSE, GP, PUT, ADV, THROUGH, NORM, ROWS, BIAS, ADVB, PIX, POST, GATT, MLP = range(15)
SCHEDULE = (
    (MLP, 0), (MLP, 1), (MLP, 2), (PUT, 8), (PUT, 9), (MLP, 3), (PUT, 10), (MLP, 4), (MLP, 5), (PUT, 11),
    (MLP, 6), (PUT, 12), (PUT, 13), (MLP, 7), (ADV, 8, 0), (ADV, 9, 0), (PUT, 14), (POST,), (ADV, 10, 0),
    (PUT, 4), (PUT, 0), (PUT, 2), (GATT,), (ADV, 9, 1), (ADV, 11, 0), (ADV, 8, 1), (HEADS, 0), (ADV, 12, 0),
    (ADV, 10, 1), (ADV, 13, 0), (HEADS, 1), (FAR, 0), (PUT, 6), (ADV, 4, 0), (HEADS, 2), (FAR, 1),
    (ADV, 14, 0), (ADV, 5, 0), (ADV, 0, 0), (ADV, 2, 0), (HEADS, 3), (FAR, 2), (CLOSE, 0), (GP, 0),
    (ADV, 12, 1), (ADV, 9, 2), (HEADS, 4), (FAR, 3), (CLOSE, 1), (ADV, 3, 0), (ADV, 1, 0), (HEADS, 5),
    (FAR, 4), (ADV, 8, 2), (ADV, 11, 1), (ADV, 10, 2), (ADV, 6, 0), (ADV, 7, 0), (HEADS, 6), (FAR, 5),
    (CLOSE, 2), (ADV, 4, 1), (ADV, 13, 1), (ADV, 14, 1), (HEADS, 7), (FAR, 6), (CLOSE, 3), (GP, 1), (GP, 2),
    (GP, 3), (ADV, 0, 1), (ADV, 5, 1), (ADV, 3, 1), (THROUGH, 0), (ADV, 2, 1), (ADV, 1, 1), (ADV, 8, 3),
    (PUT, 15), (CLOSE, 4), (ADV, 12, 2), (ADV, 9, 3), (PUT, 17), (FAR, 7), (ADV, 10, 3), (ADV, 11, 2),
    (ADV, 4, 2), (THROUGH, 1), (THROUGH, 2), (THROUGH, 3), (ADV, 13, 2), (ADV, 6, 1), (PUT, 16),
    (ADV, 2, 2), (ADV, 7, 1), (CLOSE, 5), (ADV, 10, 4), (ADV, 0, 2), (ADV, 5, 2), (ADV, 14, 2),
    (ADV, 12, 3), (PUT, 20), (ADV, 1, 2), (ADV, 3, 2), (ADV, 9, 4), (PUT, 18), (CLOSE, 6), (ADV, 11, 3),
    (ADV, 6, 2), (ADV, 8, 4), (ADV, 5, 3), (ADV, 0, 3), (PUT, 19), (PUT, 21), (ADV, 1, 3), (CLOSE, 7),
    (GP, 4), (GP, 5), (ADV, 4, 3), (THROUGH, 4), (ADV, 17, 0), (ADV, 13, 3), (THROUGH, 5), (ADV, 12, 4),
    (ADV, 14, 3), (ADV, 9, 5), (NORM,), (ROWS,), (ADV, 15, 0), (ADV, 2, 3), (ADV, 11, 4), (ADV, 5, 4),
    (ADV, 0, 4), (ADV, 3, 3), (PUT, 22), (PUT, 23), (ADV, 6, 3), (ADV, 10, 5), (PIX,), (BIAS,),
    (ADV, 16, 0), (ADV, 20, 0), (ADV, 13, 4), (ADV, 17, 1), (ADV, 18, 0), (ADV, 14, 4), (ADV, 4, 4),
    (PUT, 28), (PUT, 29), (ADV, 7, 2), (PUT, 26), (PUT, 24), (ADV, 1, 4), (ADV, 19, 0), (PUT, 27),
    (ADV, 2, 4), (ADV, 8, 5), (ADV, 12, 5), (ADV, 11, 5), (ADV, 5, 5), (ADV, 0, 5), (ADV, 15, 1), (PUT, 25),
    (ADV, 3, 4), (ADV, 6, 4), (ADV, 16, 1), (ADV, 13, 5), (ADV, 22, 0), (ADV, 23, 0), (ADV, 20, 1),
    (ADV, 14, 5), (ADVB, 0), (ADV, 17, 2), (ADV, 1, 5), (ADV, 2, 5), (ADV, 21, 0), (ADV, 4, 5),
    (ADV, 18, 1), (ADV, 7, 3), (ADV, 28, 0), (ADV, 29, 0), (ADV, 3, 5), (ADV, 6, 5), (ADV, 20, 2),
    (ADV, 26, 0), (ADV, 25, 0), (ADVB, 1), (ADV, 24, 0), (ADV, 27, 0), (ADV, 17, 3), (ADV, 23, 1),
    (ADV, 19, 1), (ADV, 22, 1), (ADV, 16, 2), (ADV, 7, 4), (ADV, 15, 2), (ADV, 29, 1), (ADV, 21, 1),
    (ADV, 26, 1), (ADV, 28, 1), (ADV, 24, 1), (ADV, 20, 3), (ADV, 18, 2), (ADV, 27, 1), (ADV, 19, 2),
    (ADVB, 2), (ADV, 15, 3), (ADV, 25, 1), (ADV, 17, 4), (ADV, 23, 2), (ADV, 16, 3), (ADV, 7, 5),
    (ADV, 21, 2), (ADV, 20, 4), (ADV, 22, 2), (ADV, 29, 2), (ADV, 28, 2), (ADV, 18, 3), (ADVB, 3),
    (ADV, 17, 5), (ADV, 27, 2), (ADV, 24, 2), (ADV, 16, 4), (ADV, 26, 2), (ADV, 23, 3), (ADV, 25, 2),
    (ADV, 19, 3), (ADV, 20, 5), (ADV, 15, 4), (ADV, 22, 3), (ADV, 29, 3), (ADV, 18, 4), (ADV, 28, 3),
    (ADV, 21, 3), (ADVB, 4), (ADV, 16, 5), (ADV, 27, 3), (ADV, 26, 3), (ADV, 23, 4), (ADV, 19, 4),
    (ADV, 24, 3), (ADV, 25, 3), (ADV, 15, 5), (ADV, 29, 4), (ADV, 22, 4), (ADV, 18, 5), (ADV, 28, 4),
    (ADV, 21, 4), (ADVB, 5), (ADV, 27, 4), (ADV, 23, 5), (ADV, 26, 4), (ADV, 19, 5), (ADV, 24, 4),
    (ADV, 25, 4), (ADV, 29, 5), (ADV, 22, 5), (ADV, 28, 5), (ADV, 21, 5), (ADV, 27, 5), (ADV, 26, 5),
    (ADV, 24, 5), (ADV, 25, 5),
)


CHUNKS = 30


def backward_kernel(
    att_in, stream_in, cot_in, hot_in, mask_in, q_in, kv_in, lse_in, n1_in, pix_in,
    gain1_in, gain2_in, bias2_in, out_bias_in, fc1_bias_in, fc2_bias_in, emb_in, qkv_in, ow_in, fc1_in, fc2_in,
    block_out, pix_out, emb_out, qkv_out, out_out, fc1_out, fc2_out, bias_out,
    x_buf, hid, hid_come, gbr_buf, gpre_buf, gout_buf, gp_buf, pix_buf, hot_buf, row_buf, lanes, sums,
    xt_buf, xht_buf, work, arrive, work_end, arrive_end, work_f, arrive_f, work_end_f, arrive_end_f,
    q_pairs, kv, gatt, mask, near_send, near_come, far_send, far_come, held, far_held, whole_grad,
    n2, stream, middle, acc, grown_buf, gs, pix_grad, tall, wide,
    lse, gain1, gain2, bias2, out_bias, fc1_bias, fc2_bias,
    ex_send, ex_recv, ex_local, send_sem, recv_sem, credit, send_f, recv_f, load_sem, kv_sem, tall_sem, wide_sem,
    kv_send_sem, kv_recv_sem, kv_credit, gp_send, gp_recv, pre_send, pre_recv, tok_send, tok_recv,
):
    where = place()
    x_hi, core, x_lo, y, z = where
    near = neighbours(where)
    bits = own_bits(where)
    partner = near["core"]
    across = ((1 - x_hi) * 2 + core, x_lo * 16 + y * 4 + z)

    def kv_load(pair):
        return pltpu.make_async_copy(kv_in.at[pair], kv.at[pair % 2], kv_sem.at[pair % 2])

    order = (0, 1, 2, 4, 3, 5)

    def tall_load(index):
        if index < 8:
            source = fc1_in.at[:, pl.ds(512 * index, 512)]
        else:
            source = qkv_in.at[:, pl.ds(512 * order[index - 8], 512)]
        return pltpu.make_async_copy(source, tall.at[index % 3], tall_sem.at[index % 3])

    def wide_load(index):
        if index < 2 or index in (10, 11):
            source = ow_in.at[pl.ds(512 * (index % 2), 512), :]
        elif index < 10:
            source = fc2_in.at[pl.ds(512 * (index - 2), 512), :]
        else:
            source = emb_in.at[pl.ds(512 * (index - 12), 512), :]
        return pltpu.make_async_copy(source, wide.at[index % 3], wide_sem.at[index % 3])

    def used(load, index, last):
        if index + 3 < last:
            load(index + 3).start()

    loads = []
    for source, dest in (
        (att_in, n2), (stream_in, stream), (hot_in, hot_buf.at[pl.ds(0, 256), :]), (cot_in, gs),
        (gain1_in, gain1), (gain2_in, gain2), (bias2_in, bias2), (out_bias_in, out_bias),
        (fc1_bias_in, fc1_bias), (fc2_bias_in, fc2_bias), (lse_in, lse), (q_in, q_pairs), (mask_in, mask),
    ):
        loads.append(pltpu.make_async_copy(source, dest, load_sem.at[len(loads)]))
    loads[0].start()
    for index in range(2):
        wide_load(index).start()
    for copy in loads[1:10]:
        copy.start()
    wide_load(2).start()
    for index in range(3):
        tall_load(index).start()
    for copy in loads[10:]:
        copy.start()
    for pair in range(2):
        kv_load(pair).start()
    greet(tuple(near.values()) + (across,))

    put, advance, drain = reducer(
        near, bits, chunk_dims, (work, arrive, work_end, arrive_end), send_sem, recv_sem, credit, CHUNKS
    )
    put_f, advance_f, drain_f = reducer(
        near, bits, lambda chunk: ROTATION, (work_f, arrive_f, work_end_f, arrive_end_f),
        send_f, recv_f, None, 1,
    )
    exchange, whole, halves, made = exchanger(core, partner, ex_send, ex_recv, ex_local)
    groups = {
        "fc1": halves(n2, x_buf.at[0], 256),
        "out": halves(att_in, x_buf.at[1], 256),
        "qkv": halves(n1_in, x_buf.at[2], 256),
        "side": whole(pix_in, pix_buf),
        "emb": halves(gs, x_buf.at[0], 256),
        "rows": [exchange(lanes.at[pl.ds(0, 16), :], lambda half: row_buf.at[half])],
    }
    begin(groups["out"])
    begin(groups["qkv"])
    begin(groups["side"])

    def mirror(buf, index, span=slice(None)):
        return pltpu.make_async_remote_copy(
            src_ref=buf.at[pl.ds(0, 256), span],
            dst_ref=buf.at[pl.ds(256, 256), span],
            send_sem=tok_send.at[index],
            recv_sem=tok_recv.at[index],
            device_id=partner,
            device_id_type=MESH,
        )

    def gout_copy():
        return mirror(gout_buf, 0)

    def gbr_copy():
        return mirror(gbr_buf, 1)

    def hot_copy():
        return mirror(hot_buf, 2)

    def hid_copy(high):
        return pltpu.make_async_remote_copy(
            src_ref=hid.at[1 - core, :, pl.ds(1024 * high, 1024)],
            dst_ref=hid_come.at[:, pl.ds(1024 * high, 1024)],
            send_sem=tok_send.at[3 + high],
            recv_sem=tok_recv.at[3 + high],
            device_id=partner,
            device_id_type=MESH,
        )

    def gpre_copy(tile):
        span = pl.ds(512 * tile, 512)
        return pltpu.make_async_remote_copy(
            src_ref=gpre_buf.at[pl.ds(0, 256), span],
            dst_ref=gpre_buf.at[pl.ds(256, 256), span],
            send_sem=pre_send.at[tile],
            recv_sem=pre_recv.at[tile],
            device_id=partner,
            device_id_type=MESH,
        )

    def gp_copy(index):
        span = pl.ds(512 * order[index], 512)
        return pltpu.make_async_remote_copy(
            src_ref=gp_buf.at[pl.ds(0, 256), span],
            dst_ref=gp_buf.at[pl.ds(256, 256), span],
            send_sem=gp_send.at[index],
            recv_sem=gp_recv.at[index],
            device_id=partner,
            device_id_type=MESH,
        )

    plan = [("fc2", tile) for tile in range(8)] + [("fc1", tile) for tile in range(8)]
    plan += [("out", tile) for tile in range(2)] + [("qkv", index) for index in range(6)]
    plan += [("emb", tile) for tile in range(6)]
    turned_from = {"fc1": 0, "out": 1, "qkv": 2, "emb": 0}
    ready = set()

    def band_pixels(tile):
        band, at = tile // 3, tile % 3
        picked = pix_buf[:, 256 * at : 256 * at + 256].astype(jnp.float32)
        return (picked * hot_buf[:, band : band + 1]).astype(jnp.bfloat16)

    def turn_wide(buf, at):
        turned = buf[...].astype(jnp.float32).T.astype(jnp.bfloat16)
        xht_buf[:, at : at + 256] = jnp.concatenate(
            [turned[32 * block : 32 * block + 32] for block in BLOCKS], axis=0
        )

    def compute(chunk):
        name, tile = plan[chunk]
        if name not in ready:
            ready.add(name)
            if name == "fc2":
                turn_wide(hid.at[core], 0)
                for high in (0, 1):
                    hid_copy(high).wait_recv()
                turn_wide(hid_come, 256)
                gout_copy().wait_recv()
            else:
                arrived(groups[name])
                if name == "out":
                    gbr_copy().wait_recv()
                turn_rows(x_buf.at[turned_from[name]], xt_buf)
        if name == "fc2":
            if tile % 2 == 0:
                both = jnp.dot(
                    xht_buf[...],
                    gout_buf[:, 128 * tile : 128 * tile + 256],
                    preferred_element_type=jnp.float32,
                ).reshape(64, 32, 256)
                put(chunk, both[:, :16].astype(jnp.bfloat16))
                put(chunk + 1, both[:, 16:].astype(jnp.bfloat16))
            return
        if name == "emb":
            right = (band_pixels(2 * tile), band_pixels(2 * tile + 1))
        else:
            if name == "qkv":
                gp_copy(tile).wait_recv()
                tile = order[tile]
            if name == "fc1":
                gpre_copy(tile).wait_recv()
            buf = {"fc1": gpre_buf, "out": gbr_buf, "qkv": gp_buf}[name]
            right = (
                buf[:, 512 * tile : 512 * tile + 256],
                buf[:, 512 * tile + 256 : 512 * tile + 512],
            )
        put(chunk, chunk_product(xt_buf[...], *right))

    def finisher(chunk):
        name, tile = plan[chunk]
        if name == "fc2":

            def finish(total):
                at = 16 * (tile % 2)
                fc2_out[at : at + 16, 128 * (tile - tile % 2) : 128 * (tile - tile % 2) + 256] = total

            return finish
        if name == "qkv":
            tile = order[tile]
        return wide_finish({"fc1": fc1_out, "out": out_out, "qkv": qkv_out, "emb": emb_out}[name], tile)

    def wave(index):
        for chunk in range(6 * index, 6 * index + 6):
            compute(chunk)

    def step_wave(*pairs):
        for index, step in pairs:
            for chunk in range(6 * index, 6 * index + 6):
                advance(chunk, step, finisher(chunk))

    def block_at(high, low):
        return pl.ds(pl.multiple_of((high * 2 + low) * 256, 256), 256)

    def near_copy(pair):
        return pltpu.make_async_remote_copy(
            src_ref=near_send.at[pair % 2],
            dst_ref=near_come.at[pair % 4],
            send_sem=kv_send_sem.at[0, pair],
            recv_sem=kv_recv_sem.at[0, pair],
            device_id=partner,
            device_id_type=MESH,
        )

    def far_copy(pair):
        return pltpu.make_async_remote_copy(
            src_ref=far_send.at[pair % 2],
            dst_ref=far_come.at[pair],
            send_sem=kv_send_sem.at[1, pair],
            recv_sem=kv_recv_sem.at[1, pair],
            device_id=across,
            device_id_type=MESH,
        )

    def heads_back(pair):
        slot = pair % 2
        kv_load(pair).wait()
        at = lax.broadcasted_iota(jnp.int32, (128, 256), 0)
        lane = lax.broadcasted_iota(jnp.int32, (256, 128), 1)
        query = q_pairs[pair].astype(jnp.float32)
        grad = gatt[pair].astype(jnp.float32)
        query_t, grad_t = query.T, grad.T
        key_rows = kv[slot, 0].T
        key_grad = value_grad = None
        query_grads = []
        for head in (0, 1):
            own = (at < 64) if head == 0 else (at >= 64)
            mine = (lane < 64) if head == 0 else (lane >= 64)
            scores = (
                jnp.dot(
                    kv[slot, 0],
                    jnp.where(own, query_t, 0.0).astype(jnp.bfloat16),
                    preferred_element_type=jnp.float32,
                )
                + mask[...]
            )
            probs = jnp.exp(scores - lse[pair, head : head + 1, :])
            prob_grad = jnp.dot(
                kv[slot, 1],
                jnp.where(own, grad_t, 0.0).astype(jnp.bfloat16),
                preferred_element_type=jnp.float32,
            )
            mean = jnp.sum(probs * prob_grad, axis=0, keepdims=True)
            score_grad = (probs * (prob_grad - mean)).astype(jnp.bfloat16)
            query_grads.append(
                jnp.dot(
                    key_rows[64 * head : 64 * head + 64],
                    score_grad,
                    preferred_element_type=jnp.float32,
                )
            )
            key_part = jnp.dot(
                score_grad,
                jnp.where(mine, query, 0.0).astype(jnp.bfloat16),
                preferred_element_type=jnp.float32,
            )
            value_part = jnp.dot(
                probs.astype(jnp.bfloat16),
                jnp.where(mine, grad, 0.0).astype(jnp.bfloat16),
                preferred_element_type=jnp.float32,
            )
            key_grad = key_part if head == 0 else key_grad + key_part
            value_grad = value_part if head == 0 else value_grad + value_part
        if pair + 2 < 8:
            kv_load(pair + 2).start()
        if pair >= 2:
            near_copy(pair - 2).wait_send()
        gp_buf[0:256, 128 * pair : 128 * pair + 128] = (
            jnp.concatenate(query_grads, axis=0).T * HD ** (-0.5)
        ).astype(jnp.bfloat16)
        whole_grad[0] = key_grad
        whole_grad[1] = value_grad
        for kind in (0, 1):
            near_send[pair % 2, 0, kind] = whole_grad[kind, block_at(x_hi, 1 - core), :].astype(
                jnp.bfloat16
            )
            near_send[pair % 2, 1, kind] = whole_grad[kind, block_at(1 - x_hi, 1 - core), :].astype(
                jnp.bfloat16
            )
        if pair >= 4:
            pl.semaphore_wait(kv_credit.at[pair - 4], 1)
        near_copy(pair).start()
        for kind in (0, 1):
            held[pair % 2, kind] = whole_grad[kind, block_at(x_hi, core), :]
            far_held[pair % 2, kind] = whole_grad[kind, block_at(1 - x_hi, core), :]

    def pass_far(pair):
        near_copy(pair).wait_recv()
        if pair >= 2:
            far_copy(pair - 2).wait_send()
        for kind in (0, 1):
            far_send[pair % 2, kind] = (
                far_held[pair % 2, kind] + near_come[pair % 4, 1, kind].astype(jnp.float32)
            ).astype(jnp.bfloat16)
        far_copy(pair).start()
        for kind in (0, 1):
            at = 1024 * (kind + 1) + 128 * pair
            gp_buf[0:256, at : at + 128] = (
                held[pair % 2, kind] + near_come[pair % 4, 0, kind].astype(jnp.float32)
            ).astype(jnp.bfloat16)
        if pair < 4:
            pl.semaphore_signal(
                kv_credit.at[pair], inc=1, device_id=partner, device_id_type=MESH
            )

    def close(pair):
        far_copy(pair).wait_recv()
        for kind in (0, 1):
            at = 1024 * (kind + 1) + 128 * pair
            gp_buf[0:256, at : at + 128] = (
                gp_buf[0:256, at : at + 128].astype(jnp.float32)
                + far_come[pair, kind].astype(jnp.float32)
            ).astype(jnp.bfloat16)

    def through_qkv(index):
        tall_load(8 + index).wait()
        tile = order[index]
        part = nt_dot(gp_buf[0:256, 512 * tile : 512 * tile + 512], tall[(8 + index) % 3])
        grown_buf[...] = part if index == 0 else grown_buf[...] + part
        used(tall_load, 8 + index, 14)

    for copy in loads[:3] + loads[4:10]:
        copy.wait()
    hot_copy().start()
    total = stream[...] + row(out_bias)
    for index in (0, 1):
        wide_load(index).wait()
        total = total + jnp.dot(
            n2[:, 512 * index : 512 * index + 512], wide[index], preferred_element_type=jnp.float32
        )
        used(wide_load, index, 18)
    middle[...] = total
    hat, _ = norm_parts(total)
    n2[...] = (hat * row(gain2) + row(bias2)).astype(jnp.bfloat16)
    begin(groups["fc1"])
    loads[3].wait()
    gout_buf[0:256, :] = (gs[...].astype(jnp.float32) * hot_buf[0:256, 4:5]).astype(jnp.bfloat16)
    gout_copy().start()
    def mlp_tile(tile):
        span = slice(512 * tile, 512 * tile + 512)
        tall_load(tile).wait()
        wide_load(2 + tile).wait()
        pre = jnp.dot(n2[...], tall[tile % 3], preferred_element_type=jnp.float32) + fc1_bias[
            span
        ].reshape(1, 512)
        cdf = 0.5 * (1.0 + lax.erf(pre * (0.5**0.5)))
        hidden = (pre * cdf).astype(jnp.bfloat16)
        at = 1024 * (tile // 4) + 512 * (tile % 2)
        hid[(tile // 2) % 2, :, at : at + 512] = hidden
        slope = cdf + pre * (jnp.exp(-0.5 * pre * pre) * 0.3989422804014327)
        back = (nt_dot(gout_buf[0:256, :], wide[(2 + tile) % 3]) * slope).astype(jnp.bfloat16)
        gpre_buf[0:256, span] = back
        gpre_copy(tile).start()
        ahead = jnp.dot(hidden, wide[(2 + tile) % 3], preferred_element_type=jnp.float32)
        used(wide_load, 2 + tile, 18)
        behind = nt_dot(back, tall[tile % 3])
        used(tall_load, tile, 14)
        acc[...] = ahead if tile == 0 else acc[...] + ahead
        grown_buf[...] = behind if tile == 0 else grown_buf[...] + behind
        quarter, at = tile // 2, 512 * (tile % 2)
        sums[4 + quarter : 5 + quarter, at : at + 512] = jnp.sum(
            back.astype(jnp.float32), axis=0, keepdims=True
        )
        if tile % 4 == 3:
            hid_copy(tile // 4).start()

    block_copy = pltpu.make_async_copy(gs, block_out, load_sem.at[13])

    def mlp_back():
        gs[...] = (
            hot_buf[0:256, 4:5] * (middle[...] + (acc[...] + row(fc2_bias)))
        ).astype(jnp.bfloat16)
        block_copy.start()
        upstream = gout_buf[0:256, :].astype(jnp.float32)
        sums[3:4, :] = jnp.sum(upstream, axis=0, keepdims=True)
        grown = grown_buf[...]
        hat, scale = norm_parts(middle[...])
        sums[1:2, :] = jnp.sum(grown * hat, axis=0, keepdims=True)
        sums[2:3, :] = jnp.sum(grown, axis=0, keepdims=True)
        grown = grown * row(gain2)
        middle[...] = upstream + scale * (
            grown
            - jnp.mean(grown, axis=-1, keepdims=True)
            - hat * jnp.mean(grown * hat, axis=-1, keepdims=True)
        )
        gbr_buf[0:256, :] = middle[...].astype(jnp.bfloat16)
        gbr_copy().start()
        sums[0:1, :] = jnp.sum(gbr_buf[0:256, :].astype(jnp.float32), axis=0, keepdims=True)

    def attention_grad():
        for index in (0, 1):
            wide_load(10 + index).wait()
            back = nt_dot(gbr_buf[0:256, :], wide[(10 + index) % 3]).astype(jnp.bfloat16)
            used(wide_load, 10 + index, 18)
            for pair in range(4):
                gatt[4 * index + pair] = back[:, 128 * pair : 128 * pair + 128]

    def norm_back():
        block_copy.wait()
        grown = grown_buf[...]
        hat, scale = norm_parts(stream[...])
        lanes[...] = jnp.zeros_like(lanes)
        lanes[4:5, :] = jnp.sum(grown * hat, axis=0, keepdims=True)
        lanes[5:6, :] = jnp.sum(grown, axis=0, keepdims=True)
        grown = grown * row(gain1)
        gs[...] = (
            middle[...]
            + scale
            * (
                grown
                - jnp.mean(grown, axis=-1, keepdims=True)
                - hat * jnp.mean(grown * hat, axis=-1, keepdims=True)
            )
        ).astype(jnp.bfloat16)
        begin(groups["emb"])
        arrived(groups["side"])
        hot_copy().wait_recv()

    def side_rows():
        lanes[6:7, :] = jnp.sum(gp_buf[0:256, 0:1024].astype(jnp.float32), axis=0, keepdims=True)
        lanes[7:8, :] = jnp.sum(gp_buf[0:256, 2048:3072].astype(jnp.float32), axis=0, keepdims=True)
        lanes[0:4, :] = tn_dot(hot_buf[0:256, :].astype(jnp.bfloat16), gs[...])[0:4]
        lanes[8:16, :] = sums[...]
        begin(groups["rows"])

    def bias_chunk():
        arrived(groups["rows"])
        groups["rows"][0][1].wait_send()
        lanes[0:16, :] = row_buf[0] + row_buf[1]
        halves_t = [
            lanes[:, pl.ds(pl.multiple_of(high * 512 + core * 256, 128), 256)].T.reshape(32, 8, 128)
            for high in (0, 1)
        ]
        lane = lax.broadcasted_iota(jnp.int32, (32, 8, 128), 2)
        quarters = lanes[...].T.reshape(32, 4, 8, 128)
        for high in (0, 1):
            wide = jnp.where(lane < 12, halves_t[high], 0.0)
            for part in range(4):
                here = jnp.where(
                    core == 0,
                    quarters[:, part, :, 12 + 2 * high : 13 + 2 * high],
                    quarters[:, part, :, 13 + 2 * high : 14 + 2 * high],
                )
                wide = wide + jnp.where(lane == 12 + part, here, 0.0)
            halves_t[high] = wide
        turned = jnp.concatenate(halves_t, axis=0)
        put_f(0, jnp.concatenate([turned[b : b + 1] for b in BLOCKS], axis=0))

    out = pltpu.make_async_copy(pix_grad, pix_out, load_sem.at[14])

    def pixels_back():
        parts = [None] * 3
        for index in range(6):
            wide_load(12 + index).wait()
            for side in (0, 1):
                band, third = divmod(2 * index + side, 3)
                term = hot_buf[0:256, band : band + 1] * nt_dot(
                    gs[...], wide[(12 + index) % 3, 256 * side : 256 * side + 256, :]
                )
                parts[third] = term if parts[third] is None else parts[third] + term
            used(wide_load, 12 + index, 18)
        for third in range(3):
            pix_grad[:, 256 * third : 256 * third + 256] = parts[third].astype(jnp.bfloat16)
        out.start()

    def finish_bias(total):
        bias_out[...] = total

    actions = {
        HEADS: heads_back,
        FAR: pass_far,
        CLOSE: close,
        GP: lambda index: gp_copy(index).start(),
        PUT: compute,
        ADV: lambda chunk, step: advance(chunk, step, finisher(chunk)),
        THROUGH: through_qkv,
        NORM: norm_back,
        ROWS: side_rows,
        BIAS: bias_chunk,
        ADVB: lambda step: advance_f(0, step, finish_bias),
        PIX: pixels_back,
        MLP: mlp_tile,
        POST: mlp_back,
        GATT: attention_grad,
    }
    for name, *where_at in SCHEDULE:
        if (name, *where_at) == (HEADS, 0):
            for copy in loads[10:]:
                copy.wait()
        actions[name](*where_at)
    out.wait()
    for _, remote in made[:-1]:
        remote.wait_send()
    for pair in range(8):
        if pair >= 6:
            near_copy(pair).wait_send()
            far_copy(pair).wait_send()
    for index in range(6):
        gp_copy(index).wait_send()
    for tile in range(8):
        gpre_copy(tile).wait_send()
    for copy in (gout_copy(), gbr_copy(), hot_copy(), hid_copy(0), hid_copy(1)):
        copy.wait_send()
    for chunk in range(CHUNKS):
        drain(chunk)
    drain_f(0)


def backward(*operands):
    any_space = pl.BlockSpec(memory_space=pl.ANY)
    in_vmem = pl.BlockSpec(memory_space=pltpu.VMEM)
    half, full = jnp.bfloat16, jnp.float32
    shape = jax.ShapeDtypeStruct
    dma = pltpu.SemaphoreType.DMA
    return pl.pallas_call(
        backward_kernel,
        out_shape=(
            shape((256, 1024), half),
            shape((256, 768), half),
            shape((8, 3072), full),
            shape((8, 3072), full),
            shape((8, 1024), full),
            shape((8, 4096), full),
            shape((32, 1024), full),
            shape((8, 128), full),
        ),
        in_specs=[any_space] * 21,
        out_specs=(any_space,) * 2 + (in_vmem,) * 6,
        scratch_shapes=[
            pltpu.VMEM((3, 512, 512), half),
            pltpu.VMEM((2, 256, 2048), half),
            pltpu.VMEM((256, 2048), half),
            pltpu.VMEM((512, 1024), half),
            pltpu.VMEM((512, 4096), half),
            pltpu.VMEM((512, 1024), half),
            pltpu.VMEM((512, 3072), half),
            pltpu.VMEM((512, 768), half),
            pltpu.VMEM((512, 128), full),
            pltpu.VMEM((2, 16, 1024), full),
            pltpu.VMEM((128, 1024), full),
            pltpu.VMEM((8, 1024), full),
            pltpu.VMEM((512, 512), half),
            pltpu.VMEM((2048, 512), half),
            pltpu.VMEM((SLOTS, 64, 16, 256), half),
            pltpu.VMEM((SLOTS, 56, 16, 256), half),
            pltpu.VMEM((CHUNKS, 14, 16, 256), half),
            pltpu.VMEM((CHUNKS, 7, 16, 256), half),
            pltpu.VMEM((1, 64, 8, 128), full),
            pltpu.VMEM((1, 56, 8, 128), full),
            pltpu.VMEM((1, 14, 8, 128), full),
            pltpu.VMEM((1, 7, 8, 128), full),
            pltpu.VMEM((8, 256, 128), half),
            pltpu.VMEM((2, 2, 1024, 128), half),
            pltpu.VMEM((8, 256, 128), half),
            pltpu.VMEM((1024, 256), full),
            pltpu.VMEM((2, 2, 2, 256, 128), half),
            pltpu.VMEM((4, 2, 2, 256, 128), half),
            pltpu.VMEM((2, 2, 256, 128), half),
            pltpu.VMEM((8, 2, 256, 128), half),
            pltpu.VMEM((2, 2, 256, 128), full),
            pltpu.VMEM((2, 2, 256, 128), full),
            pltpu.VMEM((2, 1024, 128), full),
            pltpu.VMEM((256, 1024), half),
            pltpu.VMEM((256, 1024), full),
            pltpu.VMEM((256, 1024), full),
            pltpu.VMEM((256, 1024), full),
            pltpu.VMEM((256, 1024), full),
            pltpu.VMEM((256, 1024), half),
            pltpu.VMEM((256, 768), half),
            pltpu.VMEM((3, 1024, 512), half),
            pltpu.VMEM((3, 512, 1024), half),
            pltpu.VMEM((8, 2, 256), full),
            pltpu.VMEM((1024,), full),
            pltpu.VMEM((1024,), full),
            pltpu.VMEM((1024,), full),
            pltpu.VMEM((1024,), full),
            pltpu.VMEM((4096,), full),
            pltpu.VMEM((1024,), full),
            dma((10,)),
            dma((10,)),
            dma((10,)),
            dma((CHUNKS, 6)),
            dma((CHUNKS, 6)),
            pltpu.SemaphoreType.REGULAR((CHUNKS - SLOTS, 3)),
            dma((1, 6)),
            dma((1, 6)),
            dma((15,)),
            dma((2,)),
            dma((3,)),
            dma((3,)),
            dma((2, 8)),
            dma((2, 8)),
            pltpu.SemaphoreType.REGULAR((4,)),
            dma((6,)),
            dma((6,)),
            dma((8,)),
            dma((8,)),
            dma((5,)),
            dma((5,)),
        ],
        compiler_params=pltpu.CompilerParams(
            collective_id=2, has_side_effects=True, vmem_limit_bytes=VMEM_BYTES
        ),
        name="backward",
    )(*operands)


def finish_kernel(*refs):
    sources, dests, bufs = refs[:8], refs[8:25], refs[25:33]
    cols, bands, flat, in_sem, out_sem = refs[33:]
    loads = []
    for source, buf in zip(sources, bufs):
        loads.append(pltpu.make_async_copy(source, buf, in_sem.at[len(loads)]))
    for copy in reversed(loads):
        copy.start()
    stores = []

    def store(source, dest):
        stores.append(pltpu.make_async_copy(source, dest, out_sem.at[len(stores)]))
        stores[-1].start()

    loads[7].wait()
    sums = bufs[7][...]
    cols[...] = sums.T[0:16, :]
    for index in range(8):
        store(cols.at[pl.ds(4 + index, 1), :], dests[8 + index])
    bands[...] = cols[0:4, :]
    store(bands, dests[7])
    lane = lax.broadcasted_iota(jnp.int32, (8, 128), 1)
    wide = jnp.zeros((8, 128), jnp.float32)
    for part in range(4):
        wide = wide + jnp.where(lane // 8 == part, sums[:, 12 + part : 13 + part], 0.0)
    wide = jnp.where(lane % 8 == lax.broadcasted_iota(jnp.int32, (8, 128), 0), wide, 0.0)
    flat[...] = jnp.sum(wide, axis=0, keepdims=True)[:, 0:32]
    store(flat, dests[16])
    for index in range(7):
        loads[index].wait()
        if index < 6:
            store(bufs[index], dests[index])
    for band in range(4):
        store(bufs[6].at[:, pl.ds(768 * band, 768)], dests[6].at[band])
    for copy in stores:
        copy.wait()


def finish(*operands):
    any_space = pl.BlockSpec(memory_space=pl.ANY)
    full = jnp.float32
    shape = jax.ShapeDtypeStruct
    return pl.pallas_call(
        finish_kernel,
        out_shape=tuple(shape(array.shape, array.dtype) for array in operands[:6])
        + (shape((4, 8, 768), full), shape((4, 8), full))
        + (shape((1, 8), full),) * 8
        + (shape((1, 32), full),),
        in_specs=[any_space] * 8,
        out_specs=(any_space,) * 17,
        scratch_shapes=[pltpu.VMEM(array.shape, array.dtype) for array in operands]
        + [
            pltpu.VMEM((16, 8), full),
            pltpu.VMEM((4, 8), full),
            pltpu.VMEM((1, 32), full),
            pltpu.SemaphoreType.DMA((8,)),
            pltpu.SemaphoreType.DMA((20,)),
        ],
        compiler_params=pltpu.CompilerParams(vmem_limit_bytes=VMEM_BYTES),
        name="finish",
    )(*operands)


def on_device(
    pixels,
    positions,
    segments,
    groups,
    cotangent,
    emb_weight,
    emb_bias,
    norm1_gain,
    norm1_bias,
    qkv_weight,
    query_bias,
    value_bias,
    out_weight,
    out_bias,
    norm2_gain,
    norm2_bias,
    fc1_weight,
    fc1_bias,
    fc2_weight,
    fc2_bias,
):
    rows_dev, slice_len, pix_len = pixels.shape
    model_width = qkv_weight.shape[0]
    band_count = emb_weight.shape[0]
    tok_count = rows_dev * slice_len
    flat_pixels = pixels.reshape(tok_count, pix_len)
    flat_emb = emb_weight.reshape(band_count * pix_len, model_width)
    hot_live, mask, stream, normed_one, query_pairs, key_value, log_sums, attended = forward(
        flat_pixels,
        positions.reshape(tok_count, model_width),
        segments,
        groups,
        emb_bias,
        norm1_gain,
        norm1_bias,
        query_bias,
        value_bias,
        flat_emb,
        qkv_weight,
    )
    block_out, pixel_grad, emb_sum, qkv_sum, out_sum, fc1_sum, fc2_sum, bias_sum = backward(
        attended,
        stream,
        cotangent.reshape(tok_count, model_width),
        hot_live,
        mask,
        query_pairs,
        key_value,
        log_sums,
        normed_one,
        flat_pixels,
        norm1_gain,
        norm2_gain,
        norm2_bias,
        out_bias,
        fc1_bias,
        fc2_bias,
        flat_emb,
        qkv_weight,
        out_weight,
        fc1_weight,
        fc2_weight,
    )
    block_out, pixel_grad, qkv_sum, out_sum, fc1_sum, fc2_sum, emb_sum, *rest = finish(
        block_out, pixel_grad, qkv_sum, out_sum, fc1_sum, fc2_sum, emb_sum, bias_sum
    )
    emb_bias_sum, gain1, bias1, query, value, out, gain2, bias2, last, wide = (
        part if index == 0 else part.reshape(-1) for index, part in enumerate(rest)
    )
    return (
        block_out.reshape(rows_dev, slice_len, model_width),
        pixel_grad.reshape(rows_dev, slice_len, pix_len),
        jnp.swapaxes(emb_sum, 1, 2),
        emb_bias_sum,
        gain1,
        bias1,
        qkv_sum,
        query,
        value,
        out_sum,
        out,
        gain2,
        bias2,
        fc1_sum,
        wide,
        fc2_sum,
        last,
    )


def solution(mesh):
    return jax.shard_map(
        on_device,
        mesh=mesh,
        in_specs=(
            P("batch", "blk", None),
            P("batch", "blk", None),
            P("batch", None),
            P("batch", "blk"),
            P("batch", "blk", None),
            P(),
            P(),
            P(),
            P(),
            P(),
            P(),
            P(),
            P(),
            P(),
            P(),
            P(),
            P(),
            P(),
            P(),
            P(),
        ),
        out_specs=(
            P("batch", "blk", None),
            P("batch", "blk", None),
            P(None, None, ("blk", "batch")),
            P(None, ("blk", "batch")),
            P(("blk", "batch")),
            P(("blk", "batch")),
            P(("blk", "batch"), None),
            P(("blk", "batch")),
            P(("blk", "batch")),
            P(("blk", "batch"), None),
            P(("blk", "batch")),
            P(("blk", "batch")),
            P(("blk", "batch")),
            P(("blk", "batch"), None),
            P(("blk", "batch")),
            P(("blk", "batch"), None),
            P(("blk", "batch")),
        ),
        check_vma=False,
    )
```

```python
import jax
import jax.numpy as jnp
from jax import lax
from jax.experimental import pallas as pl
from jax.experimental.pallas import tpu as pltpu
from jax.sharding import PartitionSpec as P

HD = 64
NORM_EPS = 1e-06
MASKED = -1e30
VMEM_BYTES = 64 << 20

MESH = pl.DeviceIdType.MESH
AXES = ("xb", "xa", "yb", "ya", "zb", "za")
ROTATION = ("xa", "ya", "za", "xb", "yb", "zb")
GRAY = (0, 1, 3, 2)
BLOCKS = tuple(16 * x + 4 * y + z for x in GRAY for y in GRAY for z in GRAY)


def place():
    blk = lax.axis_index("blk")
    batch = lax.axis_index("batch")
    return blk // 2, blk % 2, batch // 16, (batch // 4) % 4, batch % 4


def neighbours(where):
    x_hi, core, x_lo, y, z = where

    def device(x_hi, core, x_lo, y, z):
        return (x_hi * 2 + core, x_lo * 16 + y * 4 + z)

    return {
        "core": device(x_hi, 1 - core, x_lo, y, z),
        "xa": device(x_hi, core, 1 - x_lo, y, z),
        "xb": device(1 - x_hi, core, 1 - x_lo, y, z),
        "ya": device(x_hi, core, x_lo, y + 1 - 2 * (y % 2), z),
        "yb": device(x_hi, core, x_lo, 3 - y, z),
        "za": device(x_hi, core, x_lo, y, z + 1 - 2 * (z % 2)),
        "zb": device(x_hi, core, x_lo, y, 3 - z),
    }


def own_bits(where):
    x_hi, _, x_lo, y, z = where
    return {
        "xb": x_hi,
        "xa": (x_hi + x_lo) % 2,
        "yb": y // 2,
        "ya": (y // 2 + y) % 2,
        "zb": z // 2,
        "za": (z // 2 + z) % 2,
    }


DIMS = (
    (3, 5, 1, 0, 2, 4),
    (5, 1, 2, 4, 0, 3),
    (1, 2, 4, 5, 3, 0),
    (0, 4, 5, 3, 1, 2),
    (1, 2, 4, 5, 0, 3),
    (5, 1, 2, 4, 0, 3),
    (1, 2, 3, 4, 5, 0),
    (4, 3, 5, 1, 2, 0),
    (1, 2, 4, 5, 0, 3),
    (2, 3, 4, 5, 1, 0),
    (4, 5, 1, 2, 0, 3),
    (4, 5, 1, 2, 3, 0),
    (2, 4, 5, 1, 0, 3),
    (0, 2, 4, 3, 5, 1),
    (2, 4, 5, 1, 3, 0),
    (2, 4, 5, 1, 0, 3),
    (1, 2, 4, 5, 0, 3),
    (5, 0, 1, 2, 3, 4),
    (4, 0, 5, 1, 2, 3),
    (0, 1, 2, 3, 4, 5),
    (4, 5, 0, 1, 2, 3),
    (1, 2, 4, 5, 0, 3),
    (3, 4, 5, 0, 1, 2),
    (5, 0, 1, 2, 4, 3),
    (4, 5, 0, 1, 2, 3),
    (3, 2, 4, 0, 5, 1),
    (5, 3, 1, 2, 4, 0),
    (2, 3, 4, 5, 1, 0),
    (0, 1, 2, 3, 4, 5),
    (1, 2, 3, 4, 5, 0),
)


def chunk_dims(chunk):
    return tuple(ROTATION[axis] for axis in DIMS[chunk])


def split_shape(dims, step):
    left = [axis for axis in AXES if axis not in dims[:step]]
    at = left.index(dims[step])
    return 2**at, 2 ** (len(left) - 1 - at)


KEEP_AT = (0, 32, 0, 0, 8, 12)
SEND_AT = (32, 48, 8, 4, 10, 13)
ARRIVE_AT = (0, 32, 48, 0, 4, 6)
SLOTS = 18


def reducer(near, bits, dims_of, buffers, send_sem, recv_sem, credit, chunks):
    work, arrive, work_end, arrive_end = buffers

    def held(chunk, step):
        return work.at[chunk % SLOTS] if step < 3 else work_end.at[chunk]

    def come(chunk, step):
        return arrive.at[chunk % SLOTS] if step < 3 else arrive_end.at[chunk]

    def hop(chunk, step):
        half = 32 >> step
        return pltpu.make_async_remote_copy(
            src_ref=held(chunk, step).at[pl.ds(SEND_AT[step], half)],
            dst_ref=come(chunk, step).at[pl.ds(ARRIVE_AT[step], half)],
            send_sem=send_sem.at[chunk, step],
            recv_sem=recv_sem.at[chunk, step],
            device_id=near[dims_of(chunk)[step]],
            device_id_type=MESH,
        )

    def send(chunk, step):
        if step < 3 and chunk >= SLOTS:
            pl.semaphore_wait(credit.at[chunk - SLOTS, step], 1)
        hop(chunk, step).start()

    def put(chunk, result):
        if chunk >= SLOTS:
            for step in (1, 2):
                hop(chunk - SLOTS, step).wait_send()
        dims = dims_of(chunk)
        before, after = split_shape(dims, 0)
        own = bits[dims[0]]
        for a in range(before):
            for bit in (0, 1):
                other = own if bit == 0 else 1 - own
                piece = result[(2 * a + bit) * after : (2 * a + bit + 1) * after]
                held(chunk, 0)[pl.ds(other * 32 + a * after, after)] = piece
        send(chunk, 0)

    def advance(chunk, step, finish):
        hop(chunk, step).wait_recv()
        keep, come_at = KEEP_AT[step], ARRIVE_AT[step]
        here, there = held(chunk, step), come(chunk, step)
        if step == 5:
            finish(here[keep].astype(jnp.float32) + there[come_at].astype(jnp.float32))
            return
        if step == 0:
            hop(chunk, 0).wait_send()
        dims = dims_of(chunk)
        before, after = split_shape(dims, step + 1)
        own = bits[dims[step + 1]]
        target = held(chunk, step + 1)
        for bit, base in ((1 - own, SEND_AT[step + 1]), (own, KEEP_AT[step + 1])):

            def merge(a, carry, bit=bit, base=base):
                at = (2 * a + bit) * after
                target[pl.ds(base + a * after, after)] = (
                    here[pl.ds(keep + at, after)] + there[pl.ds(come_at + at, after)]
                )
                return carry

            lax.fori_loop(0, before, merge, 0, unroll=min(before, 8))
            if base == SEND_AT[step + 1]:
                send(chunk, step + 1)
        if step < 3 and chunk + SLOTS < chunks:
            pl.semaphore_signal(
                credit.at[chunk, step],
                inc=1,
                device_id=near[dims_of(chunk + SLOTS)[step]],
                device_id_type=MESH,
            )

    def drain(chunk):
        for step in range(1 if chunk + SLOTS >= chunks else 3, 6):
            hop(chunk, step).wait_send()

    return put, advance, drain


def nt_dot(left, right):
    return lax.dot_general(left, right, (((1,), (1,)), ((), ())), preferred_element_type=jnp.float32)


def tn_dot(left, right):
    return lax.dot_general(left, right, (((0,), (0,)), ((), ())), preferred_element_type=jnp.float32)


def norm_parts(values):
    center = values - jnp.mean(values, axis=-1, keepdims=True)
    spread = jnp.mean(center * center, axis=-1, keepdims=True)
    scale = lax.rsqrt(spread + NORM_EPS)
    return center * scale, scale


def row(vector):
    return vector[...].reshape(1, 1024)


def forward_kernel(
    pix_in, pos_in, seg_in, band_in, emb_bias_in, gain1_in, bias1_in, query_bias_in, value_bias_in, emb_in, qkv_in,
    hot_out, mask_out, stream_out, n1_out, q_out, kv_out, lse_out, att_out,
    pix, pos, hot, mask, emb_w, qkv_w, stream, flat, n1, q_pairs, kv, att,
    far_n1, run_max, run_sum, run_out, *small,
):
    (
        seg, band_of, emb_bias, gain1, bias1, query_bias, value_bias,
        load_sem, save_sem, pair_sem, send_sem, recv_sem,
    ) = small
    where = place()
    x_hi, core, x_lo, y, z = where
    partner = (x_hi * 2 + 1 - core, x_lo * 16 + y * 4 + z)
    across = ((1 - x_hi) * 2 + core, x_lo * 16 + y * 4 + z)
    barrier = pltpu.get_barrier_semaphore()
    for target in (partner, across):
        pl.semaphore_signal(barrier, inc=1, device_id=target, device_id_type=MESH)

    loads = {}

    def load(name, source, dest):
        copy = pltpu.make_async_copy(source, dest, load_sem.at[len(loads)])
        copy.start()
        loads[name] = copy

    saves = []

    def save(source, dest):
        copy = pltpu.make_async_copy(source, dest, save_sem.at[len(saves)])
        copy.start()
        saves.append(copy)

    load("seg", seg_in, seg)
    load("band", band_in, band_of)
    load("pix", pix_in, pix)
    load("eb", emb_bias_in, emb_bias)
    load("g1", gain1_in, gain1)
    load("b1", bias1_in, bias1)
    load("qb", query_bias_in, query_bias)
    load("vb", value_bias_in, value_bias)
    for band in range(4):
        span = pl.ds(768 * band, 768)
        load("emb%d" % band, emb_in.at[span, :], emb_w.at[span, :])
    load("pos", pos_in, pos)
    for part in (1, 2, 0):
        span = pl.ds(1024 * part, 1024)
        load("qkv%d" % part, qkv_in.at[:, span], qkv_w.at[:, span])
    loads["seg"].wait()
    loads["band"].wait()
    own_seg = seg[:, pl.ds(pl.multiple_of((x_hi * 2 + core) * 256, 256), 256)]
    at = lax.broadcasted_iota(jnp.int32, (128, 256), 0)
    hot[...] = (
        jnp.where(at == band_of[...], 1.0, 0.0)
        + jnp.where(at == 4, 1.0, 0.0) * jnp.where(own_seg >= 0, 1.0, 0.0)
    ).T
    save(hot, hot_out)

    for name in ("eb", "g1", "b1", "qb", "vb"):
        loads[name].wait()
    flat[0:1, :] = row(query_bias)
    flat[1:2, :] = row(value_bias)

    loads["pix"].wait()
    total = None
    for band in range(4):
        chosen = hot[:, band : band + 1]
        picked = (pix[...].astype(jnp.float32) * chosen).astype(jnp.bfloat16)
        loads["emb%d" % band].wait()
        term = jnp.dot(
            picked, emb_w[768 * band : 768 * band + 768, :], preferred_element_type=jnp.float32
        ) + chosen * emb_bias[band : band + 1, :]
        total = term if total is None else total + term
    loads["pos"].wait()
    stream[...] = total + pos[...].astype(jnp.float32)
    save(stream, stream_out)
    hat, _ = norm_parts(stream[...])
    n1[...] = (hat * row(gain1) + row(bias1)).astype(jnp.bfloat16)

    own_rows = pl.ds(pl.multiple_of((x_hi * 2 + core) * 256, 256), 256)

    def far_rows(low, piece):
        return pl.ds(pl.multiple_of(((1 - x_hi) * 2 + low) * 256 + 128 * piece, 128), 128)

    def push(source, dest, which, index, target):
        return pltpu.make_async_remote_copy(
            src_ref=source,
            dst_ref=dest,
            send_sem=send_sem.at[which, index],
            recv_sem=recv_sem.at[which, index],
            device_id=target,
            device_id_type=MESH,
        )

    def norm_copy(piece):
        span = pl.ds(128 * piece, 128)
        return push(n1.at[span, :], far_n1.at[span, :], 0, piece, across)

    def to_partner(pair):
        piece = kv.at[pair, :, own_rows, :]
        return push(piece, piece, 1, pair, partner)

    def far_copy(piece):
        part = kv.at[:, :, far_rows(core, piece), :]
        return push(part, part, 2, piece, partner)

    pl.semaphore_wait(barrier, 2)
    for piece in (0, 1):
        norm_copy(piece).start()
    save(n1, n1_out)
    loads["qkv1"].wait()
    loads["qkv2"].wait()

    def keys_values(source, tile, target):
        span = pl.ds(pl.multiple_of(1024 + 256 * tile, 256), 256)
        keys = jnp.dot(source, qkv_w[:, span], preferred_element_type=jnp.float32).astype(
            jnp.bfloat16
        )
        span = pl.ds(pl.multiple_of(2048 + 256 * tile, 256), 256)
        shift = flat[1:2, pl.ds(pl.multiple_of(256 * tile, 256), 256)]
        values = (
            jnp.dot(source, qkv_w[:, span], preferred_element_type=jnp.float32) + shift
        ).astype(jnp.bfloat16)
        for side in (0, 1):
            kv[2 * tile + side, 0, target, :] = keys[:, 128 * side : 128 * side + 128]
            kv[2 * tile + side, 1, target, :] = values[:, 128 * side : 128 * side + 128]

    def project(tile, carry):
        keys_values(n1[...], tile, own_rows)
        for side in (0, 1):
            to_partner(2 * tile + side).start()
        return carry

    lax.fori_loop(0, 4, project, 0, unroll=4)
    loads["qkv0"].wait()

    def project_query(tile, carry):
        span = pl.ds(pl.multiple_of(256 * tile, 256), 256)
        query = (
            jnp.dot(n1[...], qkv_w[:, span], preferred_element_type=jnp.float32)
            + flat[0:1, span]
        ).astype(jnp.bfloat16)
        query = (query.astype(jnp.float32) * HD ** (-0.5)).astype(jnp.bfloat16)
        for side in (0, 1):
            q_pairs[2 * tile + side] = query[:, 128 * side : 128 * side + 128]
        return carry

    lax.fori_loop(0, 4, project_query, 0, unroll=4)
    save(q_pairs, q_out)
    key_seg = jnp.broadcast_to(seg[...].astype(jnp.float32), (128, 1024)).T[:, 0:1]
    mask[...] = jnp.where(key_seg == own_seg.astype(jnp.float32), 0.0, MASKED)
    save(mask, mask_out)

    def project_far(piece):
        norm_copy(piece).wait_recv()

        def step(tile, carry):
            keys_values(far_n1[128 * piece : 128 * piece + 128, :], tile, far_rows(core, piece))
            return carry

        lax.fori_loop(0, 4, step, 0, unroll=4)
        far_copy(piece).start()

    def attend(span, first=False, last=False):
        def body(pair, carry):
            if first:
                to_partner(pair).wait_recv()
            if last:
                pltpu.make_async_copy(kv.at[pair], kv_out.at[pair], pair_sem.at[pair]).start()
            keys = kv[pair, 0, span, :]
            value_rows = kv[pair, 1, span, :].T
            bias = mask[span, :]
            turned = q_pairs[pair].astype(jnp.float32).T
            at = lax.broadcasted_iota(jnp.int32, (128, 256), 0)
            heads = []
            for head in (0, 1):
                own = (at < 64) if head == 0 else (at >= 64)
                mine = jnp.where(own, turned, 0.0).astype(jnp.bfloat16)
                scores = jnp.dot(keys, mine, preferred_element_type=jnp.float32) + bias
                peak = jnp.max(scores, axis=0, keepdims=True)
                if not first:
                    before = run_max[pair, head : head + 1, :]
                    peak = jnp.maximum(peak, before)
                    fade = jnp.exp(before - peak)
                expo = jnp.exp(scores - peak)
                norm = jnp.sum(expo, axis=0, keepdims=True)
                out = jnp.dot(
                    value_rows[64 * head : 64 * head + 64],
                    expo.astype(jnp.bfloat16),
                    preferred_element_type=jnp.float32,
                )
                if not first:
                    norm = norm + fade * run_sum[pair, head : head + 1, :]
                    out = out + fade * run_out[pair, 64 * head : 64 * head + 64, :]
                if last:
                    heads.append(out / norm)
                    lse_out[pair, head : head + 1, :] = peak + jnp.log(norm)
                else:
                    run_max[pair, head : head + 1, :] = peak
                    run_sum[pair, head : head + 1, :] = norm
                    run_out[pair, 64 * head : 64 * head + 64, :] = out
            if last:
                att[:, pl.ds(pl.multiple_of(pair * 128, 128), 128)] = jnp.concatenate(
                    heads, axis=0
                ).T.astype(jnp.bfloat16)
            return carry

        lax.fori_loop(0, 8, body, 0, unroll=2)

    attend(pl.ds(pl.multiple_of(x_hi * 512, 512), 512), first=True)
    for piece in (0, 1):
        project_far(piece)
    for piece in (0, 1):
        far_copy(piece).wait_recv()
    attend(pl.ds(pl.multiple_of((1 - x_hi) * 512, 512), 512), last=True)
    save(att, att_out)
    for copy in saves:
        copy.wait()

    def drain(pair, carry):
        to_partner(pair).wait_send()
        pltpu.make_async_copy(kv.at[pair], kv_out.at[pair], pair_sem.at[pair]).wait()
        return carry

    lax.fori_loop(0, 8, drain, 0)
    for piece in (0, 1):
        norm_copy(piece).wait_send()
        far_copy(piece).wait_send()


def forward(*operands):
    any_space = pl.BlockSpec(memory_space=pl.ANY)
    in_vmem = pl.BlockSpec(memory_space=pltpu.VMEM)
    half, full = jnp.bfloat16, jnp.float32
    shape = jax.ShapeDtypeStruct
    return pl.pallas_call(
        forward_kernel,
        out_shape=(
            shape((256, 128), full),
            shape((1024, 256), full),
            shape((256, 1024), full),
            shape((256, 1024), half),
            shape((8, 256, 128), half),
            shape((8, 2, 1024, 128), half),
            shape((8, 2, 256), full),
            shape((256, 1024), half),
        ),
        in_specs=[any_space] * 11,
        out_specs=(any_space,) * 6 + (in_vmem, any_space),
        scratch_shapes=[
            pltpu.VMEM((256, 768), half),
            pltpu.VMEM((256, 1024), half),
            pltpu.VMEM((256, 128), full),
            pltpu.VMEM((1024, 256), full),
            pltpu.VMEM((3072, 1024), half),
            pltpu.VMEM((1024, 3072), half),
            pltpu.VMEM((256, 1024), full),
            pltpu.VMEM((8, 1024), full),
            pltpu.VMEM((256, 1024), half),
            pltpu.VMEM((8, 256, 128), half),
            pltpu.VMEM((8, 2, 1024, 128), half),
            pltpu.VMEM((256, 1024), half),
            pltpu.VMEM((256, 1024), half),
            pltpu.VMEM((8, 2, 256), full),
            pltpu.VMEM((8, 2, 256), full),
            pltpu.VMEM((8, 128, 256), full),
            pltpu.VMEM((1, 1024), jnp.int32),
            pltpu.VMEM((1, 256), jnp.int32),
            pltpu.VMEM((4, 1024), full),
            pltpu.VMEM((1024,), full),
            pltpu.VMEM((1024,), full),
            pltpu.VMEM((1024,), full),
            pltpu.VMEM((1024,), full),
            pltpu.SemaphoreType.DMA((20,)),
            pltpu.SemaphoreType.DMA((8,)),
            pltpu.SemaphoreType.DMA((8,)),
            pltpu.SemaphoreType.DMA((3, 8)),
            pltpu.SemaphoreType.DMA((3, 8)),
        ],
        compiler_params=pltpu.CompilerParams(
            collective_id=1, has_side_effects=True, vmem_limit_bytes=VMEM_BYTES
        ),
        name="forward",
    )(*operands)


def exchanger(core, partner, ex_send, ex_recv, ex_local):
    made = []

    def exchange(source, dest, cut=None):
        index = len(made)

        def part(owner):
            if cut is None:
                return source
            at, span = cut
            return source.at[:, pl.ds(pl.multiple_of(at + owner * span, 128), span)]

        made.append(
            (
                pltpu.make_async_copy(part(core), dest(0), ex_local.at[index]),
                pltpu.make_async_remote_copy(
                    src_ref=part(1 - core),
                    dst_ref=dest(1),
                    send_sem=ex_send.at[index],
                    recv_sem=ex_recv.at[index],
                    device_id=partner,
                    device_id_type=MESH,
                ),
            )
        )
        return made[-1]

    def whole(source, buf):
        return [exchange(source, lambda half: buf.at[pl.ds(256 * half, 256), :])]

    def halves(source, buf, span):
        return [
            exchange(
                source,
                lambda half, high=high: buf.at[pl.ds(256 * half, 256), pl.ds(high * span, span)],
                (high * 2 * span, span),
            )
            for high in (0, 1)
        ]

    return exchange, whole, halves, made


def begin(copies):
    for local, remote in copies:
        remote.start()
        local.start()


def arrived(copies):
    for local, remote in copies:
        local.wait()
        remote.wait_recv()


def turn_rows(buf, dest):
    turned = buf[...].astype(jnp.float32).T
    dest[...] = jnp.concatenate(
        [turned[8 * block : 8 * block + 8] for block in BLOCKS], axis=0
    ).astype(jnp.bfloat16)


def chunk_product(left, right_a, right_b):
    a = jnp.dot(left, right_a, preferred_element_type=jnp.float32)
    b = jnp.dot(left, right_b, preferred_element_type=jnp.float32)
    return jnp.concatenate((a.reshape(64, 8, 256), b.reshape(64, 8, 256)), axis=1).astype(
        jnp.bfloat16
    )


def wide_finish(dest, tile):
    def finish(total):
        dest[:, 512 * tile : 512 * tile + 256] = total[:8]
        dest[:, 512 * tile + 256 : 512 * tile + 512] = total[8:]

    return finish


HEADS, FAR, CLOSE, GP, PUT, ADV, THROUGH, NORM, ROWS, BIAS, ADVB, PIX, POST, GATT, MLP = range(15)
SCHEDULE = (
    (MLP, 0), (MLP, 1), (MLP, 2), (PUT, 8), (PUT, 9), (MLP, 3), (PUT, 10), (MLP, 4), (MLP, 5), (PUT, 11),
    (MLP, 6), (PUT, 12), (PUT, 13), (MLP, 7), (POST,), (ADV, 9, 0), (ADV, 8, 0), (GATT,), (ADV, 10, 0),
    (PUT, 2), (PUT, 0), (PUT, 14), (HEADS, 0), (ADV, 12, 0), (ADV, 9, 1), (ADV, 13, 0), (PUT, 4),
    (ADV, 10, 1), (ADV, 11, 0), (HEADS, 1), (FAR, 0), (ADV, 8, 1), (HEADS, 2), (FAR, 1), (ADV, 2, 0),
    (HEADS, 3), (FAR, 2), (GP, 0), (ADV, 3, 0), (ADV, 1, 0), (ADV, 0, 0), (ADV, 12, 1), (ADV, 9, 2),
    (PUT, 15), (ADV, 14, 0), (ADV, 8, 2), (PUT, 6), (CLOSE, 0), (HEADS, 4), (FAR, 3), (ADV, 4, 0),
    (CLOSE, 1), (ADV, 13, 1), (HEADS, 5), (FAR, 4), (ADV, 5, 0), (ADV, 3, 1), (ADV, 10, 2), (ADV, 2, 1),
    (HEADS, 6), (FAR, 5), (CLOSE, 2), (ADV, 14, 1), (ADV, 1, 1), (ADV, 11, 1), (HEADS, 7), (FAR, 6),
    (CLOSE, 3), (GP, 1), (GP, 2), (GP, 3), (ADV, 0, 1), (PUT, 17), (ADV, 15, 0), (ADV, 12, 2), (THROUGH, 0),
    (CLOSE, 4), (FAR, 7), (ADV, 9, 3), (THROUGH, 1), (ADV, 6, 0), (ADV, 8, 3), (PUT, 16), (THROUGH, 2),
    (ADV, 7, 0), (THROUGH, 3), (ADV, 4, 1), (ADV, 3, 2), (CLOSE, 5), (ADV, 10, 3), (ADV, 13, 2),
    (ADV, 5, 1), (ADV, 14, 2), (ADV, 1, 2), (ADV, 2, 2), (ADV, 11, 2), (PUT, 21), (CLOSE, 6), (ADV, 0, 2),
    (ADV, 12, 3), (PUT, 19), (ADV, 6, 1), (ADV, 9, 4), (ADV, 15, 1), (PUT, 20), (CLOSE, 7), (GP, 4),
    (GP, 5), (ADV, 5, 2), (THROUGH, 4), (ADV, 4, 2), (ADV, 8, 4), (ADV, 10, 4), (ADV, 11, 3), (ADV, 17, 0),
    (THROUGH, 5), (ADV, 0, 3), (ADV, 2, 3), (ADV, 1, 3), (NORM,), (ROWS,), (ADV, 7, 1), (ADV, 12, 4),
    (PUT, 23), (ADV, 15, 2), (PUT, 18), (ADV, 3, 3), (PUT, 22), (PIX,), (BIAS,), (ADV, 16, 0), (ADV, 14, 3),
    (ADV, 13, 3), (ADV, 4, 3), (ADV, 6, 2), (ADV, 0, 4), (ADV, 11, 4), (PUT, 27), (ADV, 7, 2), (ADV, 2, 4),
    (PUT, 29), (ADV, 19, 0), (PUT, 26), (ADV, 20, 0), (PUT, 28), (ADV, 9, 5), (ADV, 8, 5), (ADV, 5, 3),
    (ADV, 10, 5), (ADV, 12, 5), (PUT, 24), (PUT, 25), (ADV, 17, 1), (ADV, 1, 4), (ADV, 21, 0), (ADV, 15, 3),
    (ADV, 16, 1), (ADV, 3, 4), (ADV, 22, 0), (ADV, 23, 0), (ADV, 7, 3), (ADV, 14, 4), (ADV, 13, 4),
    (ADVB, 0), (ADV, 18, 0), (ADV, 4, 4), (ADV, 11, 5), (ADV, 2, 5), (ADV, 6, 3), (ADV, 0, 5), (ADV, 27, 0),
    (ADV, 29, 0), (ADV, 25, 0), (ADV, 26, 0), (ADV, 1, 5), (ADV, 4, 5), (ADV, 28, 0), (ADV, 21, 1),
    (ADV, 3, 5), (ADV, 5, 4), (ADV, 24, 0), (ADV, 7, 4), (ADV, 15, 4), (ADV, 19, 1), (ADV, 20, 1),
    (ADV, 6, 4), (ADV, 16, 2), (ADV, 17, 2), (ADV, 13, 5), (ADV, 27, 1), (ADV, 23, 1), (ADV, 14, 5),
    (ADV, 29, 1), (ADVB, 1), (ADV, 22, 1), (ADV, 26, 1), (ADV, 5, 5), (ADV, 15, 5), (ADV, 24, 1),
    (ADV, 21, 2), (ADV, 18, 1), (ADV, 25, 1), (ADV, 16, 3), (ADV, 7, 5), (ADV, 28, 1), (ADV, 27, 2),
    (ADV, 29, 2), (ADV, 19, 2), (ADV, 20, 2), (ADV, 6, 5), (ADV, 23, 2), (ADV, 17, 3), (ADV, 22, 2),
    (ADVB, 2), (ADV, 21, 3), (ADV, 26, 2), (ADV, 24, 2), (ADV, 16, 4), (ADV, 25, 2), (ADV, 18, 2),
    (ADV, 28, 2), (ADV, 19, 3), (ADV, 29, 3), (ADV, 20, 3), (ADV, 27, 3), (ADV, 17, 4), (ADV, 23, 3),
    (ADV, 22, 3), (ADVB, 3), (ADV, 21, 4), (ADV, 26, 3), (ADV, 16, 5), (ADV, 24, 3), (ADV, 25, 3),
    (ADV, 18, 3), (ADV, 19, 4), (ADV, 29, 4), (ADV, 28, 3), (ADV, 20, 4), (ADV, 17, 5), (ADV, 27, 4),
    (ADV, 23, 4), (ADV, 22, 4), (ADVB, 4), (ADV, 21, 5), (ADV, 26, 4), (ADV, 24, 4), (ADV, 25, 4),
    (ADV, 19, 5), (ADV, 29, 5), (ADV, 18, 4), (ADV, 20, 5), (ADV, 28, 4), (ADV, 27, 5), (ADV, 23, 5),
    (ADV, 22, 5), (ADVB, 5), (ADV, 26, 5), (ADV, 24, 5), (ADV, 25, 5), (ADV, 18, 5), (ADV, 28, 5),
)


CHUNKS = 30


def backward_kernel(
    att_in, stream_in, cot_in, hot_in, mask_in, q_in, kv_in, lse_in, n1_in, pix_in,
    gain1_in, gain2_in, bias2_in, out_bias_in, fc1_bias_in, fc2_bias_in, emb_in, qkv_in, ow_in, fc1_in, fc2_in,
    block_out, pix_out, emb_out, qkv_out, out_out, fc1_out, fc2_out, bias_out,
    x_buf, hid, hid_come, gbr_buf, gpre_buf, gout_buf, gp_buf, pix_buf, hot_buf, row_buf, lanes, sums,
    xt_buf, xht_buf, work, arrive, work_end, arrive_end, work_f, arrive_f, work_end_f, arrive_end_f,
    q_pairs, kv, gatt, mask, near_send, near_come, far_send, far_come, held, far_held, whole_grad,
    n2, stream, middle, acc, grown_buf, gs, pix_grad, tall, wide,
    lse, gain1, gain2, bias2, out_bias, fc1_bias, fc2_bias,
    ex_send, ex_recv, ex_local, send_sem, recv_sem, credit, send_f, recv_f, load_sem, kv_sem, tall_sem, wide_sem,
    kv_send_sem, kv_recv_sem, kv_credit, gp_send, gp_recv, pre_send, pre_recv, tok_send, tok_recv,
):
    where = place()
    x_hi, core, x_lo, y, z = where
    near = neighbours(where)
    bits = own_bits(where)
    partner = near["core"]
    across = ((1 - x_hi) * 2 + core, x_lo * 16 + y * 4 + z)

    def kv_load(pair):
        return pltpu.make_async_copy(kv_in.at[pair], kv.at[pair % 2], kv_sem.at[pair % 2])

    order = (0, 1, 2, 4, 3, 5)

    def tall_load(index):
        if index < 8:
            source = fc1_in.at[:, pl.ds(512 * index, 512)]
        else:
            source = qkv_in.at[:, pl.ds(512 * order[index - 8], 512)]
        return pltpu.make_async_copy(source, tall.at[index % 3], tall_sem.at[index % 3])

    def wide_load(index):
        if index < 2 or index in (10, 11):
            source = ow_in.at[pl.ds(512 * (index % 2), 512), :]
        elif index < 10:
            source = fc2_in.at[pl.ds(512 * (index - 2), 512), :]
        else:
            source = emb_in.at[pl.ds(512 * (index - 12), 512), :]
        return pltpu.make_async_copy(source, wide.at[index % 3], wide_sem.at[index % 3])

    def used(load, index, last):
        if index + 3 < last:
            load(index + 3).start()

    loads = []
    for source, dest in (
        (att_in, n2), (stream_in, stream), (hot_in, hot_buf.at[pl.ds(0, 256), :]), (cot_in, gs),
        (gain1_in, gain1), (gain2_in, gain2), (bias2_in, bias2), (out_bias_in, out_bias),
        (fc1_bias_in, fc1_bias), (fc2_bias_in, fc2_bias), (lse_in, lse), (q_in, q_pairs), (mask_in, mask),
    ):
        loads.append(pltpu.make_async_copy(source, dest, load_sem.at[len(loads)]))
    loads[0].start()
    for index in range(2):
        wide_load(index).start()
    for copy in loads[1:10]:
        copy.start()
    wide_load(2).start()
    for index in range(3):
        tall_load(index).start()
    for copy in loads[10:]:
        copy.start()
    for pair in range(2):
        kv_load(pair).start()
    targets = tuple(near.values()) + (across,)
    barrier = pltpu.get_barrier_semaphore()
    for target in targets:
        pl.semaphore_signal(barrier, inc=1, device_id=target, device_id_type=MESH)

    put, advance, drain = reducer(
        near, bits, chunk_dims, (work, arrive, work_end, arrive_end), send_sem, recv_sem, credit, CHUNKS
    )
    put_f, advance_f, drain_f = reducer(
        near, bits, lambda chunk: ROTATION, (work_f, arrive_f, work_end_f, arrive_end_f),
        send_f, recv_f, None, 1,
    )
    exchange, whole, halves, made = exchanger(core, partner, ex_send, ex_recv, ex_local)
    groups = {
        "fc1": halves(n2, x_buf.at[0], 256),
        "out": halves(att_in, x_buf.at[1], 256),
        "qkv": halves(n1_in, x_buf.at[2], 256),
        "side": whole(pix_in, pix_buf),
        "emb": halves(gs, x_buf.at[0], 256),
        "rows": [exchange(lanes.at[pl.ds(0, 16), :], lambda half: row_buf.at[half])],
    }

    def mirror(buf, index, span=slice(None)):
        return pltpu.make_async_remote_copy(
            src_ref=buf.at[pl.ds(0, 256), span],
            dst_ref=buf.at[pl.ds(256, 256), span],
            send_sem=tok_send.at[index],
            recv_sem=tok_recv.at[index],
            device_id=partner,
            device_id_type=MESH,
        )

    def gout_copy():
        return mirror(gout_buf, 0)

    def gbr_copy():
        return mirror(gbr_buf, 1)

    def hot_copy():
        return mirror(hot_buf, 2)

    def hid_copy(high):
        return pltpu.make_async_remote_copy(
            src_ref=hid.at[1 - core, :, pl.ds(1024 * high, 1024)],
            dst_ref=hid_come.at[:, pl.ds(1024 * high, 1024)],
            send_sem=tok_send.at[3 + high],
            recv_sem=tok_recv.at[3 + high],
            device_id=partner,
            device_id_type=MESH,
        )

    def gpre_copy(tile):
        span = pl.ds(512 * tile, 512)
        return pltpu.make_async_remote_copy(
            src_ref=gpre_buf.at[pl.ds(0, 256), span],
            dst_ref=gpre_buf.at[pl.ds(256, 256), span],
            send_sem=pre_send.at[tile],
            recv_sem=pre_recv.at[tile],
            device_id=partner,
            device_id_type=MESH,
        )

    def gp_copy(index):
        span = pl.ds(512 * order[index], 512)
        return pltpu.make_async_remote_copy(
            src_ref=gp_buf.at[pl.ds(0, 256), span],
            dst_ref=gp_buf.at[pl.ds(256, 256), span],
            send_sem=gp_send.at[index],
            recv_sem=gp_recv.at[index],
            device_id=partner,
            device_id_type=MESH,
        )

    plan = [("fc2", tile) for tile in range(8)] + [("fc1", tile) for tile in range(8)]
    plan += [("out", tile) for tile in range(2)] + [("qkv", index) for index in range(6)]
    plan += [("emb", tile) for tile in range(6)]
    turned_from = {"fc1": 0, "out": 1, "qkv": 2, "emb": 0}
    ready = set()

    def band_pixels(tile):
        band, at = tile // 3, tile % 3
        picked = pix_buf[:, 256 * at : 256 * at + 256].astype(jnp.float32)
        return (picked * hot_buf[:, band : band + 1]).astype(jnp.bfloat16)

    def turn_wide(buf, at):
        turned = buf[...].astype(jnp.float32).T.astype(jnp.bfloat16)
        xht_buf[:, at : at + 256] = jnp.concatenate(
            [turned[32 * block : 32 * block + 32] for block in BLOCKS], axis=0
        )

    def compute(chunk):
        name, tile = plan[chunk]
        if name not in ready:
            ready.add(name)
            if name == "fc2":
                turn_wide(hid.at[core], 0)
                for high in (0, 1):
                    hid_copy(high).wait_recv()
                turn_wide(hid_come, 256)
                gout_copy().wait_recv()
            else:
                arrived(groups[name])
                if name == "out":
                    gbr_copy().wait_recv()
                turn_rows(x_buf.at[turned_from[name]], xt_buf)
        if name == "fc2":
            if tile % 2 == 0:
                both = jnp.dot(
                    xht_buf[...],
                    gout_buf[:, 128 * tile : 128 * tile + 256],
                    preferred_element_type=jnp.float32,
                ).reshape(64, 32, 256)
                put(chunk, both[:, :16].astype(jnp.bfloat16))
                put(chunk + 1, both[:, 16:].astype(jnp.bfloat16))
            return
        if name == "emb":
            right = (band_pixels(2 * tile), band_pixels(2 * tile + 1))
        else:
            if name == "qkv":
                gp_copy(tile).wait_recv()
                tile = order[tile]
            if name == "fc1":
                gpre_copy(tile).wait_recv()
            buf = {"fc1": gpre_buf, "out": gbr_buf, "qkv": gp_buf}[name]
            right = (
                buf[:, 512 * tile : 512 * tile + 256],
                buf[:, 512 * tile + 256 : 512 * tile + 512],
            )
        put(chunk, chunk_product(xt_buf[...], *right))

    def finisher(chunk):
        name, tile = plan[chunk]
        if name == "fc2":

            def finish(total):
                at = 16 * (tile % 2)
                fc2_out[at : at + 16, 128 * (tile - tile % 2) : 128 * (tile - tile % 2) + 256] = total

            return finish
        if name == "qkv":
            tile = order[tile]
        return wide_finish({"fc1": fc1_out, "out": out_out, "qkv": qkv_out, "emb": emb_out}[name], tile)

    def wave(index):
        for chunk in range(6 * index, 6 * index + 6):
            compute(chunk)

    def step_wave(*pairs):
        for index, step in pairs:
            for chunk in range(6 * index, 6 * index + 6):
                advance(chunk, step, finisher(chunk))

    def block_at(high, low):
        return pl.ds(pl.multiple_of((high * 2 + low) * 256, 256), 256)

    def near_copy(pair):
        return pltpu.make_async_remote_copy(
            src_ref=near_send.at[pair % 2],
            dst_ref=near_come.at[pair % 4],
            send_sem=kv_send_sem.at[0, pair],
            recv_sem=kv_recv_sem.at[0, pair],
            device_id=partner,
            device_id_type=MESH,
        )

    def far_copy(pair):
        return pltpu.make_async_remote_copy(
            src_ref=far_send.at[pair % 2],
            dst_ref=far_come.at[pair],
            send_sem=kv_send_sem.at[1, pair],
            recv_sem=kv_recv_sem.at[1, pair],
            device_id=across,
            device_id_type=MESH,
        )

    def heads_back(pair):
        slot = pair % 2
        kv_load(pair).wait()
        at = lax.broadcasted_iota(jnp.int32, (128, 256), 0)
        lane = lax.broadcasted_iota(jnp.int32, (256, 128), 1)
        query = q_pairs[pair].astype(jnp.float32)
        grad = gatt[pair].astype(jnp.float32)
        query_t, grad_t = query.T, grad.T
        key_rows = kv[slot, 0].T
        key_grad = value_grad = None
        query_grads = []
        for head in (0, 1):
            own = (at < 64) if head == 0 else (at >= 64)
            mine = (lane < 64) if head == 0 else (lane >= 64)
            scores = (
                jnp.dot(
                    kv[slot, 0],
                    jnp.where(own, query_t, 0.0).astype(jnp.bfloat16),
                    preferred_element_type=jnp.float32,
                )
                + mask[...]
            )
            probs = jnp.exp(scores - lse[pair, head : head + 1, :])
            prob_grad = jnp.dot(
                kv[slot, 1],
                jnp.where(own, grad_t, 0.0).astype(jnp.bfloat16),
                preferred_element_type=jnp.float32,
            )
            mean = jnp.sum(probs * prob_grad, axis=0, keepdims=True)
            score_grad = (probs * (prob_grad - mean)).astype(jnp.bfloat16)
            query_grads.append(
                jnp.dot(
                    key_rows[64 * head : 64 * head + 64],
                    score_grad,
                    preferred_element_type=jnp.float32,
                )
            )
            key_part = jnp.dot(
                score_grad,
                jnp.where(mine, query, 0.0).astype(jnp.bfloat16),
                preferred_element_type=jnp.float32,
            )
            value_part = jnp.dot(
                probs.astype(jnp.bfloat16),
                jnp.where(mine, grad, 0.0).astype(jnp.bfloat16),
                preferred_element_type=jnp.float32,
            )
            key_grad = key_part if head == 0 else key_grad + key_part
            value_grad = value_part if head == 0 else value_grad + value_part
        if pair + 2 < 8:
            kv_load(pair + 2).start()
        if pair >= 2:
            near_copy(pair - 2).wait_send()
        gp_buf[0:256, 128 * pair : 128 * pair + 128] = (
            jnp.concatenate(query_grads, axis=0).T * HD ** (-0.5)
        ).astype(jnp.bfloat16)
        whole_grad[0] = key_grad
        whole_grad[1] = value_grad
        for kind in (0, 1):
            near_send[pair % 2, 0, kind] = whole_grad[kind, block_at(x_hi, 1 - core), :].astype(
                jnp.bfloat16
            )
            near_send[pair % 2, 1, kind] = whole_grad[kind, block_at(1 - x_hi, 1 - core), :].astype(
                jnp.bfloat16
            )
        if pair >= 4:
            pl.semaphore_wait(kv_credit.at[pair - 4], 1)
        near_copy(pair).start()
        for kind in (0, 1):
            held[pair % 2, kind] = whole_grad[kind, block_at(x_hi, core), :]
            far_held[pair % 2, kind] = whole_grad[kind, block_at(1 - x_hi, core), :]

    def pass_far(pair):
        near_copy(pair).wait_recv()
        if pair >= 2:
            far_copy(pair - 2).wait_send()
        for kind in (0, 1):
            far_send[pair % 2, kind] = (
                far_held[pair % 2, kind] + near_come[pair % 4, 1, kind].astype(jnp.float32)
            ).astype(jnp.bfloat16)
        far_copy(pair).start()
        for kind in (0, 1):
            at = 1024 * (kind + 1) + 128 * pair
            gp_buf[0:256, at : at + 128] = (
                held[pair % 2, kind] + near_come[pair % 4, 0, kind].astype(jnp.float32)
            ).astype(jnp.bfloat16)
        if pair < 4:
            pl.semaphore_signal(
                kv_credit.at[pair], inc=1, device_id=partner, device_id_type=MESH
            )

    def close(pair):
        far_copy(pair).wait_recv()
        for kind in (0, 1):
            at = 1024 * (kind + 1) + 128 * pair
            gp_buf[0:256, at : at + 128] = (
                gp_buf[0:256, at : at + 128].astype(jnp.float32)
                + far_come[pair, kind].astype(jnp.float32)
            ).astype(jnp.bfloat16)

    def through_qkv(index):
        tall_load(8 + index).wait()
        tile = order[index]
        part = nt_dot(gp_buf[0:256, 512 * tile : 512 * tile + 512], tall[(8 + index) % 3])
        grown_buf[...] = part if index == 0 else grown_buf[...] + part
        used(tall_load, 8 + index, 14)

    for copy in loads[:3] + loads[4:10]:
        copy.wait()
    total = stream[...] + row(out_bias)
    for index in (0, 1):
        wide_load(index).wait()
        total = total + jnp.dot(
            n2[:, 512 * index : 512 * index + 512], wide[index], preferred_element_type=jnp.float32
        )
        used(wide_load, index, 18)
    middle[...] = total
    hat, _ = norm_parts(total)
    n2[...] = (hat * row(gain2) + row(bias2)).astype(jnp.bfloat16)
    pl.semaphore_wait(barrier, len(targets))
    begin(groups["fc1"])
    hot_copy().start()
    for name in ("out", "qkv", "side"):
        begin(groups[name])
    loads[3].wait()
    gout_buf[0:256, :] = (gs[...].astype(jnp.float32) * hot_buf[0:256, 4:5]).astype(jnp.bfloat16)
    gout_copy().start()
    def mlp_tile(tile):
        span = slice(512 * tile, 512 * tile + 512)
        tall_load(tile).wait()
        wide_load(2 + tile).wait()
        pre = jnp.dot(n2[...], tall[tile % 3], preferred_element_type=jnp.float32) + fc1_bias[
            span
        ].reshape(1, 512)
        cdf = 0.5 * (1.0 + lax.erf(pre * (0.5**0.5)))
        hidden = (pre * cdf).astype(jnp.bfloat16)
        at = 1024 * (tile // 4) + 512 * (tile % 2)
        hid[(tile // 2) % 2, :, at : at + 512] = hidden
        slope = cdf + pre * (jnp.exp(-0.5 * pre * pre) * 0.3989422804014327)
        back = (nt_dot(gout_buf[0:256, :], wide[(2 + tile) % 3]) * slope).astype(jnp.bfloat16)
        gpre_buf[0:256, span] = back
        gpre_copy(tile).start()
        ahead = jnp.dot(hidden, wide[(2 + tile) % 3], preferred_element_type=jnp.float32)
        used(wide_load, 2 + tile, 18)
        behind = nt_dot(back, tall[tile % 3])
        used(tall_load, tile, 14)
        acc[...] = ahead if tile == 0 else acc[...] + ahead
        grown_buf[...] = behind if tile == 0 else grown_buf[...] + behind
        quarter, at = tile // 2, 512 * (tile % 2)
        sums[4 + quarter : 5 + quarter, at : at + 512] = jnp.sum(
            back.astype(jnp.float32), axis=0, keepdims=True
        )
        if tile % 4 == 3:
            hid_copy(tile // 4).start()

    block_copy = pltpu.make_async_copy(gs, block_out, load_sem.at[13])

    def mlp_back():
        gs[...] = (
            hot_buf[0:256, 4:5] * (middle[...] + (acc[...] + row(fc2_bias)))
        ).astype(jnp.bfloat16)
        block_copy.start()
        upstream = gout_buf[0:256, :].astype(jnp.float32)
        sums[3:4, :] = jnp.sum(upstream, axis=0, keepdims=True)
        grown = grown_buf[...]
        hat, scale = norm_parts(middle[...])
        sums[1:2, :] = jnp.sum(grown * hat, axis=0, keepdims=True)
        sums[2:3, :] = jnp.sum(grown, axis=0, keepdims=True)
        grown = grown * row(gain2)
        middle[...] = upstream + scale * (
            grown
            - jnp.mean(grown, axis=-1, keepdims=True)
            - hat * jnp.mean(grown * hat, axis=-1, keepdims=True)
        )
        gbr_buf[0:256, :] = middle[...].astype(jnp.bfloat16)
        gbr_copy().start()
        sums[0:1, :] = jnp.sum(gbr_buf[0:256, :].astype(jnp.float32), axis=0, keepdims=True)

    def attention_grad():
        for index in (0, 1):
            wide_load(10 + index).wait()
            back = nt_dot(gbr_buf[0:256, :], wide[(10 + index) % 3]).astype(jnp.bfloat16)
            used(wide_load, 10 + index, 18)
            for pair in range(4):
                gatt[4 * index + pair] = back[:, 128 * pair : 128 * pair + 128]

    def norm_back():
        block_copy.wait()
        grown = grown_buf[...]
        hat, scale = norm_parts(stream[...])
        lanes[...] = jnp.zeros_like(lanes)
        lanes[4:5, :] = jnp.sum(grown * hat, axis=0, keepdims=True)
        lanes[5:6, :] = jnp.sum(grown, axis=0, keepdims=True)
        grown = grown * row(gain1)
        gs[...] = (
            middle[...]
            + scale
            * (
                grown
                - jnp.mean(grown, axis=-1, keepdims=True)
                - hat * jnp.mean(grown * hat, axis=-1, keepdims=True)
            )
        ).astype(jnp.bfloat16)
        begin(groups["emb"])
        arrived(groups["side"])
        hot_copy().wait_recv()

    def side_rows():
        lanes[6:7, :] = jnp.sum(gp_buf[0:256, 0:1024].astype(jnp.float32), axis=0, keepdims=True)
        lanes[7:8, :] = jnp.sum(gp_buf[0:256, 2048:3072].astype(jnp.float32), axis=0, keepdims=True)
        lanes[0:4, :] = tn_dot(hot_buf[0:256, :].astype(jnp.bfloat16), gs[...])[0:4]
        lanes[8:16, :] = sums[...]
        begin(groups["rows"])

    def bias_chunk():
        arrived(groups["rows"])
        groups["rows"][0][1].wait_send()
        lanes[0:16, :] = row_buf[0] + row_buf[1]
        halves_t = [
            lanes[:, pl.ds(pl.multiple_of(high * 512 + core * 256, 128), 256)].T.reshape(32, 8, 128)
            for high in (0, 1)
        ]
        lane = lax.broadcasted_iota(jnp.int32, (32, 8, 128), 2)
        quarters = lanes[...].T.reshape(32, 4, 8, 128)
        for high in (0, 1):
            wide = jnp.where(lane < 12, halves_t[high], 0.0)
            for part in range(4):
                here = jnp.where(
                    core == 0,
                    quarters[:, part, :, 12 + 2 * high : 13 + 2 * high],
                    quarters[:, part, :, 13 + 2 * high : 14 + 2 * high],
                )
                wide = wide + jnp.where(lane == 12 + part, here, 0.0)
            halves_t[high] = wide
        turned = jnp.concatenate(halves_t, axis=0)
        put_f(0, jnp.concatenate([turned[b : b + 1] for b in BLOCKS], axis=0))

    out = pltpu.make_async_copy(pix_grad, pix_out, load_sem.at[14])

    def pixels_back():
        parts = [None] * 3
        for index in range(6):
            wide_load(12 + index).wait()
            for side in (0, 1):
                band, third = divmod(2 * index + side, 3)
                term = hot_buf[0:256, band : band + 1] * nt_dot(
                    gs[...], wide[(12 + index) % 3, 256 * side : 256 * side + 256, :]
                )
                parts[third] = term if parts[third] is None else parts[third] + term
            used(wide_load, 12 + index, 18)
        for third in range(3):
            pix_grad[:, 256 * third : 256 * third + 256] = parts[third].astype(jnp.bfloat16)
        out.start()

    def finish_bias(total):
        bias_out[...] = total

    actions = {
        HEADS: heads_back,
        FAR: pass_far,
        CLOSE: close,
        GP: lambda index: gp_copy(index).start(),
        PUT: compute,
        ADV: lambda chunk, step: advance(chunk, step, finisher(chunk)),
        THROUGH: through_qkv,
        NORM: norm_back,
        ROWS: side_rows,
        BIAS: bias_chunk,
        ADVB: lambda step: advance_f(0, step, finish_bias),
        PIX: pixels_back,
        MLP: mlp_tile,
        POST: mlp_back,
        GATT: attention_grad,
    }
    for name, *where_at in SCHEDULE:
        if (name, *where_at) == (HEADS, 0):
            for copy in loads[10:]:
                copy.wait()
        actions[name](*where_at)
    out.wait()
    for _, remote in made[:-1]:
        remote.wait_send()
    for pair in range(8):
        if pair >= 6:
            near_copy(pair).wait_send()
            far_copy(pair).wait_send()
    for index in range(6):
        gp_copy(index).wait_send()
    for tile in range(8):
        gpre_copy(tile).wait_send()
    for copy in (gout_copy(), gbr_copy(), hot_copy(), hid_copy(0), hid_copy(1)):
        copy.wait_send()
    for chunk in range(CHUNKS):
        drain(chunk)
    drain_f(0)


def backward(*operands):
    any_space = pl.BlockSpec(memory_space=pl.ANY)
    in_vmem = pl.BlockSpec(memory_space=pltpu.VMEM)
    half, full = jnp.bfloat16, jnp.float32
    shape = jax.ShapeDtypeStruct
    dma = pltpu.SemaphoreType.DMA
    return pl.pallas_call(
        backward_kernel,
        out_shape=(
            shape((256, 1024), half),
            shape((256, 768), half),
            shape((8, 3072), full),
            shape((8, 3072), full),
            shape((8, 1024), full),
            shape((8, 4096), full),
            shape((32, 1024), full),
            shape((8, 128), full),
        ),
        in_specs=[any_space] * 21,
        out_specs=(any_space,) * 2 + (in_vmem,) * 6,
        scratch_shapes=[
            pltpu.VMEM((3, 512, 512), half),
            pltpu.VMEM((2, 256, 2048), half),
            pltpu.VMEM((256, 2048), half),
            pltpu.VMEM((512, 1024), half),
            pltpu.VMEM((512, 4096), half),
            pltpu.VMEM((512, 1024), half),
            pltpu.VMEM((512, 3072), half),
            pltpu.VMEM((512, 768), half),
            pltpu.VMEM((512, 128), full),
            pltpu.VMEM((2, 16, 1024), full),
            pltpu.VMEM((128, 1024), full),
            pltpu.VMEM((8, 1024), full),
            pltpu.VMEM((512, 512), half),
            pltpu.VMEM((2048, 512), half),
            pltpu.VMEM((SLOTS, 64, 16, 256), half),
            pltpu.VMEM((SLOTS, 56, 16, 256), half),
            pltpu.VMEM((CHUNKS, 14, 16, 256), half),
            pltpu.VMEM((CHUNKS, 7, 16, 256), half),
            pltpu.VMEM((1, 64, 8, 128), full),
            pltpu.VMEM((1, 56, 8, 128), full),
            pltpu.VMEM((1, 14, 8, 128), full),
            pltpu.VMEM((1, 7, 8, 128), full),
            pltpu.VMEM((8, 256, 128), half),
            pltpu.VMEM((2, 2, 1024, 128), half),
            pltpu.VMEM((8, 256, 128), half),
            pltpu.VMEM((1024, 256), full),
            pltpu.VMEM((2, 2, 2, 256, 128), half),
            pltpu.VMEM((4, 2, 2, 256, 128), half),
            pltpu.VMEM((2, 2, 256, 128), half),
            pltpu.VMEM((8, 2, 256, 128), half),
            pltpu.VMEM((2, 2, 256, 128), full),
            pltpu.VMEM((2, 2, 256, 128), full),
            pltpu.VMEM((2, 1024, 128), full),
            pltpu.VMEM((256, 1024), half),
            pltpu.VMEM((256, 1024), full),
            pltpu.VMEM((256, 1024), full),
            pltpu.VMEM((256, 1024), full),
            pltpu.VMEM((256, 1024), full),
            pltpu.VMEM((256, 1024), half),
            pltpu.VMEM((256, 768), half),
            pltpu.VMEM((3, 1024, 512), half),
            pltpu.VMEM((3, 512, 1024), half),
            pltpu.VMEM((8, 2, 256), full),
            pltpu.VMEM((1024,), full),
            pltpu.VMEM((1024,), full),
            pltpu.VMEM((1024,), full),
            pltpu.VMEM((1024,), full),
            pltpu.VMEM((4096,), full),
            pltpu.VMEM((1024,), full),
            dma((10,)),
            dma((10,)),
            dma((10,)),
            dma((CHUNKS, 6)),
            dma((CHUNKS, 6)),
            pltpu.SemaphoreType.REGULAR((CHUNKS - SLOTS, 3)),
            dma((1, 6)),
            dma((1, 6)),
            dma((15,)),
            dma((2,)),
            dma((3,)),
            dma((3,)),
            dma((2, 8)),
            dma((2, 8)),
            pltpu.SemaphoreType.REGULAR((4,)),
            dma((6,)),
            dma((6,)),
            dma((8,)),
            dma((8,)),
            dma((5,)),
            dma((5,)),
        ],
        compiler_params=pltpu.CompilerParams(
            collective_id=2, has_side_effects=True, vmem_limit_bytes=VMEM_BYTES
        ),
        name="backward",
    )(*operands)


def finish_kernel(*refs):
    sources, dests, bufs = refs[:8], refs[8:25], refs[25:33]
    cols, bands, flat, in_sem, out_sem = refs[33:]
    loads = []
    for source, buf in zip(sources, bufs):
        loads.append(pltpu.make_async_copy(source, buf, in_sem.at[len(loads)]))
    for copy in reversed(loads):
        copy.start()
    stores = []

    def store(source, dest):
        stores.append(pltpu.make_async_copy(source, dest, out_sem.at[len(stores)]))
        stores[-1].start()

    loads[7].wait()
    sums = bufs[7][...]
    cols[...] = sums.T[0:16, :]
    for index in range(8):
        store(cols.at[pl.ds(4 + index, 1), :], dests[8 + index])
    bands[...] = cols[0:4, :]
    store(bands, dests[7])
    lane = lax.broadcasted_iota(jnp.int32, (8, 128), 1)
    wide = jnp.zeros((8, 128), jnp.float32)
    for part in range(4):
        wide = wide + jnp.where(lane // 8 == part, sums[:, 12 + part : 13 + part], 0.0)
    wide = jnp.where(lane % 8 == lax.broadcasted_iota(jnp.int32, (8, 128), 0), wide, 0.0)
    flat[...] = jnp.sum(wide, axis=0, keepdims=True)[:, 0:32]
    store(flat, dests[16])
    for index in range(7):
        loads[index].wait()
        if index < 6:
            store(bufs[index], dests[index])
    for band in range(4):
        store(bufs[6].at[:, pl.ds(768 * band, 768)], dests[6].at[band])
    for copy in stores:
        copy.wait()


def finish(*operands):
    any_space = pl.BlockSpec(memory_space=pl.ANY)
    full = jnp.float32
    shape = jax.ShapeDtypeStruct
    return pl.pallas_call(
        finish_kernel,
        out_shape=tuple(shape(array.shape, array.dtype) for array in operands[:6])
        + (shape((4, 8, 768), full), shape((4, 8), full))
        + (shape((1, 8), full),) * 8
        + (shape((1, 32), full),),
        in_specs=[any_space] * 8,
        out_specs=(any_space,) * 17,
        scratch_shapes=[pltpu.VMEM(array.shape, array.dtype) for array in operands]
        + [
            pltpu.VMEM((16, 8), full),
            pltpu.VMEM((4, 8), full),
            pltpu.VMEM((1, 32), full),
            pltpu.SemaphoreType.DMA((8,)),
            pltpu.SemaphoreType.DMA((20,)),
        ],
        compiler_params=pltpu.CompilerParams(vmem_limit_bytes=VMEM_BYTES),
        name="finish",
    )(*operands)


def on_device(
    pixels,
    positions,
    segments,
    groups,
    cotangent,
    emb_weight,
    emb_bias,
    norm1_gain,
    norm1_bias,
    qkv_weight,
    query_bias,
    value_bias,
    out_weight,
    out_bias,
    norm2_gain,
    norm2_bias,
    fc1_weight,
    fc1_bias,
    fc2_weight,
    fc2_bias,
):
    rows_dev, slice_len, pix_len = pixels.shape
    model_width = qkv_weight.shape[0]
    band_count = emb_weight.shape[0]
    tok_count = rows_dev * slice_len
    flat_pixels = pixels.reshape(tok_count, pix_len)
    flat_emb = emb_weight.reshape(band_count * pix_len, model_width)
    hot_live, mask, stream, normed_one, query_pairs, key_value, log_sums, attended = forward(
        flat_pixels,
        positions.reshape(tok_count, model_width),
        segments,
        groups,
        emb_bias,
        norm1_gain,
        norm1_bias,
        query_bias,
        value_bias,
        flat_emb,
        qkv_weight,
    )
    block_out, pixel_grad, emb_sum, qkv_sum, out_sum, fc1_sum, fc2_sum, bias_sum = backward(
        attended,
        stream,
        cotangent.reshape(tok_count, model_width),
        hot_live,
        mask,
        query_pairs,
        key_value,
        log_sums,
        normed_one,
        flat_pixels,
        norm1_gain,
        norm2_gain,
        norm2_bias,
        out_bias,
        fc1_bias,
        fc2_bias,
        flat_emb,
        qkv_weight,
        out_weight,
        fc1_weight,
        fc2_weight,
    )
    block_out, pixel_grad, qkv_sum, out_sum, fc1_sum, fc2_sum, emb_sum, *rest = finish(
        block_out, pixel_grad, qkv_sum, out_sum, fc1_sum, fc2_sum, emb_sum, bias_sum
    )
    emb_bias_sum, gain1, bias1, query, value, out, gain2, bias2, last, wide = (
        part if index == 0 else part.reshape(-1) for index, part in enumerate(rest)
    )
    return (
        block_out.reshape(rows_dev, slice_len, model_width),
        pixel_grad.reshape(rows_dev, slice_len, pix_len),
        jnp.swapaxes(emb_sum, 1, 2),
        emb_bias_sum,
        gain1,
        bias1,
        qkv_sum,
        query,
        value,
        out_sum,
        out,
        gain2,
        bias2,
        fc1_sum,
        wide,
        fc2_sum,
        last,
    )


def solution(mesh):
    return jax.shard_map(
        on_device,
        mesh=mesh,
        in_specs=(
            P("batch", "blk", None),
            P("batch", "blk", None),
            P("batch", None),
            P("batch", "blk"),
            P("batch", "blk", None),
            P(),
            P(),
            P(),
            P(),
            P(),
            P(),
            P(),
            P(),
            P(),
            P(),
            P(),
            P(),
            P(),
            P(),
            P(),
        ),
        out_specs=(
            P("batch", "blk", None),
            P("batch", "blk", None),
            P(None, None, ("blk", "batch")),
            P(None, ("blk", "batch")),
            P(("blk", "batch")),
            P(("blk", "batch")),
            P(("blk", "batch"), None),
            P(("blk", "batch")),
            P(("blk", "batch")),
            P(("blk", "batch"), None),
            P(("blk", "batch")),
            P(("blk", "batch")),
            P(("blk", "batch")),
            P(("blk", "batch"), None),
            P(("blk", "batch")),
            P(("blk", "batch"), None),
            P(("blk", "batch")),
        ),
        check_vma=False,
    )
```

```python
import jax
import jax.numpy as jnp
from jax import lax
from jax.experimental import pallas as pl
from jax.experimental.pallas import tpu as pltpu
from jax.sharding import PartitionSpec as P

HD = 64
NORM_EPS = 1e-06
MASKED = -1e30
VMEM_BYTES = 64 << 20

MESH = pl.DeviceIdType.MESH
AXES = ("xb", "xa", "yb", "ya", "zb", "za")
ROTATION = ("xa", "ya", "za", "xb", "yb", "zb")
GRAY = (0, 1, 3, 2)
BLOCKS = tuple(16 * x + 4 * y + z for x in GRAY for y in GRAY for z in GRAY)


def place():
    blk = lax.axis_index("blk")
    batch = lax.axis_index("batch")
    return blk // 2, blk % 2, batch // 16, (batch // 4) % 4, batch % 4


def neighbours(where):
    x_hi, core, x_lo, y, z = where

    def device(x_hi, core, x_lo, y, z):
        return (x_hi * 2 + core, x_lo * 16 + y * 4 + z)

    return {
        "core": device(x_hi, 1 - core, x_lo, y, z),
        "xa": device(x_hi, core, 1 - x_lo, y, z),
        "xb": device(1 - x_hi, core, 1 - x_lo, y, z),
        "ya": device(x_hi, core, x_lo, y + 1 - 2 * (y % 2), z),
        "yb": device(x_hi, core, x_lo, 3 - y, z),
        "za": device(x_hi, core, x_lo, y, z + 1 - 2 * (z % 2)),
        "zb": device(x_hi, core, x_lo, y, 3 - z),
    }


def own_bits(where):
    x_hi, _, x_lo, y, z = where
    return {
        "xb": x_hi,
        "xa": (x_hi + x_lo) % 2,
        "yb": y // 2,
        "ya": (y // 2 + y) % 2,
        "zb": z // 2,
        "za": (z // 2 + z) % 2,
    }


DIMS = (
    (3, 5, 1, 0, 2, 4),
    (5, 1, 2, 4, 0, 3),
    (1, 2, 4, 5, 3, 0),
    (0, 4, 5, 3, 1, 2),
    (1, 2, 4, 5, 0, 3),
    (5, 1, 2, 4, 0, 3),
    (1, 2, 3, 4, 5, 0),
    (4, 3, 5, 1, 2, 0),
    (1, 2, 4, 5, 0, 3),
    (2, 3, 4, 5, 1, 0),
    (4, 5, 1, 2, 0, 3),
    (4, 5, 1, 2, 3, 0),
    (2, 4, 5, 1, 0, 3),
    (0, 2, 4, 3, 5, 1),
    (2, 4, 5, 1, 3, 0),
    (2, 4, 5, 1, 0, 3),
    (1, 2, 4, 5, 0, 3),
    (5, 0, 1, 2, 3, 4),
    (4, 0, 5, 1, 2, 3),
    (0, 1, 2, 3, 4, 5),
    (4, 5, 0, 1, 2, 3),
    (1, 2, 4, 5, 0, 3),
    (3, 4, 5, 0, 1, 2),
    (5, 0, 1, 2, 4, 3),
    (4, 5, 0, 1, 2, 3),
    (3, 2, 4, 0, 5, 1),
    (5, 3, 1, 2, 4, 0),
    (2, 3, 4, 5, 1, 0),
    (0, 1, 2, 3, 4, 5),
    (1, 2, 3, 4, 5, 0),
)


def chunk_dims(chunk):
    return tuple(ROTATION[axis] for axis in DIMS[chunk])


def split_shape(dims, step):
    left = [axis for axis in AXES if axis not in dims[:step]]
    at = left.index(dims[step])
    return 2**at, 2 ** (len(left) - 1 - at)


KEEP_AT = (0, 32, 0, 0, 8, 12)
SEND_AT = (32, 48, 8, 4, 10, 13)
ARRIVE_AT = (0, 32, 48, 0, 4, 6)
SLOTS = 18


def reducer(near, bits, dims_of, buffers, send_sem, recv_sem, credit, chunks):
    work, arrive, work_end, arrive_end = buffers

    def held(chunk, step):
        return work.at[chunk % SLOTS] if step < 3 else work_end.at[chunk]

    def come(chunk, step):
        return arrive.at[chunk % SLOTS] if step < 3 else arrive_end.at[chunk]

    def hop(chunk, step):
        half = 32 >> step
        return pltpu.make_async_remote_copy(
            src_ref=held(chunk, step).at[pl.ds(SEND_AT[step], half)],
            dst_ref=come(chunk, step).at[pl.ds(ARRIVE_AT[step], half)],
            send_sem=send_sem.at[chunk, step],
            recv_sem=recv_sem.at[chunk, step],
            device_id=near[dims_of(chunk)[step]],
            device_id_type=MESH,
        )

    def send(chunk, step):
        if step < 3 and chunk >= SLOTS:
            pl.semaphore_wait(credit.at[chunk - SLOTS, step], 1)
        hop(chunk, step).start()

    def put(chunk, result):
        if chunk >= SLOTS:
            for step in (1, 2):
                hop(chunk - SLOTS, step).wait_send()
        dims = dims_of(chunk)
        before, after = split_shape(dims, 0)
        own = bits[dims[0]]
        for a in range(before):
            for bit in (0, 1):
                other = own if bit == 0 else 1 - own
                piece = result[(2 * a + bit) * after : (2 * a + bit + 1) * after]
                held(chunk, 0)[pl.ds(other * 32 + a * after, after)] = piece
        send(chunk, 0)

    def advance(chunk, step, finish):
        hop(chunk, step).wait_recv()
        keep, come_at = KEEP_AT[step], ARRIVE_AT[step]
        here, there = held(chunk, step), come(chunk, step)
        if step == 5:
            finish(here[keep].astype(jnp.float32) + there[come_at].astype(jnp.float32))
            return
        if step == 0:
            hop(chunk, 0).wait_send()
        dims = dims_of(chunk)
        before, after = split_shape(dims, step + 1)
        own = bits[dims[step + 1]]
        target = held(chunk, step + 1)
        for bit, base in ((1 - own, SEND_AT[step + 1]), (own, KEEP_AT[step + 1])):

            def merge(a, carry, bit=bit, base=base):
                at = (2 * a + bit) * after
                target[pl.ds(base + a * after, after)] = (
                    here[pl.ds(keep + at, after)] + there[pl.ds(come_at + at, after)]
                )
                return carry

            lax.fori_loop(0, before, merge, 0, unroll=min(before, 8))
            if base == SEND_AT[step + 1]:
                send(chunk, step + 1)
        if step < 3 and chunk + SLOTS < chunks:
            pl.semaphore_signal(
                credit.at[chunk, step],
                inc=1,
                device_id=near[dims_of(chunk + SLOTS)[step]],
                device_id_type=MESH,
            )

    def drain(chunk):
        for step in range(1 if chunk + SLOTS >= chunks else 3, 6):
            hop(chunk, step).wait_send()

    return put, advance, drain


def nt_dot(left, right):
    return lax.dot_general(left, right, (((1,), (1,)), ((), ())), preferred_element_type=jnp.float32)


def tn_dot(left, right):
    return lax.dot_general(left, right, (((0,), (0,)), ((), ())), preferred_element_type=jnp.float32)


def norm_parts(values):
    center = values - jnp.mean(values, axis=-1, keepdims=True)
    spread = jnp.mean(center * center, axis=-1, keepdims=True)
    scale = lax.rsqrt(spread + NORM_EPS)
    return center * scale, scale


def row(vector):
    return vector[...].reshape(1, 1024)


def forward_kernel(
    pix_in, pos_in, seg_in, band_in, emb_bias_in, gain1_in, bias1_in, query_bias_in, value_bias_in, emb_in, qkv_in,
    hot_out, mask_out, stream_out, n1_out, q_out, kv_out, lse_out, att_out,
    pix, pos, hot, mask, emb_w, qkv_w, stream, flat, n1, q_pairs, kv, att,
    far_n1, run_max, run_sum, run_out, *small,
):
    (
        seg, band_of, emb_bias, gain1, bias1, query_bias, value_bias,
        load_sem, save_sem, pair_sem, send_sem, recv_sem,
    ) = small
    where = place()
    x_hi, core, x_lo, y, z = where
    partner = (x_hi * 2 + 1 - core, x_lo * 16 + y * 4 + z)
    across = ((1 - x_hi) * 2 + core, x_lo * 16 + y * 4 + z)
    barrier = pltpu.get_barrier_semaphore()
    for target in (partner, across):
        pl.semaphore_signal(barrier, inc=1, device_id=target, device_id_type=MESH)

    loads = {}

    def load(name, source, dest):
        copy = pltpu.make_async_copy(source, dest, load_sem.at[len(loads)])
        copy.start()
        loads[name] = copy

    saves = []

    def save(source, dest):
        copy = pltpu.make_async_copy(source, dest, save_sem.at[len(saves)])
        copy.start()
        saves.append(copy)

    load("seg", seg_in, seg)
    load("band", band_in, band_of)
    load("pix", pix_in, pix)
    load("eb", emb_bias_in, emb_bias)
    load("g1", gain1_in, gain1)
    load("b1", bias1_in, bias1)
    load("qb", query_bias_in, query_bias)
    load("vb", value_bias_in, value_bias)
    for band in range(4):
        span = pl.ds(768 * band, 768)
        load("emb%d" % band, emb_in.at[span, :], emb_w.at[span, :])
    load("pos", pos_in, pos)
    for part in (1, 2, 0):
        span = pl.ds(1024 * part, 1024)
        load("qkv%d" % part, qkv_in.at[:, span], qkv_w.at[:, span])
    loads["seg"].wait()
    loads["band"].wait()
    own_seg = seg[:, pl.ds(pl.multiple_of((x_hi * 2 + core) * 256, 256), 256)]
    at = lax.broadcasted_iota(jnp.int32, (128, 256), 0)
    hot[...] = (
        jnp.where(at == band_of[...], 1.0, 0.0)
        + jnp.where(at == 4, 1.0, 0.0) * jnp.where(own_seg >= 0, 1.0, 0.0)
    ).T
    save(hot, hot_out)

    for name in ("eb", "g1", "b1", "qb", "vb"):
        loads[name].wait()
    flat[0:1, :] = row(query_bias)
    flat[1:2, :] = row(value_bias)

    loads["pix"].wait()
    total = None
    for band in range(4):
        chosen = hot[:, band : band + 1]
        picked = (pix[...].astype(jnp.float32) * chosen).astype(jnp.bfloat16)
        loads["emb%d" % band].wait()
        term = jnp.dot(
            picked, emb_w[768 * band : 768 * band + 768, :], preferred_element_type=jnp.float32
        ) + chosen * emb_bias[band : band + 1, :]
        total = term if total is None else total + term
    loads["pos"].wait()
    stream[...] = total + pos[...].astype(jnp.float32)
    save(stream, stream_out)
    hat, _ = norm_parts(stream[...])
    n1[...] = (hat * row(gain1) + row(bias1)).astype(jnp.bfloat16)

    own_rows = pl.ds(pl.multiple_of((x_hi * 2 + core) * 256, 256), 256)

    def far_rows(low, piece):
        return pl.ds(pl.multiple_of(((1 - x_hi) * 2 + low) * 256 + 128 * piece, 128), 128)

    def push(source, dest, which, index, target):
        return pltpu.make_async_remote_copy(
            src_ref=source,
            dst_ref=dest,
            send_sem=send_sem.at[which, index],
            recv_sem=recv_sem.at[which, index],
            device_id=target,
            device_id_type=MESH,
        )

    def norm_copy(piece):
        span = pl.ds(128 * piece, 128)
        return push(n1.at[span, :], far_n1.at[span, :], 0, piece, across)

    def to_partner(pair):
        piece = kv.at[pair, :, own_rows, :]
        return push(piece, piece, 1, pair, partner)

    def far_copy(piece):
        part = kv.at[:, :, far_rows(core, piece), :]
        return push(part, part, 2, piece, partner)

    pl.semaphore_wait(barrier, 2)
    for piece in (0, 1):
        norm_copy(piece).start()
    save(n1, n1_out)
    loads["qkv1"].wait()
    loads["qkv2"].wait()

    def keys_values(source, tile, target):
        span = pl.ds(pl.multiple_of(1024 + 256 * tile, 256), 256)
        keys = jnp.dot(source, qkv_w[:, span], preferred_element_type=jnp.float32).astype(
            jnp.bfloat16
        )
        span = pl.ds(pl.multiple_of(2048 + 256 * tile, 256), 256)
        shift = flat[1:2, pl.ds(pl.multiple_of(256 * tile, 256), 256)]
        values = (
            jnp.dot(source, qkv_w[:, span], preferred_element_type=jnp.float32) + shift
        ).astype(jnp.bfloat16)
        for side in (0, 1):
            kv[2 * tile + side, 0, target, :] = keys[:, 128 * side : 128 * side + 128]
            kv[2 * tile + side, 1, target, :] = values[:, 128 * side : 128 * side + 128]

    def project(tile, carry):
        keys_values(n1[...], tile, own_rows)
        for side in (0, 1):
            to_partner(2 * tile + side).start()
        return carry

    lax.fori_loop(0, 4, project, 0, unroll=4)
    loads["qkv0"].wait()

    def project_query(tile, carry):
        span = pl.ds(pl.multiple_of(256 * tile, 256), 256)
        query = (
            jnp.dot(n1[...], qkv_w[:, span], preferred_element_type=jnp.float32)
            + flat[0:1, span]
        ).astype(jnp.bfloat16)
        query = (query.astype(jnp.float32) * HD ** (-0.5)).astype(jnp.bfloat16)
        for side in (0, 1):
            q_pairs[2 * tile + side] = query[:, 128 * side : 128 * side + 128]
        return carry

    lax.fori_loop(0, 4, project_query, 0, unroll=4)
    save(q_pairs, q_out)
    key_seg = jnp.broadcast_to(seg[...].astype(jnp.float32), (128, 1024)).T[:, 0:1]
    mask[...] = jnp.where(key_seg == own_seg.astype(jnp.float32), 0.0, MASKED)
    save(mask, mask_out)

    def project_far(piece):
        norm_copy(piece).wait_recv()

        def step(tile, carry):
            keys_values(far_n1[128 * piece : 128 * piece + 128, :], tile, far_rows(core, piece))
            return carry

        lax.fori_loop(0, 4, step, 0, unroll=4)
        far_copy(piece).start()

    def attend(span, first=False, last=False):
        def body(pair, carry):
            if first:
                to_partner(pair).wait_recv()
            if last:
                pltpu.make_async_copy(kv.at[pair], kv_out.at[pair], pair_sem.at[pair]).start()
            keys = kv[pair, 0, span, :]
            value_rows = kv[pair, 1, span, :].T
            bias = mask[span, :]
            turned = q_pairs[pair].astype(jnp.float32).T
            at = lax.broadcasted_iota(jnp.int32, (128, 256), 0)
            heads = []
            for head in (0, 1):
                own = (at < 64) if head == 0 else (at >= 64)
                mine = jnp.where(own, turned, 0.0).astype(jnp.bfloat16)
                scores = jnp.dot(keys, mine, preferred_element_type=jnp.float32) + bias
                peak = jnp.max(scores, axis=0, keepdims=True)
                if not first:
                    before = run_max[pair, head : head + 1, :]
                    peak = jnp.maximum(peak, before)
                    fade = jnp.exp(before - peak)
                expo = jnp.exp(scores - peak)
                norm = jnp.sum(expo, axis=0, keepdims=True)
                out = jnp.dot(
                    value_rows[64 * head : 64 * head + 64],
                    expo.astype(jnp.bfloat16),
                    preferred_element_type=jnp.float32,
                )
                if not first:
                    norm = norm + fade * run_sum[pair, head : head + 1, :]
                    out = out + fade * run_out[pair, 64 * head : 64 * head + 64, :]
                if last:
                    heads.append(out / norm)
                    lse_out[pair, head : head + 1, :] = peak + jnp.log(norm)
                else:
                    run_max[pair, head : head + 1, :] = peak
                    run_sum[pair, head : head + 1, :] = norm
                    run_out[pair, 64 * head : 64 * head + 64, :] = out
            if last:
                att[:, pl.ds(pl.multiple_of(pair * 128, 128), 128)] = jnp.concatenate(
                    heads, axis=0
                ).T.astype(jnp.bfloat16)
            return carry

        lax.fori_loop(0, 8, body, 0, unroll=2)

    attend(pl.ds(pl.multiple_of(x_hi * 512, 512), 512), first=True)
    for piece in (0, 1):
        project_far(piece)
    for piece in (0, 1):
        far_copy(piece).wait_recv()
    attend(pl.ds(pl.multiple_of((1 - x_hi) * 512, 512), 512), last=True)
    save(att, att_out)
    for copy in saves:
        copy.wait()

    def drain(pair, carry):
        to_partner(pair).wait_send()
        pltpu.make_async_copy(kv.at[pair], kv_out.at[pair], pair_sem.at[pair]).wait()
        return carry

    lax.fori_loop(0, 8, drain, 0)
    for piece in (0, 1):
        norm_copy(piece).wait_send()
        far_copy(piece).wait_send()


def forward(*operands):
    any_space = pl.BlockSpec(memory_space=pl.ANY)
    in_vmem = pl.BlockSpec(memory_space=pltpu.VMEM)
    half, full = jnp.bfloat16, jnp.float32
    shape = jax.ShapeDtypeStruct
    return pl.pallas_call(
        forward_kernel,
        out_shape=(
            shape((256, 128), full),
            shape((1024, 256), full),
            shape((256, 1024), full),
            shape((256, 1024), half),
            shape((8, 256, 128), half),
            shape((8, 2, 1024, 128), half),
            shape((8, 2, 256), full),
            shape((256, 1024), half),
        ),
        in_specs=[any_space] * 11,
        out_specs=(any_space,) * 6 + (in_vmem, any_space),
        scratch_shapes=[
            pltpu.VMEM((256, 768), half),
            pltpu.VMEM((256, 1024), half),
            pltpu.VMEM((256, 128), full),
            pltpu.VMEM((1024, 256), full),
            pltpu.VMEM((3072, 1024), half),
            pltpu.VMEM((1024, 3072), half),
            pltpu.VMEM((256, 1024), full),
            pltpu.VMEM((8, 1024), full),
            pltpu.VMEM((256, 1024), half),
            pltpu.VMEM((8, 256, 128), half),
            pltpu.VMEM((8, 2, 1024, 128), half),
            pltpu.VMEM((256, 1024), half),
            pltpu.VMEM((256, 1024), half),
            pltpu.VMEM((8, 2, 256), full),
            pltpu.VMEM((8, 2, 256), full),
            pltpu.VMEM((8, 128, 256), full),
            pltpu.VMEM((1, 1024), jnp.int32),
            pltpu.VMEM((1, 256), jnp.int32),
            pltpu.VMEM((4, 1024), full),
            pltpu.VMEM((1024,), full),
            pltpu.VMEM((1024,), full),
            pltpu.VMEM((1024,), full),
            pltpu.VMEM((1024,), full),
            pltpu.SemaphoreType.DMA((20,)),
            pltpu.SemaphoreType.DMA((8,)),
            pltpu.SemaphoreType.DMA((8,)),
            pltpu.SemaphoreType.DMA((3, 8)),
            pltpu.SemaphoreType.DMA((3, 8)),
        ],
        compiler_params=pltpu.CompilerParams(
            collective_id=1, has_side_effects=True, vmem_limit_bytes=VMEM_BYTES
        ),
        name="forward",
    )(*operands)


def exchanger(core, partner, ex_send, ex_recv, ex_local):
    made = []

    def exchange(source, dest, cut=None):
        index = len(made)

        def part(owner):
            if cut is None:
                return source
            at, span = cut
            return source.at[:, pl.ds(pl.multiple_of(at + owner * span, 128), span)]

        made.append(
            (
                pltpu.make_async_copy(part(core), dest(0), ex_local.at[index]),
                pltpu.make_async_remote_copy(
                    src_ref=part(1 - core),
                    dst_ref=dest(1),
                    send_sem=ex_send.at[index],
                    recv_sem=ex_recv.at[index],
                    device_id=partner,
                    device_id_type=MESH,
                ),
            )
        )
        return made[-1]

    def whole(source, buf):
        return [exchange(source, lambda half: buf.at[pl.ds(256 * half, 256), :])]

    def halves(source, buf, span):
        return [
            exchange(
                source,
                lambda half, high=high: buf.at[pl.ds(256 * half, 256), pl.ds(high * span, span)],
                (high * 2 * span, span),
            )
            for high in (0, 1)
        ]

    return exchange, whole, halves, made


def begin(copies):
    for local, remote in copies:
        remote.start()
        local.start()


def arrived(copies):
    for local, remote in copies:
        local.wait()
        remote.wait_recv()


def turn_rows(buf, dest):
    turned = buf[...].astype(jnp.float32).T
    dest[...] = jnp.concatenate(
        [turned[8 * block : 8 * block + 8] for block in BLOCKS], axis=0
    ).astype(jnp.bfloat16)


def chunk_product(left, right_a, right_b):
    a = jnp.dot(left, right_a, preferred_element_type=jnp.float32)
    b = jnp.dot(left, right_b, preferred_element_type=jnp.float32)
    return jnp.concatenate((a.reshape(64, 8, 256), b.reshape(64, 8, 256)), axis=1).astype(
        jnp.bfloat16
    )


def wide_finish(dest, tile):
    def finish(total):
        dest[:, 512 * tile : 512 * tile + 256] = total[:8]
        dest[:, 512 * tile + 256 : 512 * tile + 512] = total[8:]

    return finish


HEADS, FAR, CLOSE, GP, PUT, ADV, THROUGH, NORM, ROWS, BIAS, ADVB, PIX, POST, GATT, MLP = range(15)
SCHEDULE = (
    (MLP, 0), (MLP, 1), (MLP, 2), (PUT, 8), (PUT, 9), (MLP, 3), (PUT, 10), (MLP, 4), (MLP, 5), (PUT, 11),
    (MLP, 6), (PUT, 12), (PUT, 13), (MLP, 7), (POST,), (ADV, 9, 0), (ADV, 8, 0), (GATT,), (ADV, 10, 0),
    (PUT, 2), (PUT, 0), (PUT, 14), (HEADS, 0), (ADV, 12, 0), (ADV, 9, 1), (ADV, 13, 0), (PUT, 4),
    (ADV, 10, 1), (ADV, 11, 0), (HEADS, 1), (FAR, 0), (ADV, 8, 1), (HEADS, 2), (FAR, 1), (ADV, 2, 0),
    (HEADS, 3), (FAR, 2), (GP, 0), (ADV, 3, 0), (ADV, 1, 0), (ADV, 0, 0), (ADV, 12, 1), (ADV, 9, 2),
    (PUT, 15), (ADV, 14, 0), (ADV, 8, 2), (PUT, 6), (CLOSE, 0), (HEADS, 4), (FAR, 3), (ADV, 4, 0),
    (CLOSE, 1), (ADV, 13, 1), (HEADS, 5), (FAR, 4), (ADV, 5, 0), (ADV, 3, 1), (ADV, 10, 2), (ADV, 2, 1),
    (HEADS, 6), (FAR, 5), (CLOSE, 2), (ADV, 14, 1), (ADV, 1, 1), (ADV, 11, 1), (HEADS, 7), (FAR, 6),
    (CLOSE, 3), (GP, 1), (GP, 2), (GP, 3), (ADV, 0, 1), (PUT, 17), (ADV, 15, 0), (ADV, 12, 2), (THROUGH, 0),
    (CLOSE, 4), (FAR, 7), (ADV, 9, 3), (THROUGH, 1), (ADV, 6, 0), (ADV, 8, 3), (PUT, 16), (THROUGH, 2),
    (ADV, 7, 0), (THROUGH, 3), (ADV, 4, 1), (ADV, 3, 2), (CLOSE, 5), (ADV, 10, 3), (ADV, 13, 2),
    (ADV, 5, 1), (ADV, 14, 2), (ADV, 1, 2), (ADV, 2, 2), (ADV, 11, 2), (PUT, 21), (CLOSE, 6), (ADV, 0, 2),
    (ADV, 12, 3), (PUT, 19), (ADV, 6, 1), (ADV, 9, 4), (ADV, 15, 1), (PUT, 20), (CLOSE, 7), (GP, 4),
    (GP, 5), (ADV, 5, 2), (THROUGH, 4), (ADV, 4, 2), (ADV, 8, 4), (ADV, 10, 4), (ADV, 11, 3), (ADV, 17, 0),
    (THROUGH, 5), (ADV, 0, 3), (ADV, 2, 3), (ADV, 1, 3), (NORM,), (ROWS,), (ADV, 7, 1), (ADV, 12, 4),
    (PUT, 23), (ADV, 15, 2), (PUT, 18), (ADV, 3, 3), (PUT, 22), (BIAS,), (ADV, 16, 0), (ADV, 14, 3),
    (ADV, 13, 3), (ADV, 4, 3), (ADV, 6, 2), (ADV, 0, 4), (ADV, 11, 4), (PUT, 27), (ADV, 7, 2), (ADV, 2, 4),
    (PUT, 29), (ADV, 19, 0), (PUT, 26), (ADV, 20, 0), (PUT, 28), (ADV, 9, 5), (ADV, 8, 5), (ADV, 5, 3),
    (ADV, 10, 5), (ADV, 12, 5), (PUT, 24), (PUT, 25), (PIX,), (ADV, 17, 1), (ADV, 1, 4), (ADV, 21, 0),
    (ADV, 15, 3), (ADV, 16, 1), (ADV, 3, 4), (ADV, 22, 0), (ADV, 23, 0), (ADV, 7, 3), (ADV, 14, 4),
    (ADV, 13, 4), (ADVB, 0), (ADV, 18, 0), (ADV, 4, 4), (ADV, 11, 5), (ADV, 2, 5), (ADV, 6, 3), (ADV, 0, 5),
    (ADV, 27, 0), (ADV, 29, 0), (ADV, 25, 0), (ADV, 26, 0), (ADV, 1, 5), (ADV, 4, 5), (ADV, 28, 0),
    (ADV, 21, 1), (ADV, 3, 5), (ADV, 5, 4), (ADV, 24, 0), (ADV, 7, 4), (ADV, 15, 4), (ADV, 19, 1),
    (ADV, 20, 1), (ADV, 6, 4), (ADV, 16, 2), (ADV, 17, 2), (ADV, 13, 5), (ADV, 27, 1), (ADV, 23, 1),
    (ADV, 14, 5), (ADV, 29, 1), (ADVB, 1), (ADV, 22, 1), (ADV, 26, 1), (ADV, 5, 5), (ADV, 15, 5),
    (ADV, 24, 1), (ADV, 21, 2), (ADV, 18, 1), (ADV, 25, 1), (ADV, 16, 3), (ADV, 7, 5), (ADV, 28, 1),
    (ADV, 27, 2), (ADV, 29, 2), (ADV, 19, 2), (ADV, 20, 2), (ADV, 6, 5), (ADV, 23, 2), (ADV, 17, 3),
    (ADV, 22, 2), (ADVB, 2), (ADV, 21, 3), (ADV, 26, 2), (ADV, 24, 2), (ADV, 16, 4), (ADV, 25, 2),
    (ADV, 18, 2), (ADV, 28, 2), (ADV, 19, 3), (ADV, 29, 3), (ADV, 20, 3), (ADV, 27, 3), (ADV, 17, 4),
    (ADV, 23, 3), (ADV, 22, 3), (ADVB, 3), (ADV, 21, 4), (ADV, 26, 3), (ADV, 16, 5), (ADV, 24, 3),
    (ADV, 25, 3), (ADV, 18, 3), (ADV, 19, 4), (ADV, 29, 4), (ADV, 28, 3), (ADV, 20, 4), (ADV, 17, 5),
    (ADV, 27, 4), (ADV, 23, 4), (ADV, 22, 4), (ADVB, 4), (ADV, 21, 5), (ADV, 26, 4), (ADV, 24, 4),
    (ADV, 25, 4), (ADV, 19, 5), (ADV, 29, 5), (ADV, 18, 4), (ADV, 20, 5), (ADV, 28, 4), (ADV, 27, 5),
    (ADV, 23, 5), (ADV, 22, 5), (ADVB, 5), (ADV, 26, 5), (ADV, 24, 5), (ADV, 25, 5), (ADV, 18, 5),
    (ADV, 28, 5),
)


CHUNKS = 30


def backward_kernel(
    att_in, stream_in, cot_in, hot_in, mask_in, q_in, kv_in, lse_in, n1_in, pix_in,
    gain1_in, gain2_in, bias2_in, out_bias_in, fc1_bias_in, fc2_bias_in, emb_in, qkv_in, ow_in, fc1_in, fc2_in,
    block_out, pix_out, emb_out, qkv_out, out_out, fc1_out, fc2_out, bias_out,
    x_buf, hid, hid_come, gbr_buf, gpre_buf, gout_buf, gp_buf, pix_buf, hot_buf, row_buf, lanes, sums,
    xt_buf, xht_buf, work, arrive, work_end, arrive_end, work_f, arrive_f, work_end_f, arrive_end_f,
    q_pairs, kv, gatt, mask, near_send, near_come, far_send, far_come, held, far_held, whole_grad,
    n2, stream, middle, acc, grown_buf, gs, pix_grad, tall, wide,
    lse, gain1, gain2, bias2, out_bias, fc1_bias, fc2_bias,
    ex_send, ex_recv, ex_local, send_sem, recv_sem, credit, send_f, recv_f, load_sem, kv_sem, tall_sem, wide_sem,
    kv_send_sem, kv_recv_sem, kv_credit, gp_send, gp_recv, pre_send, pre_recv, tok_send, tok_recv,
):
    where = place()
    x_hi, core, x_lo, y, z = where
    near = neighbours(where)
    bits = own_bits(where)
    partner = near["core"]
    across = ((1 - x_hi) * 2 + core, x_lo * 16 + y * 4 + z)

    def kv_load(pair):
        return pltpu.make_async_copy(kv_in.at[pair], kv.at[pair % 2], kv_sem.at[pair % 2])

    order = (0, 1, 2, 4, 3, 5)

    def tall_load(index):
        if index < 8:
            source = fc1_in.at[:, pl.ds(512 * index, 512)]
        else:
            source = qkv_in.at[:, pl.ds(512 * order[index - 8], 512)]
        return pltpu.make_async_copy(source, tall.at[index % 3], tall_sem.at[index % 3])

    def wide_load(index):
        if index < 2 or index in (10, 11):
            source = ow_in.at[pl.ds(512 * (index % 2), 512), :]
        elif index < 10:
            source = fc2_in.at[pl.ds(512 * (index - 2), 512), :]
        else:
            source = emb_in.at[pl.ds(512 * (index - 12), 512), :]
        return pltpu.make_async_copy(source, wide.at[index % 3], wide_sem.at[index % 3])

    def used(load, index, last):
        if index + 3 < last:
            load(index + 3).start()

    loads = []
    for source, dest in (
        (att_in, n2), (stream_in, stream), (hot_in, hot_buf.at[pl.ds(0, 256), :]), (cot_in, gs),
        (gain1_in, gain1), (gain2_in, gain2), (bias2_in, bias2), (out_bias_in, out_bias),
        (fc1_bias_in, fc1_bias), (fc2_bias_in, fc2_bias), (lse_in, lse), (q_in, q_pairs), (mask_in, mask),
    ):
        loads.append(pltpu.make_async_copy(source, dest, load_sem.at[len(loads)]))
    loads[0].start()
    for index in range(2):
        wide_load(index).start()
    for copy in loads[1:10]:
        copy.start()
    wide_load(2).start()
    for index in range(3):
        tall_load(index).start()
    for copy in loads[10:]:
        copy.start()
    for pair in range(2):
        kv_load(pair).start()
    targets = tuple(near.values()) + (across,)
    barrier = pltpu.get_barrier_semaphore()
    for target in targets:
        pl.semaphore_signal(barrier, inc=1, device_id=target, device_id_type=MESH)

    put, advance, drain = reducer(
        near, bits, chunk_dims, (work, arrive, work_end, arrive_end), send_sem, recv_sem, credit, CHUNKS
    )
    put_f, advance_f, drain_f = reducer(
        near, bits, lambda chunk: ROTATION, (work_f, arrive_f, work_end_f, arrive_end_f),
        send_f, recv_f, None, 1,
    )
    exchange, whole, halves, made = exchanger(core, partner, ex_send, ex_recv, ex_local)
    groups = {
        "fc1": halves(n2, x_buf.at[0], 256),
        "out": halves(att_in, x_buf.at[1], 256),
        "qkv": halves(n1_in, x_buf.at[2], 256),
        "side": whole(pix_in, pix_buf),
        "emb": halves(gs, x_buf.at[0], 256),
        "rows": [exchange(lanes.at[pl.ds(0, 16), :], lambda half: row_buf.at[half])],
    }

    def mirror(buf, index, span=slice(None)):
        return pltpu.make_async_remote_copy(
            src_ref=buf.at[pl.ds(0, 256), span],
            dst_ref=buf.at[pl.ds(256, 256), span],
            send_sem=tok_send.at[index],
            recv_sem=tok_recv.at[index],
            device_id=partner,
            device_id_type=MESH,
        )

    def gout_copy():
        return mirror(gout_buf, 0)

    def gbr_copy():
        return mirror(gbr_buf, 1)

    def hot_copy():
        return mirror(hot_buf, 2)

    def hid_copy(high):
        return pltpu.make_async_remote_copy(
            src_ref=hid.at[1 - core, :, pl.ds(1024 * high, 1024)],
            dst_ref=hid_come.at[:, pl.ds(1024 * high, 1024)],
            send_sem=tok_send.at[3 + high],
            recv_sem=tok_recv.at[3 + high],
            device_id=partner,
            device_id_type=MESH,
        )

    def gpre_copy(tile):
        span = pl.ds(512 * tile, 512)
        return pltpu.make_async_remote_copy(
            src_ref=gpre_buf.at[pl.ds(0, 256), span],
            dst_ref=gpre_buf.at[pl.ds(256, 256), span],
            send_sem=pre_send.at[tile],
            recv_sem=pre_recv.at[tile],
            device_id=partner,
            device_id_type=MESH,
        )

    def gp_copy(index):
        span = pl.ds(512 * order[index], 512)
        return pltpu.make_async_remote_copy(
            src_ref=gp_buf.at[pl.ds(0, 256), span],
            dst_ref=gp_buf.at[pl.ds(256, 256), span],
            send_sem=gp_send.at[index],
            recv_sem=gp_recv.at[index],
            device_id=partner,
            device_id_type=MESH,
        )

    plan = [("fc2", tile) for tile in range(8)] + [("fc1", tile) for tile in range(8)]
    plan += [("out", tile) for tile in range(2)] + [("qkv", index) for index in range(6)]
    plan += [("emb", tile) for tile in range(6)]
    turned_from = {"fc1": 0, "out": 1, "qkv": 2, "emb": 0}
    ready = set()

    def band_pixels(tile):
        band, at = tile // 3, tile % 3
        picked = pix_buf[:, 256 * at : 256 * at + 256].astype(jnp.float32)
        return (picked * hot_buf[:, band : band + 1]).astype(jnp.bfloat16)

    def turn_wide(buf, at):
        turned = buf[...].astype(jnp.float32).T.astype(jnp.bfloat16)
        xht_buf[:, at : at + 256] = jnp.concatenate(
            [turned[32 * block : 32 * block + 32] for block in BLOCKS], axis=0
        )

    def compute(chunk):
        name, tile = plan[chunk]
        if name not in ready:
            ready.add(name)
            if name == "fc2":
                turn_wide(hid.at[core], 0)
                for high in (0, 1):
                    hid_copy(high).wait_recv()
                turn_wide(hid_come, 256)
                gout_copy().wait_recv()
            else:
                arrived(groups[name])
                if name == "out":
                    gbr_copy().wait_recv()
                turn_rows(x_buf.at[turned_from[name]], xt_buf)
        if name == "fc2":
            if tile % 2 == 0:
                both = jnp.dot(
                    xht_buf[...],
                    gout_buf[:, 128 * tile : 128 * tile + 256],
                    preferred_element_type=jnp.float32,
                ).reshape(64, 32, 256)
                put(chunk, both[:, :16].astype(jnp.bfloat16))
                put(chunk + 1, both[:, 16:].astype(jnp.bfloat16))
            return
        if name == "emb":
            right = (band_pixels(2 * tile), band_pixels(2 * tile + 1))
        else:
            if name == "qkv":
                gp_copy(tile).wait_recv()
                tile = order[tile]
            if name == "fc1":
                gpre_copy(tile).wait_recv()
            buf = {"fc1": gpre_buf, "out": gbr_buf, "qkv": gp_buf}[name]
            right = (
                buf[:, 512 * tile : 512 * tile + 256],
                buf[:, 512 * tile + 256 : 512 * tile + 512],
            )
        put(chunk, chunk_product(xt_buf[...], *right))

    def finisher(chunk):
        name, tile = plan[chunk]
        if name == "fc2":

            def finish(total):
                at = 16 * (tile % 2)
                fc2_out[at : at + 16, 128 * (tile - tile % 2) : 128 * (tile - tile % 2) + 256] = total

            return finish
        if name == "qkv":
            tile = order[tile]
        return wide_finish({"fc1": fc1_out, "out": out_out, "qkv": qkv_out, "emb": emb_out}[name], tile)

    def wave(index):
        for chunk in range(6 * index, 6 * index + 6):
            compute(chunk)

    def step_wave(*pairs):
        for index, step in pairs:
            for chunk in range(6 * index, 6 * index + 6):
                advance(chunk, step, finisher(chunk))

    def block_at(high, low):
        return pl.ds(pl.multiple_of((high * 2 + low) * 256, 256), 256)

    def near_copy(pair):
        return pltpu.make_async_remote_copy(
            src_ref=near_send.at[pair % 2],
            dst_ref=near_come.at[pair % 4],
            send_sem=kv_send_sem.at[0, pair],
            recv_sem=kv_recv_sem.at[0, pair],
            device_id=partner,
            device_id_type=MESH,
        )

    def far_copy(pair):
        return pltpu.make_async_remote_copy(
            src_ref=far_send.at[pair % 2],
            dst_ref=far_come.at[pair],
            send_sem=kv_send_sem.at[1, pair],
            recv_sem=kv_recv_sem.at[1, pair],
            device_id=across,
            device_id_type=MESH,
        )

    def heads_back(pair):
        slot = pair % 2
        kv_load(pair).wait()
        at = lax.broadcasted_iota(jnp.int32, (128, 256), 0)
        lane = lax.broadcasted_iota(jnp.int32, (256, 128), 1)
        query = q_pairs[pair].astype(jnp.float32)
        grad = gatt[pair].astype(jnp.float32)
        query_t, grad_t = query.T, grad.T
        key_rows = kv[slot, 0].T
        key_grad = value_grad = None
        query_grads = []
        for head in (0, 1):
            own = (at < 64) if head == 0 else (at >= 64)
            mine = (lane < 64) if head == 0 else (lane >= 64)
            scores = (
                jnp.dot(
                    kv[slot, 0],
                    jnp.where(own, query_t, 0.0).astype(jnp.bfloat16),
                    preferred_element_type=jnp.float32,
                )
                + mask[...]
            )
            probs = jnp.exp(scores - lse[pair, head : head + 1, :])
            prob_grad = jnp.dot(
                kv[slot, 1],
                jnp.where(own, grad_t, 0.0).astype(jnp.bfloat16),
                preferred_element_type=jnp.float32,
            )
            mean = jnp.sum(probs * prob_grad, axis=0, keepdims=True)
            score_grad = (probs * (prob_grad - mean)).astype(jnp.bfloat16)
            query_grads.append(
                jnp.dot(
                    key_rows[64 * head : 64 * head + 64],
                    score_grad,
                    preferred_element_type=jnp.float32,
                )
            )
            key_part = jnp.dot(
                score_grad,
                jnp.where(mine, query, 0.0).astype(jnp.bfloat16),
                preferred_element_type=jnp.float32,
            )
            value_part = jnp.dot(
                probs.astype(jnp.bfloat16),
                jnp.where(mine, grad, 0.0).astype(jnp.bfloat16),
                preferred_element_type=jnp.float32,
            )
            key_grad = key_part if head == 0 else key_grad + key_part
            value_grad = value_part if head == 0 else value_grad + value_part
        if pair + 2 < 8:
            kv_load(pair + 2).start()
        if pair >= 2:
            near_copy(pair - 2).wait_send()
        gp_buf[0:256, 128 * pair : 128 * pair + 128] = (
            jnp.concatenate(query_grads, axis=0).T * HD ** (-0.5)
        ).astype(jnp.bfloat16)
        whole_grad[0] = key_grad
        whole_grad[1] = value_grad
        for kind in (0, 1):
            near_send[pair % 2, 0, kind] = whole_grad[kind, block_at(x_hi, 1 - core), :].astype(
                jnp.bfloat16
            )
            near_send[pair % 2, 1, kind] = whole_grad[kind, block_at(1 - x_hi, 1 - core), :].astype(
                jnp.bfloat16
            )
        if pair >= 4:
            pl.semaphore_wait(kv_credit.at[pair - 4], 1)
        near_copy(pair).start()
        for kind in (0, 1):
            held[pair % 2, kind] = whole_grad[kind, block_at(x_hi, core), :]
            far_held[pair % 2, kind] = whole_grad[kind, block_at(1 - x_hi, core), :]

    def pass_far(pair):
        near_copy(pair).wait_recv()
        if pair >= 2:
            far_copy(pair - 2).wait_send()
        for kind in (0, 1):
            far_send[pair % 2, kind] = (
                far_held[pair % 2, kind] + near_come[pair % 4, 1, kind].astype(jnp.float32)
            ).astype(jnp.bfloat16)
        far_copy(pair).start()
        for kind in (0, 1):
            at = 1024 * (kind + 1) + 128 * pair
            gp_buf[0:256, at : at + 128] = (
                held[pair % 2, kind] + near_come[pair % 4, 0, kind].astype(jnp.float32)
            ).astype(jnp.bfloat16)
        if pair < 4:
            pl.semaphore_signal(
                kv_credit.at[pair], inc=1, device_id=partner, device_id_type=MESH
            )

    def close(pair):
        far_copy(pair).wait_recv()
        for kind in (0, 1):
            at = 1024 * (kind + 1) + 128 * pair
            gp_buf[0:256, at : at + 128] = (
                gp_buf[0:256, at : at + 128].astype(jnp.float32)
                + far_come[pair, kind].astype(jnp.float32)
            ).astype(jnp.bfloat16)

    def through_qkv(index):
        tall_load(8 + index).wait()
        tile = order[index]
        part = nt_dot(gp_buf[0:256, 512 * tile : 512 * tile + 512], tall[(8 + index) % 3])
        grown_buf[...] = part if index == 0 else grown_buf[...] + part
        used(tall_load, 8 + index, 14)

    for copy in loads[:3] + loads[4:10]:
        copy.wait()
    total = stream[...] + row(out_bias)
    for index in (0, 1):
        wide_load(index).wait()
        total = total + jnp.dot(
            n2[:, 512 * index : 512 * index + 512], wide[index], preferred_element_type=jnp.float32
        )
        used(wide_load, index, 18)
    middle[...] = total
    hat, _ = norm_parts(total)
    n2[...] = (hat * row(gain2) + row(bias2)).astype(jnp.bfloat16)
    pl.semaphore_wait(barrier, len(targets))
    begin(groups["fc1"])
    hot_copy().start()
    for name in ("out", "qkv", "side"):
        begin(groups[name])
    loads[3].wait()
    gout_buf[0:256, :] = (gs[...].astype(jnp.float32) * hot_buf[0:256, 4:5]).astype(jnp.bfloat16)
    gout_copy().start()
    def mlp_tile(tile):
        span = slice(512 * tile, 512 * tile + 512)
        tall_load(tile).wait()
        wide_load(2 + tile).wait()
        pre = jnp.dot(n2[...], tall[tile % 3], preferred_element_type=jnp.float32) + fc1_bias[
            span
        ].reshape(1, 512)
        cdf = 0.5 * (1.0 + lax.erf(pre * (0.5**0.5)))
        hidden = (pre * cdf).astype(jnp.bfloat16)
        at = 1024 * (tile // 4) + 512 * (tile % 2)
        hid[(tile // 2) % 2, :, at : at + 512] = hidden
        slope = cdf + pre * (jnp.exp(-0.5 * pre * pre) * 0.3989422804014327)
        back = (nt_dot(gout_buf[0:256, :], wide[(2 + tile) % 3]) * slope).astype(jnp.bfloat16)
        gpre_buf[0:256, span] = back
        gpre_copy(tile).start()
        ahead = jnp.dot(hidden, wide[(2 + tile) % 3], preferred_element_type=jnp.float32)
        used(wide_load, 2 + tile, 18)
        behind = nt_dot(back, tall[tile % 3])
        used(tall_load, tile, 14)
        acc[...] = ahead if tile == 0 else acc[...] + ahead
        grown_buf[...] = behind if tile == 0 else grown_buf[...] + behind
        quarter, at = tile // 2, 512 * (tile % 2)
        sums[4 + quarter : 5 + quarter, at : at + 512] = jnp.sum(
            back.astype(jnp.float32), axis=0, keepdims=True
        )
        if tile % 4 == 3:
            hid_copy(tile // 4).start()

    block_copy = pltpu.make_async_copy(gs, block_out, load_sem.at[13])

    def mlp_back():
        gs[...] = (
            hot_buf[0:256, 4:5] * (middle[...] + (acc[...] + row(fc2_bias)))
        ).astype(jnp.bfloat16)
        block_copy.start()
        upstream = gout_buf[0:256, :].astype(jnp.float32)
        sums[3:4, :] = jnp.sum(upstream, axis=0, keepdims=True)
        grown = grown_buf[...]
        hat, scale = norm_parts(middle[...])
        sums[1:2, :] = jnp.sum(grown * hat, axis=0, keepdims=True)
        sums[2:3, :] = jnp.sum(grown, axis=0, keepdims=True)
        grown = grown * row(gain2)
        middle[...] = upstream + scale * (
            grown
            - jnp.mean(grown, axis=-1, keepdims=True)
            - hat * jnp.mean(grown * hat, axis=-1, keepdims=True)
        )
        gbr_buf[0:256, :] = middle[...].astype(jnp.bfloat16)
        gbr_copy().start()
        sums[0:1, :] = jnp.sum(gbr_buf[0:256, :].astype(jnp.float32), axis=0, keepdims=True)

    def attention_grad():
        for index in (0, 1):
            wide_load(10 + index).wait()
            back = nt_dot(gbr_buf[0:256, :], wide[(10 + index) % 3]).astype(jnp.bfloat16)
            used(wide_load, 10 + index, 18)
            for pair in range(4):
                gatt[4 * index + pair] = back[:, 128 * pair : 128 * pair + 128]

    def norm_back():
        block_copy.wait()
        grown = grown_buf[...]
        hat, scale = norm_parts(stream[...])
        lanes[...] = jnp.zeros_like(lanes)
        lanes[4:5, :] = jnp.sum(grown * hat, axis=0, keepdims=True)
        lanes[5:6, :] = jnp.sum(grown, axis=0, keepdims=True)
        grown = grown * row(gain1)
        gs[...] = (
            middle[...]
            + scale
            * (
                grown
                - jnp.mean(grown, axis=-1, keepdims=True)
                - hat * jnp.mean(grown * hat, axis=-1, keepdims=True)
            )
        ).astype(jnp.bfloat16)
        begin(groups["emb"])
        arrived(groups["side"])
        hot_copy().wait_recv()

    def side_rows():
        lanes[6:7, :] = jnp.sum(gp_buf[0:256, 0:1024].astype(jnp.float32), axis=0, keepdims=True)
        lanes[7:8, :] = jnp.sum(gp_buf[0:256, 2048:3072].astype(jnp.float32), axis=0, keepdims=True)
        lanes[0:4, :] = tn_dot(hot_buf[0:256, :].astype(jnp.bfloat16), gs[...])[0:4]
        lanes[8:16, :] = sums[...]
        begin(groups["rows"])

    def bias_chunk():
        arrived(groups["rows"])
        groups["rows"][0][1].wait_send()
        lanes[0:16, :] = row_buf[0] + row_buf[1]
        halves_t = [
            lanes[:, pl.ds(pl.multiple_of(high * 512 + core * 256, 128), 256)].T.reshape(32, 8, 128)
            for high in (0, 1)
        ]
        lane = lax.broadcasted_iota(jnp.int32, (32, 8, 128), 2)
        quarters = lanes[...].T.reshape(32, 4, 8, 128)
        for high in (0, 1):
            wide = jnp.where(lane < 12, halves_t[high], 0.0)
            for part in range(4):
                here = jnp.where(
                    core == 0,
                    quarters[:, part, :, 12 + 2 * high : 13 + 2 * high],
                    quarters[:, part, :, 13 + 2 * high : 14 + 2 * high],
                )
                wide = wide + jnp.where(lane == 12 + part, here, 0.0)
            halves_t[high] = wide
        turned = jnp.concatenate(halves_t, axis=0)
        put_f(0, jnp.concatenate([turned[b : b + 1] for b in BLOCKS], axis=0))

    out = pltpu.make_async_copy(pix_grad, pix_out, load_sem.at[14])

    def pixels_back():
        parts = [None] * 3
        for index in range(6):
            wide_load(12 + index).wait()
            for side in (0, 1):
                band, third = divmod(2 * index + side, 3)
                term = hot_buf[0:256, band : band + 1] * nt_dot(
                    gs[...], wide[(12 + index) % 3, 256 * side : 256 * side + 256, :]
                )
                parts[third] = term if parts[third] is None else parts[third] + term
            used(wide_load, 12 + index, 18)
        for third in range(3):
            pix_grad[:, 256 * third : 256 * third + 256] = parts[third].astype(jnp.bfloat16)
        out.start()

    def finish_bias(total):
        bias_out[...] = total

    actions = {
        HEADS: heads_back,
        FAR: pass_far,
        CLOSE: close,
        GP: lambda index: gp_copy(index).start(),
        PUT: compute,
        ADV: lambda chunk, step: advance(chunk, step, finisher(chunk)),
        THROUGH: through_qkv,
        NORM: norm_back,
        ROWS: side_rows,
        BIAS: bias_chunk,
        ADVB: lambda step: advance_f(0, step, finish_bias),
        PIX: pixels_back,
        MLP: mlp_tile,
        POST: mlp_back,
        GATT: attention_grad,
    }
    for name, *where_at in SCHEDULE:
        if (name, *where_at) == (HEADS, 0):
            for copy in loads[10:]:
                copy.wait()
        actions[name](*where_at)
    out.wait()
    for _, remote in made[:-1]:
        remote.wait_send()
    for pair in range(8):
        if pair >= 6:
            near_copy(pair).wait_send()
            far_copy(pair).wait_send()
    for index in range(6):
        gp_copy(index).wait_send()
    for tile in range(8):
        gpre_copy(tile).wait_send()
    for copy in (gout_copy(), gbr_copy(), hot_copy(), hid_copy(0), hid_copy(1)):
        copy.wait_send()
    for chunk in range(CHUNKS):
        drain(chunk)
    drain_f(0)


def backward(*operands):
    any_space = pl.BlockSpec(memory_space=pl.ANY)
    in_vmem = pl.BlockSpec(memory_space=pltpu.VMEM)
    half, full = jnp.bfloat16, jnp.float32
    shape = jax.ShapeDtypeStruct
    dma = pltpu.SemaphoreType.DMA
    return pl.pallas_call(
        backward_kernel,
        out_shape=(
            shape((256, 1024), half),
            shape((256, 768), half),
            shape((8, 3072), full),
            shape((8, 3072), full),
            shape((8, 1024), full),
            shape((8, 4096), full),
            shape((32, 1024), full),
            shape((8, 128), full),
        ),
        in_specs=[any_space] * 21,
        out_specs=(any_space,) * 2 + (in_vmem,) * 6,
        scratch_shapes=[
            pltpu.VMEM((3, 512, 512), half),
            pltpu.VMEM((2, 256, 2048), half),
            pltpu.VMEM((256, 2048), half),
            pltpu.VMEM((512, 1024), half),
            pltpu.VMEM((512, 4096), half),
            pltpu.VMEM((512, 1024), half),
            pltpu.VMEM((512, 3072), half),
            pltpu.VMEM((512, 768), half),
            pltpu.VMEM((512, 128), full),
            pltpu.VMEM((2, 16, 1024), full),
            pltpu.VMEM((128, 1024), full),
            pltpu.VMEM((8, 1024), full),
            pltpu.VMEM((512, 512), half),
            pltpu.VMEM((2048, 512), half),
            pltpu.VMEM((SLOTS, 64, 16, 256), half),
            pltpu.VMEM((SLOTS, 56, 16, 256), half),
            pltpu.VMEM((CHUNKS, 14, 16, 256), half),
            pltpu.VMEM((CHUNKS, 7, 16, 256), half),
            pltpu.VMEM((1, 64, 8, 128), full),
            pltpu.VMEM((1, 56, 8, 128), full),
            pltpu.VMEM((1, 14, 8, 128), full),
            pltpu.VMEM((1, 7, 8, 128), full),
            pltpu.VMEM((8, 256, 128), half),
            pltpu.VMEM((2, 2, 1024, 128), half),
            pltpu.VMEM((8, 256, 128), half),
            pltpu.VMEM((1024, 256), full),
            pltpu.VMEM((2, 2, 2, 256, 128), half),
            pltpu.VMEM((4, 2, 2, 256, 128), half),
            pltpu.VMEM((2, 2, 256, 128), half),
            pltpu.VMEM((8, 2, 256, 128), half),
            pltpu.VMEM((2, 2, 256, 128), full),
            pltpu.VMEM((2, 2, 256, 128), full),
            pltpu.VMEM((2, 1024, 128), full),
            pltpu.VMEM((256, 1024), half),
            pltpu.VMEM((256, 1024), full),
            pltpu.VMEM((256, 1024), full),
            pltpu.VMEM((256, 1024), full),
            pltpu.VMEM((256, 1024), full),
            pltpu.VMEM((256, 1024), half),
            pltpu.VMEM((256, 768), half),
            pltpu.VMEM((3, 1024, 512), half),
            pltpu.VMEM((3, 512, 1024), half),
            pltpu.VMEM((8, 2, 256), full),
            pltpu.VMEM((1024,), full),
            pltpu.VMEM((1024,), full),
            pltpu.VMEM((1024,), full),
            pltpu.VMEM((1024,), full),
            pltpu.VMEM((4096,), full),
            pltpu.VMEM((1024,), full),
            dma((10,)),
            dma((10,)),
            dma((10,)),
            dma((CHUNKS, 6)),
            dma((CHUNKS, 6)),
            pltpu.SemaphoreType.REGULAR((CHUNKS - SLOTS, 3)),
            dma((1, 6)),
            dma((1, 6)),
            dma((15,)),
            dma((2,)),
            dma((3,)),
            dma((3,)),
            dma((2, 8)),
            dma((2, 8)),
            pltpu.SemaphoreType.REGULAR((4,)),
            dma((6,)),
            dma((6,)),
            dma((8,)),
            dma((8,)),
            dma((5,)),
            dma((5,)),
        ],
        compiler_params=pltpu.CompilerParams(
            collective_id=2, has_side_effects=True, vmem_limit_bytes=VMEM_BYTES
        ),
        name="backward",
    )(*operands)


def finish_kernel(*refs):
    sources, dests, bufs = refs[:8], refs[8:25], refs[25:33]
    cols, bands, flat, in_sem, out_sem = refs[33:]
    loads = []
    for source, buf in zip(sources, bufs):
        loads.append(pltpu.make_async_copy(source, buf, in_sem.at[len(loads)]))
    for copy in reversed(loads):
        copy.start()
    stores = []

    def store(source, dest):
        stores.append(pltpu.make_async_copy(source, dest, out_sem.at[len(stores)]))
        stores[-1].start()

    loads[7].wait()
    sums = bufs[7][...]
    cols[...] = sums.T[0:16, :]
    for index in range(8):
        store(cols.at[pl.ds(4 + index, 1), :], dests[8 + index])
    bands[...] = cols[0:4, :]
    store(bands, dests[7])
    lane = lax.broadcasted_iota(jnp.int32, (8, 128), 1)
    wide = jnp.zeros((8, 128), jnp.float32)
    for part in range(4):
        wide = wide + jnp.where(lane // 8 == part, sums[:, 12 + part : 13 + part], 0.0)
    wide = jnp.where(lane % 8 == lax.broadcasted_iota(jnp.int32, (8, 128), 0), wide, 0.0)
    flat[...] = jnp.sum(wide, axis=0, keepdims=True)[:, 0:32]
    store(flat, dests[16])
    for index in range(7):
        loads[index].wait()
        if index < 6:
            store(bufs[index], dests[index])
    for band in range(4):
        store(bufs[6].at[:, pl.ds(768 * band, 768)], dests[6].at[band])
    for copy in stores:
        copy.wait()


def finish(*operands):
    any_space = pl.BlockSpec(memory_space=pl.ANY)
    full = jnp.float32
    shape = jax.ShapeDtypeStruct
    return pl.pallas_call(
        finish_kernel,
        out_shape=tuple(shape(array.shape, array.dtype) for array in operands[:6])
        + (shape((4, 8, 768), full), shape((4, 8), full))
        + (shape((1, 8), full),) * 8
        + (shape((1, 32), full),),
        in_specs=[any_space] * 8,
        out_specs=(any_space,) * 17,
        scratch_shapes=[pltpu.VMEM(array.shape, array.dtype) for array in operands]
        + [
            pltpu.VMEM((16, 8), full),
            pltpu.VMEM((4, 8), full),
            pltpu.VMEM((1, 32), full),
            pltpu.SemaphoreType.DMA((8,)),
            pltpu.SemaphoreType.DMA((20,)),
        ],
        compiler_params=pltpu.CompilerParams(vmem_limit_bytes=VMEM_BYTES),
        name="finish",
    )(*operands)


def on_device(
    pixels,
    positions,
    segments,
    groups,
    cotangent,
    emb_weight,
    emb_bias,
    norm1_gain,
    norm1_bias,
    qkv_weight,
    query_bias,
    value_bias,
    out_weight,
    out_bias,
    norm2_gain,
    norm2_bias,
    fc1_weight,
    fc1_bias,
    fc2_weight,
    fc2_bias,
):
    rows_dev, slice_len, pix_len = pixels.shape
    model_width = qkv_weight.shape[0]
    band_count = emb_weight.shape[0]
    tok_count = rows_dev * slice_len
    flat_pixels = pixels.reshape(tok_count, pix_len)
    flat_emb = emb_weight.reshape(band_count * pix_len, model_width)
    hot_live, mask, stream, normed_one, query_pairs, key_value, log_sums, attended = forward(
        flat_pixels,
        positions.reshape(tok_count, model_width),
        segments,
        groups,
        emb_bias,
        norm1_gain,
        norm1_bias,
        query_bias,
        value_bias,
        flat_emb,
        qkv_weight,
    )
    block_out, pixel_grad, emb_sum, qkv_sum, out_sum, fc1_sum, fc2_sum, bias_sum = backward(
        attended,
        stream,
        cotangent.reshape(tok_count, model_width),
        hot_live,
        mask,
        query_pairs,
        key_value,
        log_sums,
        normed_one,
        flat_pixels,
        norm1_gain,
        norm2_gain,
        norm2_bias,
        out_bias,
        fc1_bias,
        fc2_bias,
        flat_emb,
        qkv_weight,
        out_weight,
        fc1_weight,
        fc2_weight,
    )
    block_out, pixel_grad, qkv_sum, out_sum, fc1_sum, fc2_sum, emb_sum, *rest = finish(
        block_out, pixel_grad, qkv_sum, out_sum, fc1_sum, fc2_sum, emb_sum, bias_sum
    )
    emb_bias_sum, gain1, bias1, query, value, out, gain2, bias2, last, wide = (
        part if index == 0 else part.reshape(-1) for index, part in enumerate(rest)
    )
    return (
        block_out.reshape(rows_dev, slice_len, model_width),
        pixel_grad.reshape(rows_dev, slice_len, pix_len),
        jnp.swapaxes(emb_sum, 1, 2),
        emb_bias_sum,
        gain1,
        bias1,
        qkv_sum,
        query,
        value,
        out_sum,
        out,
        gain2,
        bias2,
        fc1_sum,
        wide,
        fc2_sum,
        last,
    )


def solution(mesh):
    return jax.shard_map(
        on_device,
        mesh=mesh,
        in_specs=(
            P("batch", "blk", None),
            P("batch", "blk", None),
            P("batch", None),
            P("batch", "blk"),
            P("batch", "blk", None),
            P(),
            P(),
            P(),
            P(),
            P(),
            P(),
            P(),
            P(),
            P(),
            P(),
            P(),
            P(),
            P(),
            P(),
            P(),
        ),
        out_specs=(
            P("batch", "blk", None),
            P("batch", "blk", None),
            P(None, None, ("blk", "batch")),
            P(None, ("blk", "batch")),
            P(("blk", "batch")),
            P(("blk", "batch")),
            P(("blk", "batch"), None),
            P(("blk", "batch")),
            P(("blk", "batch")),
            P(("blk", "batch"), None),
            P(("blk", "batch")),
            P(("blk", "batch")),
            P(("blk", "batch")),
            P(("blk", "batch"), None),
            P(("blk", "batch")),
            P(("blk", "batch"), None),
            P(("blk", "batch")),
        ),
        check_vma=False,
    )
```
